32 devices in a mesh: ctx: 8 (over z, y), fsdp: 4 (over x, core).
Axes of the slice: x: 2, y: 2, z: 4, core: 2. Of those that a mesh axis runs over, the one named last changes fastest.
Arguments:
- tokens: bfloat16 [4096, 1152], P(('ctx', 'fsdp')), may hold values from -6 to 6
- cotangent: bfloat16 [4096, 1152], P(('ctx', 'fsdp')), may hold values from -6 to 6
- block_table: int32 [64], replicated, may hold values from 0 to 63, as said below
- sequence_ids: int32 [4096], replicated, may hold values from 0 to 1, as said below
- w_query: bfloat16 [1152, 1024], P('fsdp'), may hold values from -0.1875 to 0.1875
- w_key: bfloat16 [1152, 256], P('fsdp'), may hold values from -0.1875 to 0.1875
- w_value: bfloat16 [1152, 256], P('fsdp'), may hold values from -0.1875 to 0.1875
- w_out: bfloat16 [1024, 1152], P('fsdp'), may hold values from -0.1875 to 0.1875
- w_in: bfloat16 [1152, 2, 6912], P('fsdp'), may hold values from -0.1875 to 0.1875
- w_down: bfloat16 [6912, 1152], P('fsdp'), may hold values from -0.078125 to 0.078125
- gain_attn_in: bfloat16 [1152], P('fsdp'), may hold values from 0.099609375 to 1.8984375
- gain_attn_out: bfloat16 [1152], P('fsdp'), may hold values from 0.099609375 to 1.8984375
- gain_ffn_in: bfloat16 [1152], P('fsdp'), may hold values from 0.099609375 to 1.8984375
- gain_ffn_out: bfloat16 [1152], P('fsdp'), may hold values from 0.099609375 to 1.8984375
- gain_query: bfloat16 [256], P('fsdp'), may hold values from 0.099609375 to 1.8984375
- gain_key: bfloat16 [256], P('fsdp'), may hold values from 0.099609375 to 1.8984375
Outputs:
- block_out: bfloat16 [4096, 1152], P(('ctx', 'fsdp'))
- grad_tokens: float32 [4096, 1152], P(('ctx', 'fsdp'))
- grad_query: float32 [1152, 1024], P('fsdp')
- grad_key: float32 [1152, 256], P('fsdp')
- grad_value: float32 [1152, 256], P('fsdp')
- grad_out: float32 [1024, 1152], P('fsdp')
- grad_in: float32 [1152, 2, 6912], P('fsdp')
- grad_down: float32 [6912, 1152], P('fsdp')
- grad_gain_attn_in: float32 [1152], P('fsdp')
- grad_gain_attn_out: float32 [1152], P('fsdp')
- grad_gain_ffn_in: float32 [1152], P('fsdp')
- grad_gain_ffn_out: float32 [1152], P('fsdp')
- grad_gain_query: float32 [256], P('fsdp')
- grad_gain_key: float32 [256], P('fsdp')
The draws below stay inside these ranges and needn't reach their ends.
Inputs may be any that keep to these rules, and one draw needn't show every extreme that they name: Device d of ctx+fsdp (ctx slowest) holds rows of stream blocks block_table[2 d] and block_table[2 d + 1]; these two sum to 63, and every block appears once. `sequence_ids`: 0 on the places of the first sequence, then 1 on those of the second; each sequence has 1024 places or more.
All inputs are finite; a program needn't handle non-finite values.
Results may differ from the reference program's by a relative error of at most 0.023.
Values may be sent and summed in bfloat16 or wider, within the bound.
No kernel may reach another device: no remote copies, remote signals or barrier semaphores. Data moves between devices by JAX's collectives and lax.ppermute only.
A program may use at most 384 MiB of HBM per device.

```python
import jax
import jax.numpy as jnp
from jax import lax

D = 1152
FF = 6912
H = 4
HD = 256
TOKENS = 4096
PAIRS = 32
NBLK = 64
BLK = 64


def draw_block_table(key, part):
    key = jax.random.fold_in(key, 11)
    paired = jax.random.permutation(key, PAIRS).astype(jnp.int32)
    mirror = (NBLK - 1 - paired).astype(jnp.int32)
    return jnp.stack([paired, mirror], axis=1).reshape(NBLK)


def draw_sequence_ids(key, part):
    key = jax.random.fold_in(key, 23)
    boundary = jax.random.randint(key, (), TOKENS // 4, 3 * TOKENS // 4 + 1, dtype=jnp.int32)
    return (jnp.arange(TOKENS, dtype=jnp.int32) >= boundary).astype(jnp.int32)


def levels(stream_key, shape, shards, smallest, top_value):
    level = 1.0
    for dim, shards_of in shards:
        heights = jax.random.uniform(jax.random.fold_in(jax.random.fold_in(stream_key, 6), dim), (shards_of,), jnp.float32, smallest / len(shards), top_value / len(shards))
        level = level * jnp.repeat(jnp.exp(heights), shape[dim] // shards_of).reshape((-1,) + (1,) * (len(shape) - 1 - dim))
    return level


def centred(own_key, extent, width, most, shards=(), held_as=jnp.bfloat16):
    values = width * jax.random.normal(own_key, extent, jnp.float32)
    if shards:
        values = values * levels(own_key, extent, shards, -0.22, 0.18)
    return jnp.clip(values, -most, most).astype(held_as)


def setup_inputs(seed: int = 0) -> dict:
    arg_keys = jax.random.split(jax.random.key(seed), 17)
    return {
        "tokens": centred(arg_keys[0], (TOKENS, D), 1.0, 6.0, ((0, 32),)),
        "cotangent": centred(arg_keys[1], (TOKENS, D), 1.0, 6.0, ((0, 32),)),
        "block_table": draw_block_table(jax.random.fold_in(arg_keys[16], 71), 0),
        "sequence_ids": draw_sequence_ids(jax.random.fold_in(arg_keys[16], 71), 0),
        "w_query": centred(arg_keys[4], (D, H * HD), D ** -0.5, 0.1875, ((0, 4),)),
        "w_key": centred(arg_keys[5], (D, HD), D ** -0.5, 0.1875, ((0, 4),)),
        "w_value": centred(arg_keys[6], (D, HD), D ** -0.5, 0.1875, ((0, 4),)),
        "w_out": centred(arg_keys[7], (H * HD, D), (H * HD) ** -0.5, 0.1875, ((0, 4),)),
        "w_in": centred(arg_keys[8], (D, 2, FF), D ** -0.5, 0.1875, ((0, 4),)),
        "w_down": centred(arg_keys[9], (FF, D), FF ** -0.5, 0.078125, ((0, 4),)),
        "gain_attn_in": jnp.clip(1.0 + 0.18 * jax.random.normal(arg_keys[10], (D,), jnp.float32), 0.099609375, 1.8984375).astype(jnp.bfloat16),
        "gain_attn_out": jnp.clip(1.0 + 0.18 * jax.random.normal(arg_keys[11], (D,), jnp.float32), 0.099609375, 1.8984375).astype(jnp.bfloat16),
        "gain_ffn_in": jnp.clip(1.0 + 0.18 * jax.random.normal(arg_keys[12], (D,), jnp.float32), 0.099609375, 1.8984375).astype(jnp.bfloat16),
        "gain_ffn_out": jnp.clip(1.0 + 0.18 * jax.random.normal(arg_keys[13], (D,), jnp.float32), 0.099609375, 1.8984375).astype(jnp.bfloat16),
        "gain_query": jnp.clip(1.0 + 0.18 * jax.random.normal(arg_keys[14], (HD,), jnp.float32), 0.099609375, 1.8984375).astype(jnp.bfloat16),
        "gain_key": jnp.clip(1.0 + 0.18 * jax.random.normal(arg_keys[15], (HD,), jnp.float32), 0.099609375, 1.8984375).astype(jnp.bfloat16),
    }


EPS = 1e-06
HIGH = lax.Precision.HIGHEST

@jax.custom_vjp
def low(v):
    return lax.optimization_barrier(v.astype(jnp.bfloat16)).astype(jnp.float32)

@jax.custom_vjp
def low_back(v):
    return v

def low_keep(v):
    return (low(v), None)

def low_pass(kept, grad):
    return (grad,)

def back_keep(v):
    return (v, None)

def back_low(kept, grad):
    return (low(grad),)
low.defvjp(low_keep, low_pass)
low_back.defvjp(back_keep, back_low)

def rms_norm(values, scaling):
    return values * lax.rsqrt(lax.optimization_barrier(jnp.mean(values * values, axis=-1, keepdims=True)) + EPS) * scaling

def rotate(values, angles):
    half_width = values.shape[-1] // 2
    cosine = jnp.cos(angles)
    sine_part = jnp.sin(angles)
    first_half = values[..., :half_width]
    second_half = values[..., half_width:]
    return jnp.concatenate([first_half * cosine - second_half * sine_part, second_half * cosine + first_half * sine_part], axis=-1)

def place_rows(block_table, sequence_ids, layout_rows):
    stream = block_table[layout_rows // BLK] * BLK + layout_rows % BLK
    boundary = jnp.sum((sequence_ids == 0).astype(jnp.int32))
    sequence = sequence_ids[stream]
    position = stream - sequence * boundary
    return (position, sequence)

def angles_of(position):
    half_width = HD // 2
    inverse = 1000000.0 ** (-jnp.arange(half_width, dtype=jnp.float32) / half_width)
    return position.astype(jnp.float32)[:, None] * inverse[None, :]

def attention(queries, key_rows, value_rows, position, sequence):
    total_rows = queries.shape[0]
    block_width = min(512, total_rows)
    block_count = total_rows // block_width

    def one_block(section):
        query_block, query_pos, query_seq = section
        scores = jnp.einsum('qhd,kd->hqk', query_block, key_rows, precision=HIGH)
        scores = low_back(scores)
        allowed = (sequence[None, :] == query_seq[:, None]) & (position[None, :] <= query_pos[:, None])
        scores = jnp.where(allowed[None], scores, -1e+30)
        probs = jax.nn.softmax(scores, axis=-1)
        return jnp.einsum('hqk,kd->qhd', low(probs), value_rows, precision=HIGH)
    outcome = lax.map(jax.checkpoint(one_block), (queries.reshape(block_count, block_width, H, HD), position.reshape(block_count, block_width), sequence.reshape(block_count, block_width)))
    return outcome.reshape(total_rows, H, HD)

def reference(tokens, cotangent, block_table, sequence_ids, w_query, w_key, w_value, w_out, w_in, w_down, gain_attn_in, gain_attn_out, gain_ffn_in, gain_ffn_out, gain_query, gain_key):
    total_rows = tokens.shape[0]
    position, sequence = place_rows(block_table, sequence_ids, jnp.arange(total_rows, dtype=jnp.int32))
    angles = angles_of(position)

    def forward(inputs, query_mat, key_mat, value_mat, out_mat, in_mat, down_mat, attn_in_gain, attn_out_gain, ffn_in_gain, ffn_out_gain, query_gain, key_gain):
        first_low = low(rms_norm(inputs, attn_in_gain))
        query_raw = low_back(jnp.dot(first_low, query_mat, precision=HIGH))
        key_raw = low_back(jnp.dot(first_low, key_mat, precision=HIGH))
        value_raw = low_back(jnp.dot(first_low, value_mat, precision=HIGH))
        query_heads = rms_norm(query_raw.reshape(total_rows, H, HD), query_gain)
        queries = low(rotate(query_heads, angles[:, None, :]) * HD ** (-0.5))
        key_rows = low(rotate(rms_norm(key_raw, key_gain), angles))
        value_rows = low(value_raw)
        heads_out = attention(queries, key_rows, value_rows, position, sequence)
        heads_low = low(low_back(heads_out)).reshape(total_rows, H * HD)
        attn_raw = low_back(jnp.dot(heads_low, out_mat, precision=HIGH))
        hidden = inputs + rms_norm(attn_raw, attn_out_gain)
        second_low = low(rms_norm(hidden, ffn_in_gain))
        gate_up = low_back(jnp.einsum('td,dkf->tkf', second_low, in_mat, precision=HIGH))
        act_low = low(jax.nn.gelu(gate_up[:, 0], approximate=True) * gate_up[:, 1])
        ffn_raw = low_back(jnp.dot(act_low, down_mat, precision=HIGH))
        return hidden + rms_norm(ffn_raw, ffn_out_gain)
    floats = [argument.astype(jnp.float32) for argument in (tokens, w_query, w_key, w_value, w_out, w_in, w_down, gain_attn_in, gain_attn_out, gain_ffn_in, gain_ffn_out, gain_query, gain_key)]
    result, backward = jax.vjp(forward, *floats)
    grads = backward(cotangent.astype(jnp.float32))
    return (result.astype(jnp.bfloat16), grads[0], grads[1], grads[2], grads[3], grads[4], grads[5], grads[6], grads[7], grads[8], grads[9], grads[10], grads[11], grads[12])
```

```python
import functools
import math

import jax
import jax.numpy as jnp
from jax import lax
from jax.experimental import pallas as pl
from jax.experimental.pallas import tpu as pltpu
from jax.sharding import PartitionSpec as P

H = 4
HD = 256
EPS = 1e-06
AXES = ("ctx", "fsdp")
BF = jnp.bfloat16
F32 = jnp.float32
KEY_BLOCK = 512


def rms_norm(values, scaling):
    return values * lax.rsqrt(jnp.mean(values * values, axis=-1, keepdims=True) + EPS) * scaling


def rotate(values, cosine, sine):
    half_width = values.shape[-1] // 2
    first_half = values[..., :half_width]
    second_half = values[..., half_width:]
    return jnp.concatenate(
        [first_half * cosine - second_half * sine, second_half * cosine + first_half * sine],
        axis=-1,
    )


def after(value, *earlier):
    return lax.optimization_barrier((value, *earlier))[0]


def swap(value, offset):
    count = lax.axis_size("ctx") * lax.axis_size("fsdp")
    return lax.ppermute(value, AXES, [(i, i ^ offset) for i in range(count)])


def join(*parts):
    return jnp.concatenate(parts, axis=0)


def gather_group(value):
    pair = join(value, swap(value, 2))
    return join(pair, swap(pair, 1))


def scatter_group(terms):
    half = terms.shape[0] // 2
    pair = terms[:half] + swap(terms[half:].astype(BF), 1).astype(F32)
    quarter = half // 2
    return pair[:quarter] + swap(pair[quarter:].astype(BF), 2).astype(F32)


def wide_offsets():
    highs = [8 * s for s in range(lax.axis_size("ctx") // 2)]
    chip = [low + high for low in (0, 4, 2, 6) for high in highs]
    return chip + [1 + o for o in chip]


def gather_wide(value):
    highs = lax.axis_size("ctx") // 2
    line = join(value, *[swap(value, 8 * s) for s in range(1, highs)])
    half = line.shape[0] // 2
    along_y, along_x = swap(line, 4), swap(line, 2)
    corner = (swap(along_y[:half], 2), swap(along_x[half:], 4))
    chip = join(line, along_y, along_x, *corner)
    return join(chip, swap(chip, 1))


def scatter_wide(terms):
    highs = lax.axis_size("ctx") // 2
    half = terms.shape[0] // 2
    chip = terms[:half].astype(F32) + swap(terms[half:], 1).astype(F32)
    line, along_y, along_x, corner = jnp.split(chip, 4, axis=0)
    mid = line.shape[0] // 2
    corner = corner.astype(BF)
    from_x, from_y = swap(corner[:mid], 2), swap(corner[mid:], 4)
    along_y = join(along_y[:mid] + from_x.astype(F32), along_y[mid:])
    along_x = join(along_x[:mid], along_x[mid:] + from_y.astype(F32))
    line = (
        line
        + swap(along_y.astype(BF), 4).astype(F32)
        + swap(along_x.astype(BF), 2).astype(F32)
    )
    rows = line.shape[0] // highs
    total = line[:rows]
    for s in range(1, highs):
        total = total + swap(line[s * rows : (s + 1) * rows].astype(BF), 8 * s).astype(F32)
    return total


def sum_over_ctx(value):
    count, me = lax.axis_size("ctx"), lax.axis_index("ctx")
    highs, low, high = count // 2, me % 2, me // 2
    rows, columns = value.shape
    parts = value.reshape(highs, 2, rows // count, columns)
    line = lax.dynamic_index_in_dim(parts, low, 1, keepdims=False) + swap(
        lax.dynamic_index_in_dim(parts, 1 - low, 1, keepdims=False).astype(BF), 4
    ).astype(F32)
    total = lax.dynamic_index_in_dim(line, high, 0, keepdims=False)
    line_low = line.astype(BF)
    for s in range(1, highs):
        total = total + swap(
            lax.dynamic_index_in_dim(line_low, high ^ s, 0, keepdims=False), 8 * s
        ).astype(F32)
    total = total.astype(BF)
    line = jnp.zeros(line_low.shape, BF)
    for s in range(highs):
        piece = total if s == 0 else swap(total, 8 * s)
        line = lax.dynamic_update_index_in_dim(line, piece, high ^ s, 0)
    other = swap(line, 4)
    even, odd = jnp.where(low == 0, line, other), jnp.where(low == 0, other, line)
    return jnp.stack([even, odd], axis=1).reshape(rows, columns).astype(F32)


def in_place(pieces, me, axis):
    size = pieces[0].shape[axis]
    shape = list(pieces[0].shape)
    shape[axis] = size * len(pieces)
    out = jnp.zeros(shape, pieces[0].dtype)
    for offset, piece in enumerate(pieces):
        out = lax.dynamic_update_slice_in_dim(out, piece, (me ^ offset) * size, axis)
    return out


def gather_rows(value, me):
    pair = join(value, swap(value, 2))
    other = swap(pair, 1)
    rows = value.shape[0]
    return in_place([value, other[:rows], pair[rows:], other[rows:]], me, 0)


def scatter_rows(value, me):
    rows = value.shape[0] // 4
    return scatter_group(
        join(*[lax.dynamic_slice_in_dim(value, (me ^ o) * rows, rows, 0) for o in (0, 2, 1, 3)])
    )


def attend_kernel(blocks, q, q_place, q_start, k, v, probs, heads, mass):
    step = pl.program_id(0)

    @pl.when(step == 0)
    def _():
        heads[...] = jnp.zeros_like(heads)
        mass[...] = jnp.zeros_like(mass)

    scores = lax.dot_general(
        k[...], q[...], (((1,), (1,)), ((), ())), preferred_element_type=F32
    )
    rows = k.shape[0]
    block = 64
    place, start = q_place[...], q_start[...]
    total = jnp.zeros_like(mass)
    for i in range(rows // block):
        first = blocks[step * (rows // block) + i] * block
        keys = first + lax.broadcasted_iota(jnp.int32, (block, scores.shape[1]), 0)
        allowed = (keys <= place) & (keys >= start)
        weights = jnp.where(allowed, jnp.exp(scores[i * block : (i + 1) * block]), 0.0)
        probs[i * block : (i + 1) * block, :] = weights.astype(BF)
        total = total + jnp.sum(weights, axis=0, keepdims=True)
    mass[...] += total
    heads[...] += lax.dot_general(
        v[...], probs[...], (((0,), (0,)), ((), ())), preferred_element_type=F32
    )


def attend(blocks, queries, q_place, q_start, pairs):
    head_rows = queries.shape[0]
    keys = pairs.shape[0]
    return pl.pallas_call(
        attend_kernel,
        grid_spec=pltpu.PrefetchScalarGridSpec(
            num_scalar_prefetch=1,
            grid=(keys // KEY_BLOCK,),
            in_specs=[
                pl.BlockSpec((head_rows, HD), lambda i, b: (0, 0)),
                pl.BlockSpec((1, head_rows), lambda i, b: (0, 0)),
                pl.BlockSpec((1, head_rows), lambda i, b: (0, 0)),
                pl.BlockSpec((KEY_BLOCK, HD), lambda i, b: (i, 0)),
                pl.BlockSpec((KEY_BLOCK, HD), lambda i, b: (i, 1)),
            ],
            out_specs=[
                pl.BlockSpec((KEY_BLOCK, head_rows), lambda i, b: (i, 0)),
                pl.BlockSpec((HD, head_rows), lambda i, b: (0, 0)),
                pl.BlockSpec((1, head_rows), lambda i, b: (0, 0)),
            ],
        ),
        out_shape=[
            jax.ShapeDtypeStruct((keys, head_rows), BF),
            jax.ShapeDtypeStruct((HD, head_rows), F32),
            jax.ShapeDtypeStruct((1, head_rows), F32),
        ],
        compiler_params=pltpu.CompilerParams(vmem_limit_bytes=32 * 2**20),
        cost_estimate=pl.CostEstimate(
            flops=4 * keys * head_rows * HD,
            bytes_accessed=keys * (head_rows + 2 * HD) * 2,
            transcendentals=keys * head_rows,
        ),
        name="attend",
    )(blocks, queries, q_place, q_start, pairs, pairs)


def attend_back_kernel(q, d_heads, inverse, dots, probs, k, v, d_queries, d_pairs):
    @pl.when(pl.program_id(0) == 0)
    def _():
        d_queries[...] = jnp.zeros_like(d_queries)

    d_probs = lax.dot_general(
        v[...], d_heads[...], (((1,), (1,)), ((), ())), preferred_element_type=F32
    )
    chance = probs[...].astype(F32) * inverse[...]
    d_scores = (chance * (d_probs - dots[...])).astype(BF)
    d_pairs[:, :HD] = jnp.dot(d_scores, q[...], preferred_element_type=F32).astype(BF)
    d_pairs[:, HD:] = jnp.dot(
        chance.astype(BF), d_heads[...], preferred_element_type=F32
    ).astype(BF)
    d_queries[...] += lax.dot_general(
        k[...], d_scores, (((0,), (0,)), ((), ())), preferred_element_type=F32
    )


def attend_back(queries, d_heads, inverse, dots, probs, pairs):
    head_rows = queries.shape[0]
    keys = pairs.shape[0]
    whole = pl.BlockSpec((head_rows, HD), lambda i: (0, 0))
    line = pl.BlockSpec((1, head_rows), lambda i: (0, 0))
    return pl.pallas_call(
        attend_back_kernel,
        grid=(keys // KEY_BLOCK,),
        in_specs=[
            whole,
            whole,
            line,
            line,
            pl.BlockSpec((KEY_BLOCK, head_rows), lambda i: (i, 0)),
            pl.BlockSpec((KEY_BLOCK, HD), lambda i: (i, 0)),
            pl.BlockSpec((KEY_BLOCK, HD), lambda i: (i, 1)),
        ],
        out_specs=[
            pl.BlockSpec((HD, head_rows), lambda i: (0, 0)),
            pl.BlockSpec((KEY_BLOCK, 2 * HD), lambda i: (i, 0)),
        ],
        out_shape=[
            jax.ShapeDtypeStruct((HD, head_rows), F32),
            jax.ShapeDtypeStruct((keys, 2 * HD), BF),
        ],
        compiler_params=pltpu.CompilerParams(vmem_limit_bytes=32 * 2**20),
        cost_estimate=pl.CostEstimate(
            flops=8 * keys * head_rows * HD,
            bytes_accessed=keys * (head_rows + 4 * HD) * 2,
            transcendentals=0,
        ),
        name="attend_back",
    )(queries, d_heads, inverse, dots, probs, pairs, pairs)


def left_of(owner, part):
    return pl.multiple_of(owner * part - part % 128 * (owner % 2), 128)


def carve_kernel(part, mine, w, *outs):
    wide = outs[0].shape[2]
    for offset, out in enumerate(outs):
        out[...] = w[:, :, pl.ds(left_of(mine[0] ^ offset, part), wide)]


def carve(w, mine, part, wide):
    rows, step = w.shape[1], 48
    return pl.pallas_call(
        functools.partial(carve_kernel, part),
        grid_spec=pltpu.PrefetchScalarGridSpec(
            num_scalar_prefetch=1,
            grid=(rows // step,),
            in_specs=[pl.BlockSpec((2, step, w.shape[2]), lambda i, m: (0, i, 0))],
            out_specs=[pl.BlockSpec((2, step, wide), lambda i, m: (0, i, 0))] * 4,
        ),
        out_shape=[jax.ShapeDtypeStruct((2, rows, wide), BF)] * 4,
        compiler_params=pltpu.CompilerParams(vmem_limit_bytes=32 * 2**20),
        name="carve",
    )(mine[None], w)


def lay_kernel(places, own, core, x2, y2, x3, y3, out):
    step = pl.program_id(0)
    for i, source in enumerate((own, own, core, core, x2, y2, x3, y3)):

        @pl.when(step == i)
        def _(source=source):
            out[...] = source[...]


def lay(places, own, core, x2, y2, x3, y3):
    half, wide = x2.shape[1], x2.shape[2]
    shape = (2, half, wide)
    still = pl.BlockSpec(shape, lambda i, p: (0, 0, 0))
    return pl.pallas_call(
        lay_kernel,
        grid_spec=pltpu.PrefetchScalarGridSpec(
            num_scalar_prefetch=1,
            grid=(8,),
            in_specs=[
                pl.BlockSpec(shape, lambda i, p: (0, jnp.minimum(i, 1), 0)),
                pl.BlockSpec(shape, lambda i, p: (0, jnp.clip(i - 2, 0, 1), 0)),
            ]
            + [still] * 4,
            out_specs=pl.BlockSpec(shape, lambda i, p: (0, p[i], 0)),
        ),
        out_shape=jax.ShapeDtypeStruct((2, 8 * half, wide), BF),
        compiler_params=pltpu.CompilerParams(vmem_limit_bytes=32 * 2**20),
        name="lay",
    )(places, own, core, x2, y2, x3, y3)


def contract(left, right, left_dim, right_dim):
    return lax.dot_general(
        left, right, (((left_dim,), (right_dim,)), ((), ())), preferred_element_type=F32
    )


def gelu_and_slope(x):
    scale = math.sqrt(2.0 / math.pi)
    square = x * x
    turn = jnp.tanh(x * (scale + (scale * 0.044715) * square))
    share = 0.5 + 0.5 * turn
    slope = share + (0.5 * x) * (1.0 - turn * turn) * (scale + (3 * scale * 0.044715) * square)
    return x * share, slope


def ffn_kernel(mine, second, d_ffn, w_gate, w_up, w_down, *rest):
    outs, down, act, d_both, both_sum = rest[:4], *rest[4:]
    step = pl.program_id(1)
    rows, slab = second.shape[0], 256
    width = down.shape[0]

    def products(r):
        at = pl.ds(r * slab, slab)
        return (
            contract(second[at, :], w_gate[0], 1, 0),
            contract(second[at, :], w_up[0], 1, 0),
            contract(d_ffn[at, :], w_down[...], 1, 1),
        )

    ahead = products(0)
    for r in range(rows // slab):
        at = pl.ds(r * slab, slab)
        gate, upper, d_act = ahead
        if r + 1 < rows // slab:
            ahead = products(r + 1)
        value, slope = gelu_and_slope(gate)
        act[at, :] = (value * upper).astype(BF)
        d_both[at, :width] = (d_act * upper * slope).astype(BF)
        d_both[at, width:] = (d_act * value).astype(BF)
    grad_both = contract(second[...], d_both[...], 0, 0)
    grad_down = contract(act[...], d_ffn[...], 0, 0)

    @pl.when(step == 0)
    def _():
        both_sum[...] = grad_both
        down[...] = grad_down

    @pl.when(step > 0)
    def _():
        both_sum[...] += grad_both
        down[...] += grad_down

    @pl.when(step == pl.num_programs(1) - 1)
    def _():
        quarter = second.shape[1] // 4
        for offset, out in enumerate(outs):
            at = pl.ds(pl.multiple_of((mine[0] ^ offset) * quarter, 32), quarter)
            out[0] = both_sum[at, :width].astype(BF)
            out[1] = both_sum[at, width:].astype(BF)


def ffn_gradients(mine, second_all, d_ffn_all, in_mat, down_mat, first, last):
    tokens, model = second_all.shape
    slab, width = min(2048, tokens), 256
    columns = (last - first) * width
    tall = pl.BlockSpec((slab, model), lambda j, t, m: (t, 0))
    return pl.pallas_call(
        ffn_kernel,
        grid_spec=pltpu.PrefetchScalarGridSpec(
            num_scalar_prefetch=1,
            grid=(last - first, tokens // slab),
            in_specs=[
                tall,
                tall,
                pl.BlockSpec((1, model, width), lambda j, t, m: (0, 0, j + first)),
                pl.BlockSpec((1, model, width), lambda j, t, m: (1, 0, j + first)),
                pl.BlockSpec((width, model), lambda j, t, m: (j + first, 0)),
            ],
            out_specs=[pl.BlockSpec((2, model // 4, width), lambda j, t, m: (0, 0, j))] * 4
            + [pl.BlockSpec((width, model), lambda j, t, m: (j, 0))],
            scratch_shapes=[
                pltpu.VMEM((slab, width), BF),
                pltpu.VMEM((slab, 2 * width), BF),
                pltpu.VMEM((model, 2 * width), F32),
            ],
        ),
        out_shape=[jax.ShapeDtypeStruct((2, model // 4, columns), BF)] * 4
        + [jax.ShapeDtypeStruct((columns, model), F32)],
        compiler_params=pltpu.CompilerParams(vmem_limit_bytes=56 * 2**20),
        cost_estimate=pl.CostEstimate(
            flops=12 * tokens * model * columns,
            bytes_accessed=4 * tokens * model * (last - first),
            transcendentals=tokens * columns,
        ),
        name="ffn_gradients",
    )(mine[None], second_all, d_ffn_all, in_mat, in_mat, down_mat)


def unfold_kernel(part, mine, *refs):
    out, sources = refs[-1], refs[:-1]
    ranges = len(sources) // 4
    extra = part % 128
    for m in range(4):

        @pl.when(mine[0] == m)
        def _(m=m):
            for side in range(2):
                rows = [
                    jnp.concatenate(
                        [sources[r * 4 + (m ^ owner)][side] for r in range(ranges)], axis=1
                    ).astype(F32)
                    for owner in range(4)
                ]
                wide = rows[0].shape[1]
                cut = wide - 128
                left = lax.broadcasted_iota(jnp.int32, (rows[0].shape[0], 128), 1) < extra
                pieces = []
                for even, odd in (rows[:2], rows[2:]):
                    shared = jnp.where(left, even[:, cut:], odd[:, :128])
                    pieces += [even[:, :cut], shared, odd[:, 128:]]
                out[:, side, :] = jnp.concatenate(pieces, axis=1)


def unfold(mine, part, ranges):
    sources = [piece for pieces in ranges for piece in pieces]
    rows, step = sources[0].shape[1], 16
    return pl.pallas_call(
        functools.partial(unfold_kernel, part),
        grid_spec=pltpu.PrefetchScalarGridSpec(
            num_scalar_prefetch=1,
            grid=(rows // step,),
            in_specs=[
                pl.BlockSpec((2, step, s.shape[2]), lambda i, m: (0, i, 0)) for s in sources
            ],
            out_specs=pl.BlockSpec((step, 2, 4 * part), lambda i, m: (i, 0, 0)),
        ),
        out_shape=jax.ShapeDtypeStruct((rows, 2, 4 * part), F32),
        compiler_params=pltpu.CompilerParams(vmem_limit_bytes=32 * 2**20),
        name="unfold",
    )(mine[None], *sources)


def activate(gate_part, upper_part):
    return jax.nn.gelu(gate_part, approximate=True) * upper_part


def pick(table, index):
    hit = index[:, None] == jnp.arange(table.shape[0], dtype=jnp.int32)[None, :]
    return jnp.sum(jnp.where(hit, table[None, :], 0), axis=1)


def dot(left, right):
    return jnp.dot(left, right, preferred_element_type=F32)


def dot_rows(left, right):
    return lax.dot_general(left, right, (((0,), (0,)), ((), ())), preferred_element_type=F32)


def dot_columns(left, right):
    return lax.dot_general(left, right, (((1,), (1,)), ((), ())), preferred_element_type=F32)


def body(
    tokens,
    cotangent,
    block_table,
    sequence_ids,
    w_query,
    w_key,
    w_value,
    w_out,
    w_in,
    w_down,
    gain_attn_in,
    gain_attn_out,
    gain_ffn_in,
    gain_ffn_out,
    gain_query,
    gain_key,
):
    rows = tokens.shape[0]
    block = rows // 2
    model, part = w_in.shape[0] * 4, w_down.shape[0]
    mine = lax.axis_index("fsdp")
    me = lax.axis_index("ctx") * 4 + mine

    sizes = [g.shape[0] for g in (gain_attn_in, gain_attn_out, gain_ffn_in, gain_ffn_out, gain_query, gain_key)]
    width = 384
    packed = jnp.stack(
        [
            jnp.pad(g, (0, width - g.shape[0]))
            for g in (gain_attn_in, gain_attn_out, gain_ffn_in, gain_ffn_out, gain_query, gain_key)
        ]
    )
    packed = jnp.pad(packed, ((0, 10), (0, 0)))
    all_gains = gather_rows(packed, mine).reshape(4, 16, width).astype(F32)
    attn_in_gain, attn_out_gain, ffn_in_gain, ffn_out_gain, query_gain, key_gain = [
        all_gains[:, i, :size].reshape(4 * size) for i, size in enumerate(sizes)
    ]

    pair_mat = gather_rows(jnp.concatenate([w_key, w_value], axis=1), mine)
    query_mat = gather_rows(after(w_query, pair_mat), mine)
    out_mat = gather_rows(after(w_out, query_mat), mine)

    wide = -(-part // 256) * 256
    low_bit = lax.axis_index("ctx") % 2
    own, to_core, to_x, to_corner = carve(jnp.swapaxes(w_in, 0, 1), mine, part, wide)
    quarter = model // 4
    half = quarter // 2
    to_x, to_corner = [
        lax.dynamic_slice_in_dim(c, low_bit * half, half, 1) for c in (to_x, to_corner)
    ]
    from_x = swap(after(to_x, query_mat), 2)
    from_corner = swap(after(to_corner, query_mat), 3)
    places = jnp.stack(
        [mine * 2, mine * 2 + 1, (mine ^ 1) * 2, (mine ^ 1) * 2 + 1]
        + [(mine ^ o) * 2 + bit for o in (2, 3) for bit in (low_bit, 1 - low_bit)]
    )
    in_mat = lay(
        places, own, swap(to_core, 1), from_x, swap(from_x, 4), from_corner, swap(from_corner, 4)
    )
    gate_mat, up_mat = in_mat[0], in_mat[1]
    down_mat = lax.dynamic_update_slice_in_dim(
        jnp.zeros((wide, model), BF), w_down, part % 128 * (mine % 2), 0
    )

    boundary = jnp.sum((sequence_ids == 0).astype(jnp.int32))
    everyone = me ^ jnp.array(wide_offsets(), jnp.int32)
    blocks = pick(block_table, jnp.stack([2 * everyone, 2 * everyone + 1], axis=1).reshape(-1))
    place = (blocks[:2, None] * block + jnp.arange(block, dtype=jnp.int32)[None, :]).reshape(-1)
    start = jnp.where(place >= boundary, boundary, 0)
    position = place - start
    inverse_angle = 1000000.0 ** (-jnp.arange(HD // 2, dtype=F32) / (HD // 2))
    angles = position.astype(F32)[:, None] * inverse_angle[None, :]
    cosine, sine = jnp.cos(angles), jnp.sin(angles)

    inputs = tokens.astype(F32)
    first_norm, first_back = jax.vjp(rms_norm, inputs, attn_in_gain)
    first_low = first_norm.astype(BF)

    def prepare_key(key_in, key_scaling):
        return rotate(rms_norm(key_in, key_scaling), cosine, sine)

    def prepare_query(query_in, query_scaling):
        query_heads = rms_norm(query_in.reshape(rows, H, HD), query_scaling)
        return rotate(query_heads, cosine[:, None, :], sine[:, None, :]) * HD ** (-0.5)

    pair_raw = dot(first_low, pair_mat)
    key_turned, key_back = jax.vjp(prepare_key, pair_raw[:, :HD], key_gain)
    pairs = gather_wide(
        jnp.concatenate([key_turned.astype(BF), pair_raw[:, HD:].astype(BF)], axis=1)
    )
    query_turned, query_back = jax.vjp(prepare_query, dot(first_low, query_mat), query_gain)
    queries = jnp.swapaxes(query_turned.astype(BF), 0, 1).reshape(H * rows, HD)

    probs, weighted, mass = attend(
        blocks, queries, jnp.tile(place, H)[None], jnp.tile(start, H)[None], pairs
    )
    inverse = 1.0 / mass
    heads = (weighted * inverse).T
    heads_low = jnp.swapaxes(heads.astype(BF).reshape(H, rows, HD), 0, 1).reshape(rows, H * HD)
    attn_raw = dot(heads_low, out_mat)
    attn_normed, attn_back = jax.vjp(rms_norm, attn_raw, attn_out_gain)
    hidden = inputs + attn_normed
    second_norm, second_back = jax.vjp(rms_norm, hidden, ffn_in_gain)
    second_low = second_norm.astype(BF)

    second_group = gather_group(second_low)
    gate, upper = dot(second_group, gate_mat), dot(second_group, up_mat)
    act_value, act_back = jax.vjp(activate, gate, upper)
    ffn_raw = scatter_group(dot(act_value.astype(BF), down_mat))
    ffn_normed, ffn_back = jax.vjp(rms_norm, ffn_raw, ffn_out_gain)
    block_out = (hidden + ffn_normed).astype(BF)
    upstream = cotangent.astype(F32)
    d_ffn, d_gain_ffn_out = ffn_back(upstream)
    d_ffn_low = d_ffn.astype(BF)
    d_ffn_group = gather_group(d_ffn_low)
    d_gate, d_upper = act_back(dot_columns(d_ffn_group, down_mat))
    d_second = scatter_group(
        dot_columns(d_gate.astype(BF), gate_mat) + dot_columns(d_upper.astype(BF), up_mat)
    )
    d_hidden_extra, d_gain_ffn_in = second_back(d_second)
    d_hidden = upstream + d_hidden_extra
    d_attn, d_gain_attn_out = attn_back(d_hidden)
    d_attn_low = d_attn.astype(BF)

    d_heads = jnp.swapaxes(
        dot_columns(d_attn_low, out_mat).astype(BF).reshape(rows, H, HD), 0, 1
    ).reshape(H * rows, HD)
    dots = jnp.sum(d_heads.astype(F32) * heads, axis=1)[None]
    d_queries, d_pairs = attend_back(queries, d_heads, inverse, dots, probs, pairs)
    own_sums = scatter_wide(d_pairs)
    d_queries = jnp.swapaxes(d_queries.T.reshape(H, rows, HD), 0, 1)
    d_query_raw, d_gain_query = query_back(d_queries)
    query_low = d_query_raw.astype(BF)
    d_key_raw, d_gain_key = key_back(own_sums[:, :HD])
    pair_low = jnp.concatenate([d_key_raw, own_sums[:, HD:]], axis=1).astype(BF)
    d_first = dot_columns(query_low, query_mat) + dot_columns(pair_low, pair_mat)
    d_inputs_extra, d_gain_attn_in = first_back(d_first)
    grad_tokens = d_hidden + d_inputs_extra

    grad_out = sum_over_ctx(scatter_rows(dot_rows(heads_low, d_attn_low), mine))
    grad_query = sum_over_ctx(scatter_rows(dot_rows(first_low, query_low), mine))
    gain_rows = jnp.stack(
        [d_gain_attn_in, d_gain_attn_out, d_gain_ffn_in, d_gain_ffn_out]
        + [
            jnp.pad(g.reshape(4, -1), ((0, 0), (0, model // 4 - g.shape[0] // 4))).reshape(-1)
            for g in (d_gain_query, d_gain_key)
        ],
        axis=1,
    )
    gain_rows = jnp.pad(gain_rows, ((0, 0), (0, 122)))
    tail = sum_over_ctx(
        scatter_rows(jnp.concatenate([dot_rows(first_low, pair_low), gain_rows], axis=1), mine)
    )
    grad_key, grad_value = tail[:, :HD], tail[:, HD : 2 * HD]
    gain_grads = [tail[: size, 2 * HD + i] for i, size in enumerate(sizes)]

    second_all = gather_wide(second_low)
    d_ffn_all = gather_wide(d_ffn_low)
    blocks_of_columns = wide // 256
    cuts = [blocks_of_columns * i // 3 for i in range(4)]
    ranges, downs = [], []
    for first, last in zip(cuts[:-1], cuts[1:]):
        *sides, down = ffn_gradients(mine, second_all, d_ffn_all, in_mat, down_mat, first, last)
        ranges.append([sides[0]] + [swap(sides[o], o) for o in (1, 2, 3)])
        downs.append(down)
    grad_in = unfold(mine, part, ranges)
    grad_down = lax.dynamic_slice_in_dim(join(*downs), part % 128 * (mine % 2), part, 0)

    return (
        block_out,
        grad_tokens,
        grad_query,
        grad_key,
        grad_value,
        grad_out,
        grad_in,
        grad_down,
        *gain_grads,
    )


def solution(mesh):
    in_specs = (
        P(AXES, None),
        P(AXES, None),
        P(),
        P(),
        P("fsdp", None),
        P("fsdp", None),
        P("fsdp", None),
        P("fsdp", None),
        P("fsdp", None, None),
        P("fsdp", None),
        P("fsdp"),
        P("fsdp"),
        P("fsdp"),
        P("fsdp"),
        P("fsdp"),
        P("fsdp"),
    )
    out_specs = (
        P(AXES, None),
        P(AXES, None),
        P("fsdp", None),
        P("fsdp", None),
        P("fsdp", None),
        P("fsdp", None),
        P("fsdp", None, None),
        P("fsdp", None),
        P("fsdp"),
        P("fsdp"),
        P("fsdp"),
        P("fsdp"),
        P("fsdp"),
        P("fsdp"),
    )
    return jax.shard_map(body, mesh=mesh, in_specs=in_specs, out_specs=out_specs, check_vma=False)
```

```python
import functools
import math

import jax
import jax.numpy as jnp
from jax import lax
from jax.experimental import pallas as pl
from jax.experimental.pallas import tpu as pltpu
from jax.sharding import PartitionSpec as P

H = 4
HD = 256
EPS = 1e-06
AXES = ("ctx", "fsdp")
BF = jnp.bfloat16
F32 = jnp.float32
KEY_BLOCK = 512
VMEM_LIMIT = 32 * 2**20
VMEM_ALL = 60 * 2**20


def root(values):
    return lax.rsqrt(jnp.mean(values * values, axis=-1, keepdims=True) + EPS)


def rms_back(values, gain, grad):
    scale = root(values)
    scaled = gain * grad
    mean = jnp.mean(values * scaled, axis=-1, keepdims=True)
    return (
        scale * scaled - values * (scale * scale * scale * mean),
        jnp.sum(grad * values * scale, axis=0, keepdims=True),
    )


def rotate(values, cosine, sine):
    half = values.shape[-1] // 2
    first, second = values[:, :half], values[:, half:]
    return jnp.concatenate(
        [first * cosine - second * sine, second * cosine + first * sine], axis=1
    )


class Flow:
    def __init__(self, steps):
        self.steps = steps
        self.result = None
        self.flying = next(steps)

    def land(self, arrays):
        try:
            self.flying = self.steps.send(arrays)
        except StopIteration as stop:
            self.flying, self.result = None, stop.value


def pace(values, *flows):
    flying = [flow.flying for flow in flows]
    values, flying = lax.optimization_barrier((values, flying))
    for flow, arrays in zip(flows, flying):
        flow.land(arrays)
    return values


def finish(flow):
    while flow.flying is not None:
        flow.land(flow.flying)
    return flow.result


def swap(value, offset):
    count = lax.axis_size("ctx") * lax.axis_size("fsdp")
    return lax.ppermute(value, AXES, [(i, i ^ offset) for i in range(count)])


def join(*parts):
    return jnp.concatenate(parts, axis=0)


def iter_once(arrays):
    return (yield arrays)


def gather_group(value):
    (other,) = yield [swap(value, 2)]
    pair = join(value, other)
    (other,) = yield [swap(pair, 1)]
    return pair, other


def scatter_group(keep, send):
    (other,) = yield [swap(send, 1)]
    half = keep.shape[0] // 2
    (far,) = yield [swap((keep[half:] + other[half:].astype(F32)).astype(BF), 2)]
    return keep[:half] + other[:half].astype(F32), far


def wide_offsets():
    highs = [8 * s for s in range(lax.axis_size("ctx") // 2)]
    chip = [low + high for low in (0, 4, 2, 6) for high in highs]
    return chip + [1 + o for o in chip]


def gather_wide(value):
    highs = lax.axis_size("ctx") // 2
    line = join(value, *(yield [swap(value, 8 * s) for s in range(1, highs)]))
    half = line.shape[0] // 2
    along_y, along_x = yield [swap(line, o) for o in (4, 2)]
    corner = yield [swap(along_y[:half], 2), swap(along_x[half:], 4)]
    chip = join(line, along_y, along_x, *corner)
    (other,) = yield [swap(chip, 1)]
    return chip, other


def scatter_wide(near, far):
    highs = lax.axis_size("ctx") // 2
    (other,) = yield [swap(far, 1)]
    chip = near.astype(F32) + other.astype(F32)
    line, along_y, along_x, corner = jnp.split(chip, 4, axis=0)
    mid = line.shape[0] // 2
    corner = corner.astype(BF)
    from_x, from_y = yield [swap(corner[:mid], 2), swap(corner[mid:], 4)]
    along_y = join(along_y[:mid] + from_x.astype(F32), along_y[mid:])
    along_x = join(along_x[:mid], along_x[mid:] + from_y.astype(F32))
    from_y, from_x = yield [swap(along_y.astype(BF), 4), swap(along_x.astype(BF), 2)]
    line = line + from_y.astype(F32) + from_x.astype(F32)
    rows = line.shape[0] // highs
    terms = yield [
        swap(line[s * rows : (s + 1) * rows].astype(BF), 8 * s) for s in range(1, highs)
    ]
    return [line[:rows], *terms]


def sum_over_ctx(value):
    count, me = lax.axis_size("ctx"), lax.axis_index("ctx")
    highs, low, high = count // 2, me % 2, me // 2
    half, step = value.shape[0] // 2, value.shape[0] // count
    (other,) = yield [swap(lax.dynamic_slice_in_dim(value, (1 - low) * half, half, 0).astype(BF), 4)]
    line = lax.dynamic_slice_in_dim(value, low * half, half, 0) + other.astype(F32)
    line_low = line.astype(BF)
    terms = yield [
        swap(lax.dynamic_slice_in_dim(line_low, (high ^ s) * step, step, 0), 8 * s)
        for s in range(1, highs)
    ]
    total = lax.dynamic_slice_in_dim(line, high * step, step, 0)
    total = (total + sum(term.astype(F32) for term in terms)).astype(BF)
    pieces = yield [swap(total, 8 * s) for s in range(1, highs)]
    line = line_low
    for s, piece in enumerate([total, *pieces]):
        line = lax.dynamic_update_slice_in_dim(line, piece, (high ^ s) * step, 0)
    (other,) = yield [swap(line, 4)]
    even, odd = jnp.where(low == 0, line, other), jnp.where(low == 0, other, line)
    return join(even, odd).astype(F32)


def gather_rows(value, me):
    (other,) = yield [swap(value, 2)]
    pair = join(value, other)
    (other,) = yield [swap(pair, 1)]
    return settle(me ^ jnp.array([0, 2, 1, 3], jnp.int32), value.shape[0], pair, other)


def exchange_columns(quarters):
    first, second = yield [swap(quarters[0], 2), swap(quarters[1], 3)]
    (first_z,) = yield [swap(first, 8)]
    second_z, second_y = yield [swap(second, 8), swap(second, 4)]
    first_y, first_far, second_far = yield [swap(first, 4), swap(first_z, 4), swap(second_y, 8)]
    return [(first, first_y, first_z, first_far), (second, second_y, second_z, second_far)]


def kernel_call(kernel, out_shape, *operands, scalars=(), scratch=(), name):
    whole = pl.BlockSpec(memory_space=pltpu.VMEM)
    return pl.pallas_call(
        kernel,
        out_shape=[jax.ShapeDtypeStruct(shape, dtype) for shape, dtype in out_shape],
        in_specs=[pl.BlockSpec(memory_space=pltpu.SMEM)] * len(scalars) + [whole] * len(operands),
        out_specs=[whole] * len(out_shape),
        scratch_shapes=[pltpu.VMEM(shape, dtype) for shape, dtype in scratch],
        compiler_params=pltpu.CompilerParams(vmem_limit_bytes=VMEM_LIMIT),
        name=name,
    )(*scalars, *operands)


def gains_kernel(mine, *refs):
    sources, (wide, narrow) = refs[:4], refs[4:]
    part, head_part = wide.shape[1] // 4, narrow.shape[1] // 4
    for m in range(4):

        @pl.when(mine[0] == m)
        def _(m=m):
            owners = [sources[m ^ r][...] for r in range(4)]
            for i in range(4):
                wide[i : i + 1, :] = jnp.concatenate(
                    [o[:, i * part : (i + 1) * part] for o in owners], axis=1
                )
            for i in range(2):
                first = 4 * part + i * head_part
                narrow[i : i + 1, :] = jnp.concatenate(
                    [o[:, first : first + head_part] for o in owners], axis=1
                )


def key_kernel(tokens, gain, key_gain, pair_mat, cosine, sine, first_low, key_raw, pairs):
    inputs = tokens[...].astype(F32)
    low = (inputs * root(inputs) * gain[0:1, :]).astype(BF)
    first_low[...] = low
    raw = contract(low, pair_mat[...], 1, 0)
    key = raw[:, :HD]
    key_raw[...] = key
    key = key * root(key) * key_gain[1:2, :]
    pairs[:, :HD] = rotate(key, cosine[...], sine[...]).astype(BF)
    pairs[:, HD:] = raw[:, HD:].astype(BF)


def query_kernel(first_low, query_gain, query_mat, cosine, sine, query_raw, queries):
    rows = first_low.shape[0]
    raw = contract(first_low[...], query_mat[...], 1, 0)
    query_raw[...] = raw
    for h in range(H):
        head = raw[:, h * HD : (h + 1) * HD]
        head = rotate(head * root(head) * query_gain[0:1, :], cosine[...], sine[...])
        queries[h * rows : (h + 1) * rows, :] = (head * HD ** (-0.5)).astype(BF)


def attend_kernel(blocks, q, q_place, q_start, k_near, v_near, k_far, v_far, near, far, heads, mass):
    step = pl.program_id(0)
    middle = pl.num_programs(0) // 2

    @pl.when(step == 0)
    def _():
        heads[...] = jnp.zeros_like(heads)
        mass[...] = jnp.zeros_like(mass)

    def section(k, v, probs):
        scores = contract(k[...], q[...], 1, 1)
        rows = k.shape[0]
        block = 64
        place, start = q_place[...], q_start[...]
        total = jnp.zeros_like(mass)
        for i in range(rows // block):
            first = blocks[step * (rows // block) + i] * block
            keys = first + lax.broadcasted_iota(jnp.int32, (block, scores.shape[1]), 0)
            allowed = (keys <= place) & (keys >= start)
            weights = jnp.where(allowed, jnp.exp(scores[i * block : (i + 1) * block]), 0.0)
            probs[i * block : (i + 1) * block, :] = weights.astype(BF)
            total = total + jnp.sum(weights, axis=0, keepdims=True)
        mass[...] += total
        heads[...] += contract(v[...], probs[...], 0, 0)

    @pl.when(step < middle)
    def _():
        section(k_near, v_near, near)

    @pl.when(step >= middle)
    def _():
        section(k_far, v_far, far)


def halves_of(shape, steps, column=0):
    half = steps // 2
    return [
        pl.BlockSpec(shape, lambda i, *s: (jnp.minimum(i, half - 1), column)),
        pl.BlockSpec(shape, lambda i, *s: (jnp.maximum(i - half, 0), column)),
    ]


def attend(blocks, queries, q_place, q_start, near, far):
    head_rows = queries.shape[0]
    keys = near.shape[0]
    steps = 2 * keys // KEY_BLOCK
    key_blocks, value_blocks = [halves_of((KEY_BLOCK, HD), steps, c) for c in (0, 1)]
    return pl.pallas_call(
        attend_kernel,
        grid_spec=pltpu.PrefetchScalarGridSpec(
            num_scalar_prefetch=1,
            grid=(steps,),
            in_specs=[
                pl.BlockSpec((head_rows, HD), lambda i, b: (0, 0)),
                pl.BlockSpec((1, head_rows), lambda i, b: (0, 0)),
                pl.BlockSpec((1, head_rows), lambda i, b: (0, 0)),
                key_blocks[0],
                value_blocks[0],
                key_blocks[1],
                value_blocks[1],
            ],
            out_specs=[
                *halves_of((KEY_BLOCK, head_rows), steps),
                pl.BlockSpec((HD, head_rows), lambda i, b: (0, 0)),
                pl.BlockSpec((1, head_rows), lambda i, b: (0, 0)),
            ],
        ),
        out_shape=[
            jax.ShapeDtypeStruct((keys, head_rows), BF),
            jax.ShapeDtypeStruct((keys, head_rows), BF),
            jax.ShapeDtypeStruct((HD, head_rows), F32),
            jax.ShapeDtypeStruct((1, head_rows), F32),
        ],
        compiler_params=pltpu.CompilerParams(vmem_limit_bytes=VMEM_LIMIT),
        cost_estimate=pl.CostEstimate(
            flops=8 * keys * head_rows * HD,
            bytes_accessed=2 * keys * (head_rows + 2 * HD) * 2,
            transcendentals=2 * keys * head_rows,
        ),
        name="attend",
    )(blocks, queries, q_place, q_start, near, near, far, far)


def turned_line(column):
    return jnp.broadcast_to(column, (column.shape[0], 128)).T[0:1, :]


def after_attend_kernel(weighted, mass, out_mat, tokens, gains, heads, heads_low, attn_raw, hidden, second_low):
    rows = tokens.shape[0]
    heads[...] = (weighted[...] * (1.0 / mass[...])).T
    for h in range(H):
        heads_low[:, h * HD : (h + 1) * HD] = heads[h * rows : (h + 1) * rows, :].astype(BF)
    raw = contract(heads_low[...], out_mat[...], 1, 0)
    attn_raw[...] = raw
    total = tokens[...].astype(F32) + raw * root(raw) * gains[1:2, :]
    hidden[...] = total
    second_low[...] = (total * root(total) * gains[2:3, :]).astype(BF)


def after_ffn_kernel(part, other, hidden, cotangent, gains, block_out, d_ffn_low, d_gain):
    raw = part[...] + other[...].astype(F32)
    block_out[...] = (hidden[...] + raw * root(raw) * gains[3:4, :]).astype(BF)
    d_ffn, d_gain[...] = rms_back(raw, gains[3:4, :], cotangent[...].astype(F32))
    d_ffn_low[...] = d_ffn.astype(BF)


def before_attend_back_kernel(
    part, other, hidden, cotangent, gains, attn_raw, out_mat, heads,
    d_hidden, d_attn_low, d_heads, dots, d_gain_ffn_in, d_gain_attn_out,
):
    rows = part.shape[0]
    d_second = part[...] + other[...].astype(F32)
    extra, d_gain_ffn_in[...] = rms_back(hidden[...], gains[2:3, :], d_second)
    total = cotangent[...].astype(F32) + extra
    d_hidden[...] = total
    d_attn, d_gain_attn_out[...] = rms_back(attn_raw[...], gains[1:2, :], total)
    low = d_attn.astype(BF)
    d_attn_low[...] = low
    for h in range(H):
        at = pl.ds(h * rows, rows)
        head = contract(low, out_mat[h * HD : (h + 1) * HD, :], 1, 1).astype(BF)
        d_heads[at, :] = head
        dots[:, at] = turned_line(
            jnp.sum(head.astype(F32) * heads[at, :], axis=1, keepdims=True)
        )


def attend_back_kernel(
    q, d_heads, mass, dots, near, far, k_near, v_near, k_far, v_far, d_queries, d_near, d_far
):
    step = pl.program_id(0)
    middle = pl.num_programs(0) // 2

    @pl.when(step == 0)
    def _():
        d_queries[...] = jnp.zeros_like(d_queries)

    def section(probs, k, v, out):
        d_probs = contract(v[...], d_heads[...], 1, 1)
        chance = probs[...].astype(F32) * (1.0 / mass[...])
        d_scores = (chance * (d_probs - dots[...])).astype(BF)
        out[:, :HD] = contract(d_scores, q[...], 1, 0).astype(BF)
        out[:, HD:] = contract(chance.astype(BF), d_heads[...], 1, 0).astype(BF)
        d_queries[...] += contract(k[...], d_scores, 0, 0)

    @pl.when(step < middle)
    def _():
        section(near, k_near, v_near, d_near)

    @pl.when(step >= middle)
    def _():
        section(far, k_far, v_far, d_far)


def attend_back(queries, d_heads, mass, dots, probs, pairs):
    head_rows = queries.shape[0]
    keys = pairs[0].shape[0]
    steps = 2 * keys // KEY_BLOCK
    whole = pl.BlockSpec((head_rows, HD), lambda i: (0, 0))
    line = pl.BlockSpec((1, head_rows), lambda i: (0, 0))
    key_blocks, value_blocks = [halves_of((KEY_BLOCK, HD), steps, c) for c in (0, 1)]
    return pl.pallas_call(
        attend_back_kernel,
        grid=(steps,),
        in_specs=[
            whole,
            whole,
            line,
            line,
            *halves_of((KEY_BLOCK, head_rows), steps),
            key_blocks[0],
            value_blocks[0],
            key_blocks[1],
            value_blocks[1],
        ],
        out_specs=[
            pl.BlockSpec((HD, head_rows), lambda i: (0, 0)),
            *halves_of((KEY_BLOCK, 2 * HD), steps),
        ],
        out_shape=[
            jax.ShapeDtypeStruct((HD, head_rows), F32),
            jax.ShapeDtypeStruct((keys, 2 * HD), BF),
            jax.ShapeDtypeStruct((keys, 2 * HD), BF),
        ],
        compiler_params=pltpu.CompilerParams(vmem_limit_bytes=VMEM_LIMIT),
        cost_estimate=pl.CostEstimate(
            flops=16 * keys * head_rows * HD,
            bytes_accessed=2 * keys * (head_rows + 4 * HD) * 2,
            transcendentals=0,
        ),
        name="attend_back",
    )(queries, d_heads, mass, dots, *probs, pairs[0], pairs[0], pairs[1], pairs[1])


def spread_rows(product, mine, size, keep, send, first):
    step = keep.shape[0] // 2
    width = product.shape[1]
    for offset in range(4):
        rows = product[pl.ds(pl.multiple_of((mine ^ offset) * size, 32), size), :]
        out = send if offset % 2 else keep
        begin = offset // 2 * step + first
        out[begin : begin + size, :width] = rows.astype(out.dtype)


def query_back_kernel(
    mine, d_queries, query_raw, gains, cosine, sine, query_mat, first_low, heads_low, d_attn_low,
    keep, send, d_first, d_gain, product, out_product, query_low,
):
    rows = first_low.shape[0]
    gain = gains[0:1, :]
    d_gain[...] = jnp.zeros_like(d_gain)
    for h in range(H):
        columns = pl.ds(h * HD, HD)
        head = d_queries[:, h * rows : (h + 1) * rows].T * HD ** (-0.5)
        head = rotate(head, cosine[...], -sine[...])
        d_raw, d_head_gain = rms_back(query_raw[:, columns], gain, head)
        d_gain[...] += d_head_gain
        query_low[:, columns] = d_raw.astype(BF)
    d_first[...] = contract(query_low[...], query_mat[...], 1, 1)
    model, inner = product.shape[0] // 4, out_product.shape[0] // 4
    keep[...] = jnp.zeros_like(keep)
    send[...] = jnp.zeros_like(send)
    product[...] = contract(first_low[...], query_low[...], 0, 0)
    spread_rows(product, mine[0], model, keep, send, 0)
    out_product[...] = contract(heads_low[...], d_attn_low[...], 0, 0)
    spread_rows(out_product, mine[0], inner, keep, send, model)


def key_back_kernel(
    mine, sums, *refs
):
    terms, refs = refs[:-19], refs[-19:]
    (
        key_raw, gains, head_gains, cosine, sine, pair_mat, first_low, d_first_query, tokens, d_hidden,
        d_gain_attn_out, d_gain_ffn_in, d_gain_ffn_out, d_gain_query,
        grad_tokens, keep, send, product, gain_lines,
    ) = refs
    total = sums[...]
    for term in terms:
        total = total + term[...].astype(F32)
    d_key = rotate(total[:, :HD], cosine[...], -sine[...])
    d_raw, d_gain_key = rms_back(key_raw[...], head_gains[1:2, :], d_key)
    low = jnp.concatenate([d_raw, total[:, HD:]], axis=1).astype(BF)
    d_first = d_first_query[...] + contract(low, pair_mat[...], 1, 1)
    extra, d_gain_attn_in = rms_back(tokens[...].astype(F32), gains[0:1, :], d_first)
    grad_tokens[...] = d_hidden[...] + extra
    product[:, : 2 * HD] = contract(first_low[...], low, 0, 0)
    gain_lines[...] = jnp.zeros_like(gain_lines)
    for i, line in enumerate(
        (d_gain_attn_in, d_gain_attn_out[...], d_gain_ffn_in[...], d_gain_ffn_out[...])
    ):
        gain_lines[i : i + 1, :] = line
    size, head_size = product.shape[0] // 4, HD // 4
    for i, line in enumerate((d_gain_query[...], d_gain_key)):
        pieces = []
        for r in range(4):
            pieces += [line[:, r * head_size : (r + 1) * head_size], jnp.zeros((1, size - head_size), F32)]
        gain_lines[4 + i : 5 + i, :] = jnp.concatenate(pieces, axis=1)
    product[:, 2 * HD :] = gain_lines[...].T
    keep[...] = jnp.zeros_like(keep)
    send[...] = jnp.zeros_like(send)
    spread_rows(product, mine[0], size, keep, send, 0)


def left_of(owner, part):
    return pl.multiple_of(owner * part - part % 128 * (owner % 2), 128)


def carve_kernel(part, place, w, own, core, near, corner):
    wide, step = own.shape[2], pl.program_id(0)
    mine, low, high = place[0], place[1], place[2]
    for offset, out in enumerate((own, core)):
        out[...] = w[:, :, pl.ds(left_of(mine ^ offset, part), wide)]

    @pl.when(step // (pl.num_programs(0) // 2) == low)
    def _():
        for offset, out in ((2, near), (3, corner)):
            out[...] = w[pl.ds(high, 1), :, pl.ds(left_of(mine ^ offset, part), wide)]


def carve(w, place, part, wide):
    rows, step = w.shape[1], 48
    half = rows // 2 // step

    def quarter(i, p):
        return (0, jnp.clip(i - half * p[1], 0, half - 1), 0)

    return pl.pallas_call(
        functools.partial(carve_kernel, part),
        grid_spec=pltpu.PrefetchScalarGridSpec(
            num_scalar_prefetch=1,
            grid=(rows // step,),
            in_specs=[pl.BlockSpec((2, step, w.shape[2]), lambda i, p: (0, i, 0))],
            out_specs=[pl.BlockSpec((2, step, wide), lambda i, p: (0, i, 0))] * 2
            + [pl.BlockSpec((1, step, wide), quarter)] * 2,
        ),
        out_shape=[jax.ShapeDtypeStruct((2, rows, wide), BF)] * 2
        + [jax.ShapeDtypeStruct((1, rows // 2, wide), BF)] * 2,
        compiler_params=pltpu.CompilerParams(vmem_limit_bytes=VMEM_LIMIT),
        name="carve",
    )(place, w)


def walk(shape, first, count, scalars, dim=0):
    def place(i, *unused):
        return tuple(jnp.clip(i - first, 0, count - 1) if d == dim else 0 for d in range(len(shape)))

    return pl.BlockSpec(shape, place)


def settle_kernel(counts, places, *refs):
    out, sources = refs[-1], refs[:-1]
    step, first = pl.program_id(0), 0
    for source, count in zip(sources, counts):

        @pl.when((step >= first) & (step < first + count))
        def _(source=source):
            out[...] = source[...]

        first += count


def settle(places, rows, *sources):
    counts = [source.shape[0] // rows for source in sources]
    width = sources[0].shape[1]
    starts = [sum(counts[:i]) for i in range(len(counts))]
    return pl.pallas_call(
        functools.partial(settle_kernel, counts),
        grid_spec=pltpu.PrefetchScalarGridSpec(
            num_scalar_prefetch=1,
            grid=(sum(counts),),
            in_specs=[walk((rows, width), f, c, 1) for f, c in zip(starts, counts)],
            out_specs=pl.BlockSpec((rows, width), lambda i, p: (p[i], 0)),
        ),
        out_shape=jax.ShapeDtypeStruct((sum(counts) * rows, width), sources[0].dtype),
        compiler_params=pltpu.CompilerParams(vmem_limit_bytes=VMEM_LIMIT),
        name="settle",
    )(places, *sources)


def lay_kernel(sides, rows, *refs):
    out, sources = refs[-1], refs[:-1]
    step = pl.program_id(0)
    width = out.shape[3]
    for i, source in enumerate([sources[0]] * 4 + [sources[1]] * 4 + list(sources[2:])):

        @pl.when(step == i)
        def _(source=source):
            for block in range(out.shape[1]):
                out[0, block] = source[0, :, block * width : (block + 1) * width]


def lay(sides, rows, own, core, quarters):
    half, wide = own.shape[1] // 2, own.shape[2]
    shape = (1, half, wide)

    def run(first):
        def place(i, s, r):
            j = jnp.clip(i - first, 0, 3)
            return (j // 2, j % 2, 0)

        return pl.BlockSpec(shape, place)

    still = pl.BlockSpec(shape, lambda i, s, r: (0, 0, 0))
    return pl.pallas_call(
        lay_kernel,
        grid_spec=pltpu.PrefetchScalarGridSpec(
            num_scalar_prefetch=2,
            grid=(16,),
            in_specs=[run(0), run(4)] + [still] * 8,
            out_specs=pl.BlockSpec(
                (1, wide // 256, half, 256), lambda i, s, r: (s[i], 0, r[i], 0)
            ),
        ),
        out_shape=jax.ShapeDtypeStruct((2, wide // 256, 8 * half, 256), BF),
        compiler_params=pltpu.CompilerParams(vmem_limit_bytes=VMEM_LIMIT),
        name="lay",
    )(sides, rows, own, core, *quarters)


def contract(left, right, left_dim, right_dim):
    return lax.dot_general(
        left, right, (((left_dim,), (right_dim,)), ((), ())), preferred_element_type=F32
    )


def gelu_and_slope(x):
    scale = math.sqrt(2.0 / math.pi)
    square = x * x
    turn = jnp.tanh(x * (scale + (scale * 0.044715) * square))
    share = 0.5 + 0.5 * turn
    slope = share + (0.5 * x) * (1.0 - turn * turn) * (scale + (3 * scale * 0.044715) * square)
    return x * share, slope


def ffn_factors_kernel(second, w_gate, w_up, act, value, factor):
    rows, slab = second.shape[0], 256

    def products(r):
        at = pl.ds(r * slab, slab)
        return contract(second[at, :], w_gate[0, 0], 1, 0), contract(second[at, :], w_up[0, 0], 1, 0)

    ahead = products(0)
    for r in range(rows // slab):
        at = pl.ds(r * slab, slab)
        gate, upper = ahead
        if r + 1 < rows // slab:
            ahead = products(r + 1)
        gelu, slope = gelu_and_slope(gate)
        act[at, :] = (gelu * upper).astype(BF)
        value[at, :] = gelu.astype(BF)
        factor[at, :] = (upper * slope).astype(BF)


def ffn_factors(second_all, in_mat, first, last):
    tokens, model = second_all.shape
    slab, width = min(2048, tokens), 256
    columns = (last - first) * width
    return pl.pallas_call(
        ffn_factors_kernel,
        grid=(last - first, tokens // slab),
        in_specs=[
            pl.BlockSpec((slab, model), lambda j, t: (t, 0)),
            pl.BlockSpec((1, 1, model, width), lambda j, t: (0, j + first, 0, 0)),
            pl.BlockSpec((1, 1, model, width), lambda j, t: (1, j + first, 0, 0)),
        ],
        out_specs=[pl.BlockSpec((slab, width), lambda j, t: (t, j))] * 3,
        out_shape=[jax.ShapeDtypeStruct((tokens, columns), BF)] * 3,
        compiler_params=pltpu.CompilerParams(vmem_limit_bytes=VMEM_ALL),
        cost_estimate=pl.CostEstimate(
            flops=4 * tokens * model * columns,
            bytes_accessed=2 * tokens * model * (last - first) + 6 * tokens * columns,
            transcendentals=tokens * columns,
        ),
        name="ffn_factors",
    )(second_all, in_mat, in_mat)


def ffn_gradients_kernel(part, first, blocks, mine, second, d_ffn, act, value, factor, w_down, *rest):
    outs, down_rows, d_both, both_sum, down_sum, sem = rest[-9:-5], *rest[-5:]
    step = pl.program_id(1)
    rows, slab = second.shape[0], 256
    width = act.shape[1]

    def products(r):
        return contract(d_ffn[pl.ds(r * slab, slab), :], w_down[...], 1, 1)

    ahead = products(0)
    for r in range(rows // slab):
        at = pl.ds(r * slab, slab)
        d_act = ahead
        if r + 1 < rows // slab:
            ahead = products(r + 1)
        d_both[at, :width] = (d_act * factor[at, :].astype(F32)).astype(BF)
        d_both[at, width:] = (d_act * value[at, :].astype(F32)).astype(BF)
    grad_both = contract(second[...], d_both[...], 0, 0)
    grad_down = contract(act[...], d_ffn[...], 0, 0)

    @pl.when(step == 0)
    def _():
        both_sum[...] = grad_both
        down_sum[...] = grad_down

    @pl.when(step > 0)
    def _():
        both_sum[...] += grad_both
        down_sum[...] += grad_down

    @pl.when(step == pl.num_programs(1) - 1)
    def _():
        block = first + pl.program_id(0)
        odd = mine[0] % 2
        extra = blocks * width - part
        begins = (block == 0) & (odd == 1)
        ends = (block == blocks - 1) & (odd == 0)

        def put(source, at, size):
            copy = pltpu.make_async_copy(
                down_sum.at[pl.ds(source, size), :], down_rows.at[pl.ds(at, size), :], sem
            )
            copy.start()
            copy.wait()

        @pl.when(begins)
        def _():
            put(extra, 0, width - extra)

        @pl.when(ends)
        def _():
            put(0, (blocks - 1) * width, width - extra)

        @pl.when(jnp.logical_not(begins | ends))
        def _():
            put(0, pl.multiple_of(block * width - odd * extra, 64), width)

        quarter = second.shape[1] // 4
        for offset, out in enumerate(outs):
            at = pl.ds(pl.multiple_of((mine[0] ^ offset) * quarter, 32), quarter)
            out[0] = both_sum[at, :width].astype(BF)
            out[1] = both_sum[at, width:].astype(BF)


def ffn_gradients(mine, second_all, d_ffn_all, factors, down_mat, part, first, last, down_rows):
    tokens, model = second_all.shape
    slab, width = min(2048, tokens), 256
    columns = (last - first) * width
    tall = pl.BlockSpec((slab, model), lambda j, t, m: (t, 0))
    tile = pl.BlockSpec((slab, width), lambda j, t, m: (t, j))
    anywhere = pl.BlockSpec(memory_space=pl.ANY)
    earlier = [] if down_rows is None else [down_rows]
    return pl.pallas_call(
        functools.partial(ffn_gradients_kernel, part, first, down_mat.shape[0] // width),
        grid_spec=pltpu.PrefetchScalarGridSpec(
            num_scalar_prefetch=1,
            grid=(last - first, tokens // slab),
            in_specs=[
                tall,
                tall,
                tile,
                tile,
                tile,
                pl.BlockSpec((width, model), lambda j, t, m: (j + first, 0)),
            ]
            + [anywhere] * len(earlier),
            out_specs=[pl.BlockSpec((2, model // 4, width), lambda j, t, m: (0, 0, j))] * 4
            + [anywhere],
            scratch_shapes=[
                pltpu.VMEM((slab, 2 * width), BF),
                pltpu.VMEM((model, 2 * width), F32),
                pltpu.VMEM((width, model), F32),
                pltpu.SemaphoreType.DMA,
            ],
        ),
        out_shape=[jax.ShapeDtypeStruct((2, model // 4, columns), BF)] * 4
        + [jax.ShapeDtypeStruct((part, model), F32)],
        input_output_aliases={7: 4} if earlier else {},
        compiler_params=pltpu.CompilerParams(vmem_limit_bytes=VMEM_ALL),
        cost_estimate=pl.CostEstimate(
            flops=8 * tokens * model * columns,
            bytes_accessed=4 * tokens * model * (last - first) + 6 * tokens * columns,
            transcendentals=0,
        ),
        name="ffn_gradients",
    )(mine[None], second_all, d_ffn_all, *factors, down_mat, *earlier)


def ffn_forward_kernel(near, far, w_gate, w_up, w_down, gate, up, keep, send, act, total):
    step, half = pl.program_id(0), near.shape[0]

    @pl.when(step == 0)
    def _():
        total[...] = jnp.zeros_like(total)

    def products(rows):
        return contract(rows[...], w_gate[0, 0], 1, 0), contract(rows[...], w_up[0, 0], 1, 0)

    ahead = products(near)
    for i in range(2):
        at = pl.ds(i * half, half)
        left, right = ahead
        if i == 0:
            ahead = products(far)
        gate[at, :], up[at, :] = left, right
        act[at, :] = (gelu_and_slope(left)[0] * right).astype(BF)
    total[...] += contract(act[...], w_down[...], 1, 0)

    @pl.when(step == pl.num_programs(0) - 1)
    def _():
        keep[...], send[...] = total[:half, :], total[half:, :].astype(BF)


def ffn_backward_kernel(near, far, gate, up, w_gate, w_up, w_down, keep, send, d_gate, d_up, total):
    step, half = pl.program_id(0), near.shape[0]

    @pl.when(step == 0)
    def _():
        total[...] = jnp.zeros_like(total)

    ahead = contract(near[...], w_down[...], 1, 1)
    for i in range(2):
        at = pl.ds(i * half, half)
        d_act = ahead
        if i == 0:
            ahead = contract(far[...], w_down[...], 1, 1)
        value, slope = gelu_and_slope(gate[at, :])
        d_gate[at, :] = (d_act * up[at, :] * slope).astype(BF)
        d_up[at, :] = (d_act * value).astype(BF)
    total[...] += contract(d_gate[...], w_gate[0, 0], 1, 1) + contract(d_up[...], w_up[0, 0], 1, 1)

    @pl.when(step == pl.num_programs(0) - 1)
    def _():
        keep[...], send[...] = total[:half, :], total[half:, :].astype(BF)


def ffn_group(kernel, near, far, in_mat, down_mat, *kept):
    half, model = near.shape
    wide, width = down_mat.shape[0], 256
    rows = pl.BlockSpec((half, model), lambda j: (0, 0))
    column = pl.BlockSpec((2 * half, width), lambda j: (0, j))
    forward = not kept
    shape = jax.ShapeDtypeStruct((2 * half, wide), F32)
    return pl.pallas_call(
        kernel,
        grid=(wide // width,),
        in_specs=[rows, rows]
        + [column] * len(kept)
        + [
            pl.BlockSpec((1, 1, model, width), lambda j: (0, j, 0, 0)),
            pl.BlockSpec((1, 1, model, width), lambda j: (1, j, 0, 0)),
            pl.BlockSpec((width, model), lambda j: (j, 0)),
        ],
        out_specs=[column] * (2 * forward) + [rows, rows],
        out_shape=[shape] * (2 * forward)
        + [jax.ShapeDtypeStruct((half, model), F32), jax.ShapeDtypeStruct((half, model), BF)],
        scratch_shapes=[pltpu.VMEM((2 * half, width), BF)] * (1 if forward else 2)
        + [pltpu.VMEM((2 * half, model), F32)],
        compiler_params=pltpu.CompilerParams(vmem_limit_bytes=VMEM_ALL),
        cost_estimate=pl.CostEstimate(
            flops=12 * half * model * wide,
            bytes_accessed=6 * model * wide + 16 * half * wide,
            transcendentals=2 * half * wide,
        ),
        name="ffn_forward" if forward else "ffn_backward",
    )(near, far, *kept, in_mat, in_mat, down_mat)


def unfold_kernel(part, mine, *refs):
    out, sources = refs[-1], refs[:-1]
    ranges = len(sources) // 4
    extra = part % 128
    for m in range(4):

        @pl.when(mine[0] == m)
        def _(m=m):
            for side in range(2):
                rows = [
                    jnp.concatenate(
                        [sources[r * 4 + (m ^ owner)][side] for r in range(ranges)], axis=1
                    ).astype(F32)
                    for owner in range(4)
                ]
                wide = rows[0].shape[1]
                cut = wide - 128
                left = lax.broadcasted_iota(jnp.int32, (rows[0].shape[0], 128), 1) < extra
                pieces = []
                for even, odd in (rows[:2], rows[2:]):
                    shared = jnp.where(left, even[:, cut:], odd[:, :128])
                    pieces += [even[:, :cut], shared, odd[:, 128:]]
                out[:, side, :] = jnp.concatenate(pieces, axis=1)


def unfold(mine, part, ranges):
    sources = [piece for pieces in ranges for piece in pieces]
    rows, step = sources[0].shape[1], 16
    return pl.pallas_call(
        functools.partial(unfold_kernel, part),
        grid_spec=pltpu.PrefetchScalarGridSpec(
            num_scalar_prefetch=1,
            grid=(rows // step,),
            in_specs=[
                pl.BlockSpec((2, step, s.shape[2]), lambda i, m: (0, i, 0)) for s in sources
            ],
            out_specs=pl.BlockSpec((step, 2, 4 * part), lambda i, m: (i, 0, 0)),
        ),
        out_shape=jax.ShapeDtypeStruct((rows, 2, 4 * part), F32),
        compiler_params=pltpu.CompilerParams(vmem_limit_bytes=VMEM_LIMIT),
        name="unfold",
    )(mine[None], *sources)


def pick(table, index):
    hit = index[:, None] == jnp.arange(table.shape[0], dtype=jnp.int32)[None, :]
    return jnp.sum(jnp.where(hit, table[None, :], 0), axis=1)


def body(
    tokens,
    cotangent,
    block_table,
    sequence_ids,
    w_query,
    w_key,
    w_value,
    w_out,
    w_in,
    w_down,
    gain_attn_in,
    gain_attn_out,
    gain_ffn_in,
    gain_ffn_out,
    gain_query,
    gain_key,
):
    rows = tokens.shape[0]
    block = rows // 2
    model, part = w_in.shape[0] * 4, w_down.shape[0]
    mine = lax.axis_index("fsdp")
    me = lax.axis_index("ctx") * 4 + mine

    gains = (gain_attn_in, gain_attn_out, gain_ffn_in, gain_ffn_out, gain_query, gain_key)
    sizes = [g.shape[0] for g in gains]
    pair_flow = Flow(gather_rows(jnp.concatenate([w_key, w_value], axis=1), mine))
    packed = jnp.concatenate(gains).astype(F32)[None]
    gains_flow = Flow(iter_once([swap(packed, o) for o in (1, 2, 3)]))

    wide = -(-part // 256) * 256
    quarter = model // 4
    boundary = jnp.sum((sequence_ids == 0).astype(jnp.int32))
    everyone = me ^ jnp.array(wide_offsets(), jnp.int32)
    blocks = pick(block_table, jnp.stack([2 * everyone, 2 * everyone + 1], axis=1).reshape(-1))
    place = (blocks[:2, None] * block + jnp.arange(block, dtype=jnp.int32)[None, :]).reshape(-1)
    start = jnp.where(place >= boundary, boundary, 0)
    position = place - start
    inverse_angle = 1000000.0 ** (-jnp.arange(HD // 2, dtype=F32) / (HD // 2))
    angles = position.astype(F32)[:, None] * inverse_angle[None, :]
    cosine, sine = jnp.cos(angles), jnp.sin(angles)
    q_place, q_start = jnp.tile(place, H)[None], jnp.tile(start, H)[None]

    low_bit, high_bit = lax.axis_index("ctx") % 2, lax.axis_index("ctx") // 2 % 2
    own, to_core, to_x, to_corner = carve(
        jnp.swapaxes(w_in, 0, 1), jnp.stack([mine, low_bit, high_bit]), part, wide
    )
    own, to_core, to_x, to_corner = pace((own, to_core, to_x, to_corner), pair_flow)
    columns_flow = Flow(exchange_columns((to_x, to_corner)))

    cosine, sine, q_place, q_start, w_query = pace(
        (cosine, sine, q_place, q_start, w_query), gains_flow, pair_flow
    )
    query_flow = Flow(gather_rows(w_query, mine))
    model_gains, head_gains = kernel_call(
        gains_kernel,
        [((8, model), F32), ((8, HD), F32)],
        packed,
        *gains_flow.result,
        scalars=(mine[None],),
        name="gains",
    )
    pair_mat = pair_flow.result
    first_low, key_raw, pair_rows = kernel_call(
        key_kernel,
        [((rows, model), BF), ((rows, HD), F32), ((rows, 2 * HD), BF)],
        tokens,
        model_gains,
        head_gains,
        pair_mat,
        cosine,
        sine,
        name="keys",
    )
    pairs_flow = Flow(gather_wide(pair_rows))
    pace((), pairs_flow, columns_flow)
    to_core, w_out, w_down = pace(
        (to_core, w_out, w_down), pairs_flow, query_flow, columns_flow
    )
    out_flow = Flow(gather_rows(w_out, mine))
    from_core = swap(to_core, 1)
    query_mat = finish(query_flow)
    query_raw, queries = kernel_call(
        query_kernel,
        [((rows, H * HD), F32), ((H * rows, HD), BF)],
        first_low,
        head_gains,
        query_mat,
        cosine,
        sine,
        name="queries",
    )
    down_mat = lax.dynamic_update_slice_in_dim(
        jnp.zeros((wide, model), BF), w_down, part % 128 * (mine % 2), 0
    )
    queries, down_mat = pace((queries, down_mat), pairs_flow, columns_flow)
    pairs = finish(pairs_flow)
    *probs, weighted, mass = attend(blocks, queries, q_place, q_start, *pairs)
    weighted, mass = pace((weighted, mass), out_flow)
    out_mat = finish(out_flow)
    heads, heads_low, attn_raw, hidden, second_low = kernel_call(
        after_attend_kernel,
        [
            ((H * rows, HD), F32),
            ((rows, H * HD), BF),
            ((rows, model), F32),
            ((rows, model), F32),
            ((rows, model), BF),
        ],
        weighted,
        mass,
        out_mat,
        tokens,
        model_gains,
        name="after_attend",
    )

    group_flow = Flow(gather_group(second_low))
    second_all = lax.all_gather(second_low, AXES, axis=0, tiled=True)
    sides, halves = [], []
    for offset in (0, 1):
        sides += [0, 0, 1, 1]
        halves += [(mine ^ offset) * 2 + bit for bit in (0, 1, 0, 1)]
    for offset in (2, 3):
        sides += [high_bit, high_bit, 1 - high_bit, 1 - high_bit]
        halves += [(mine ^ offset) * 2 + bit for bit in (low_bit, 1 - low_bit) * 2]
    pace((), group_flow, columns_flow)
    from_x, from_corner = finish(columns_flow)
    in_mat = lay(
        jnp.stack([jnp.asarray(s, jnp.int32) for s in sides]),
        jnp.stack(halves),
        own,
        from_core,
        (*from_x, *from_corner),
    )
    gate, upper, keep, send = ffn_group(ffn_forward_kernel, *finish(group_flow), in_mat, down_mat)
    block_out, d_ffn_low, d_gain_ffn_out = kernel_call(
        after_ffn_kernel,
        [((rows, model), BF), ((rows, model), BF), ((1, model), F32)],
        *finish(Flow(scatter_group(keep, send))),
        hidden,
        cotangent,
        model_gains,
        name="after_ffn",
    )
    group_flow = Flow(gather_group(d_ffn_low))
    d_ffn_all = lax.all_gather(d_ffn_low, AXES, axis=0, tiled=True)
    keep, send = ffn_group(
        ffn_backward_kernel, *finish(group_flow), in_mat, down_mat, gate, upper
    )
    d_hidden, d_attn_low, d_heads, dots, d_gain_ffn_in, d_gain_attn_out = kernel_call(
        before_attend_back_kernel,
        [
            ((rows, model), F32),
            ((rows, model), BF),
            ((H * rows, HD), BF),
            ((1, H * rows), F32),
            ((1, model), F32),
            ((1, model), F32),
        ],
        *finish(Flow(scatter_group(keep, send))),
        hidden,
        cotangent,
        model_gains,
        attn_raw,
        out_mat,
        heads,
        name="before_attend_back",
    )

    d_queries, *d_pairs = attend_back(queries, d_heads, mass, dots, probs, pairs)
    sums_flow = Flow(scatter_wide(*d_pairs))
    early_rows = -(-(quarter + H * HD // 4) // 128) * 128
    tail_rows = -(-quarter // 128) * 128
    keep, send, d_first_query, d_gain_query = kernel_call(
        query_back_kernel,
        [
            ((2 * early_rows, model), F32),
            ((2 * early_rows, model), BF),
            ((rows, model), F32),
            ((1, HD), F32),
        ],
        d_queries,
        query_raw,
        head_gains,
        cosine,
        sine,
        query_mat,
        first_low,
        heads_low,
        d_attn_low,
        scalars=(mine[None],),
        scratch=[((model, H * HD), F32), ((H * HD, model), F32), ((rows, H * HD), BF)],
        name="query_back",
    )
    blocks_of_columns = wide // 256
    cuts = [0] + [blocks_of_columns - 2 * i for i in (3, 2, 1, 0)]
    factors = []

    def factors_step(index, values, *flows):
        values, second = values
        factors.append(ffn_factors(second, in_mat, cuts[index], cuts[index + 1]))
        (values, second), factors[-1] = pace(((values, second), factors[-1]), *flows)
        return values, second

    keep, send, d_first_query, second_all = pace(
        (keep, send, d_first_query, second_all), sums_flow
    )
    early_flow = Flow(scatter_group(keep, send))
    d_first_query, second_all = factors_step(0, (d_first_query, second_all), sums_flow, early_flow)
    d_first_query, second_all = factors_step(1, (d_first_query, second_all), sums_flow)
    d_first_query, second_all = factors_step(2, (d_first_query, second_all), sums_flow, early_flow)
    grad_tokens, keep, send = kernel_call(
        key_back_kernel,
        [
            ((rows, model), F32),
            ((2 * tail_rows, 2 * HD + 128), F32),
            ((2 * tail_rows, 2 * HD + 128), BF),
        ],
        *sums_flow.result,
        key_raw,
        model_gains,
        head_gains,
        cosine,
        sine,
        pair_mat,
        first_low,
        d_first_query,
        tokens,
        d_hidden,
        d_gain_attn_out,
        d_gain_ffn_in,
        d_gain_ffn_out,
        d_gain_query,
        scalars=(mine[None],),
        scratch=[((model, 2 * HD + 128), F32), ((128, model), F32)],
        name="key_back",
    )
    tail_flow = Flow(scatter_group(keep, send))

    def total(flow):
        near, far = flow.result
        return near + far.astype(F32)

    early_flow = Flow(sum_over_ctx(total(early_flow)))
    grad_tokens, second_all = factors_step(3, (grad_tokens, second_all), tail_flow, early_flow)
    both = pace((second_all, d_ffn_all))
    ranges, grad_down = [], None

    def columns_step(*flows):
        nonlocal both, grad_down
        i = len(ranges)
        *pieces, grad_down = ffn_gradients(
            mine, *both, factors[i], down_mat, part, cuts[i], cuts[i + 1], grad_down
        )
        both, grad_down, ranges[:] = pace((both, grad_down, list(ranges)), *flows)
        ranges.append([pieces[0]] + [swap(pieces[o], o) for o in (1, 2, 3)])

    columns_step(tail_flow, early_flow)
    tail_flow = Flow(sum_over_ctx(total(tail_flow)))
    columns_step(tail_flow, early_flow)
    columns_step(tail_flow, early_flow)
    columns_step(tail_flow)
    finish(tail_flow)
    early, tail = early_flow.result, tail_flow.result
    grad_query = early[:quarter, : H * HD]
    grad_out = early[quarter : quarter + w_out.shape[0]]
    grad_key, grad_value = tail[:quarter, :HD], tail[:quarter, HD : 2 * HD]
    gain_grads = [tail[:size, 2 * HD + i] for i, size in enumerate(sizes)]
    grad_in = unfold(mine, part, ranges)

    return (
        block_out,
        grad_tokens,
        grad_query,
        grad_key,
        grad_value,
        grad_out,
        grad_in,
        grad_down,
        *gain_grads,
    )


def solution(mesh):
    in_specs = (
        P(AXES, None),
        P(AXES, None),
        P(),
        P(),
        P("fsdp", None),
        P("fsdp", None),
        P("fsdp", None),
        P("fsdp", None),
        P("fsdp", None, None),
        P("fsdp", None),
        P("fsdp"),
        P("fsdp"),
        P("fsdp"),
        P("fsdp"),
        P("fsdp"),
        P("fsdp"),
    )
    out_specs = (
        P(AXES, None),
        P(AXES, None),
        P("fsdp", None),
        P("fsdp", None),
        P("fsdp", None),
        P("fsdp", None),
        P("fsdp", None, None),
        P("fsdp", None),
        P("fsdp"),
        P("fsdp"),
        P("fsdp"),
        P("fsdp"),
        P("fsdp"),
        P("fsdp"),
    )
    return jax.shard_map(body, mesh=mesh, in_specs=in_specs, out_specs=out_specs, check_vma=False)
```

```python
import functools
import math

import jax
import jax.numpy as jnp
from jax import lax
from jax.experimental import pallas as pl
from jax.experimental.pallas import tpu as pltpu
from jax.sharding import PartitionSpec as P

H = 4
HD = 256
EPS = 1e-06
AXES = ("ctx", "fsdp")
BF = jnp.bfloat16
F32 = jnp.float32
KEY_BLOCK = 512
VMEM_LIMIT = 32 * 2**20
VMEM_ALL = 60 * 2**20


def root(values):
    return lax.rsqrt(jnp.mean(values * values, axis=-1, keepdims=True) + EPS)


def rms_back(values, gain, grad):
    scale = root(values)
    scaled = gain * grad
    mean = jnp.mean(values * scaled, axis=-1, keepdims=True)
    return (
        scale * scaled - values * (scale * scale * scale * mean),
        jnp.sum(grad * values * scale, axis=0, keepdims=True),
    )


def rotate(values, cosine, sine):
    half = values.shape[-1] // 2
    first, second = values[:, :half], values[:, half:]
    return jnp.concatenate(
        [first * cosine - second * sine, second * cosine + first * sine], axis=1
    )


class Flow:
    def __init__(self, steps):
        self.steps = steps
        self.result = None
        self.flying = next(steps)

    def land(self, arrays):
        try:
            self.flying = self.steps.send(arrays)
        except StopIteration as stop:
            self.flying, self.result = None, stop.value


def pace(values, *flows):
    flying = [flow.flying for flow in flows]
    values, flying = lax.optimization_barrier((values, flying))
    for flow, arrays in zip(flows, flying):
        flow.land(arrays)
    return values


def finish(flow):
    while flow.flying is not None:
        flow.land(flow.flying)
    return flow.result


def swap(value, offset):
    count = lax.axis_size("ctx") * lax.axis_size("fsdp")
    return lax.ppermute(value, AXES, [(i, i ^ offset) for i in range(count)])


def join(*parts):
    return jnp.concatenate(parts, axis=0)


def iter_once(arrays):
    return (yield arrays)


def gather_group(value):
    (other,) = yield [swap(value, 2)]
    pair = join(value, other)
    (other,) = yield [swap(pair, 1)]
    return pair, other


def scatter_group(keep, send):
    (other,) = yield [swap(send, 1)]
    half = keep.shape[0] // 2
    (far,) = yield [swap((keep[half:] + other[half:].astype(F32)).astype(BF), 2)]
    return keep[:half] + other[:half].astype(F32), far


def wide_offsets():
    highs = [8 * s for s in range(lax.axis_size("ctx") // 2)]
    chip = [low + high for low in (0, 4, 2, 6) for high in highs]
    return chip + [1 + o for o in chip]


def gather_wide(value):
    highs = lax.axis_size("ctx") // 2
    line = join(value, *(yield [swap(value, 8 * s) for s in range(1, highs)]))
    half = line.shape[0] // 2
    along_y, along_x = yield [swap(line, o) for o in (4, 2)]
    corner = yield [swap(along_y[:half], 2), swap(along_x[half:], 4)]
    chip = join(line, along_y, along_x, *corner)
    (other,) = yield [swap(chip, 1)]
    return chip, other


def scatter_wide(near, far):
    highs = lax.axis_size("ctx") // 2
    (other,) = yield [swap(far, 1)]
    chip = near.astype(F32) + other.astype(F32)
    line, along_y, along_x, corner = jnp.split(chip, 4, axis=0)
    mid = line.shape[0] // 2
    corner = corner.astype(BF)
    from_x, from_y = yield [swap(corner[:mid], 2), swap(corner[mid:], 4)]
    along_y = join(along_y[:mid] + from_x.astype(F32), along_y[mid:])
    along_x = join(along_x[:mid], along_x[mid:] + from_y.astype(F32))
    from_y, from_x = yield [swap(along_y.astype(BF), 4), swap(along_x.astype(BF), 2)]
    line = line + from_y.astype(F32) + from_x.astype(F32)
    rows = line.shape[0] // highs
    terms = yield [
        swap(line[s * rows : (s + 1) * rows].astype(BF), 8 * s) for s in range(1, highs)
    ]
    return [line[:rows], *terms]


def sum_over_ctx(value):
    count, me = lax.axis_size("ctx"), lax.axis_index("ctx")
    highs, low, high = count // 2, me % 2, me // 2
    half, step = value.shape[0] // 2, value.shape[0] // count
    (other,) = yield [swap(lax.dynamic_slice_in_dim(value, (1 - low) * half, half, 0).astype(BF), 4)]
    line = lax.dynamic_slice_in_dim(value, low * half, half, 0) + other.astype(F32)
    line_low = line.astype(BF)
    terms = yield [
        swap(lax.dynamic_slice_in_dim(line_low, (high ^ s) * step, step, 0), 8 * s)
        for s in range(1, highs)
    ]
    total = lax.dynamic_slice_in_dim(line, high * step, step, 0)
    total = (total + sum(term.astype(F32) for term in terms)).astype(BF)
    pieces = yield [swap(total, 8 * s) for s in range(1, highs)]
    line = line_low
    for s, piece in enumerate([total, *pieces]):
        line = lax.dynamic_update_slice_in_dim(line, piece, (high ^ s) * step, 0)
    (other,) = yield [swap(line, 4)]
    even, odd = jnp.where(low == 0, line, other), jnp.where(low == 0, other, line)
    return join(even, odd).astype(F32)


def gather_rows(value, me):
    pair, other = yield from gather_group(value)
    return settle(me ^ jnp.array([0, 2, 1, 3], jnp.int32), value.shape[0], pair, other)


def exchange_columns(quarters, arrived):
    first, second = yield [swap(quarters[0], 2), swap(quarters[1], 3)]
    (first_z,) = yield [swap(first, 8)]
    second_z, second_y = yield [swap(second, 8), swap(second, 4)]
    first_far, second_far = yield [swap(first_z, 4), swap(second_y, 8)]
    arrived += [first, first_z, first_far, second, second_y, second_z, second_far]
    return (yield [swap(first, 4)])


def kernel_call(kernel, out_shape, *operands, scalars=(), scratch=(), name):
    whole = pl.BlockSpec(memory_space=pltpu.VMEM)
    return pl.pallas_call(
        kernel,
        out_shape=[jax.ShapeDtypeStruct(shape, dtype) for shape, dtype in out_shape],
        in_specs=[pl.BlockSpec(memory_space=pltpu.SMEM)] * len(scalars) + [whole] * len(operands),
        out_specs=[whole] * len(out_shape),
        scratch_shapes=[pltpu.VMEM(shape, dtype) for shape, dtype in scratch],
        compiler_params=pltpu.CompilerParams(vmem_limit_bytes=VMEM_LIMIT),
        name=name,
    )(*scalars, *operands)


def pack_kernel(w_key, w_value, *refs):
    gains, out = refs[:-1], refs[-1]
    rows, width = w_key.shape[0], out.shape[1]
    out[:rows, : w_key.shape[1]] = w_key[...]
    out[:rows, w_key.shape[1] :] = w_value[...]
    lines = [
        jnp.concatenate([g[...].astype(F32), jnp.zeros((1, width - g.shape[1]), F32)], axis=1)
        for g in gains
    ]
    lines.append(jnp.zeros((out.shape[0] - rows - len(lines), width), F32))
    out[rows:, :] = jnp.concatenate(lines, axis=0).astype(BF)


def unpack_kernel(mine, pair, other, pair_mat, wide, narrow):
    size, head_part = wide.shape[1] // 4, narrow.shape[1] // 4
    block = pair.shape[0] // 2
    for m in range(4):

        @pl.when(mine[0] == m)
        def _(m=m):
            lines = []
            for r in range(4):
                source, first = (pair, other)[(m ^ r) % 2], (m ^ r) // 2 * block
                pair_mat[r * size : (r + 1) * size, :] = source[first : first + size, :]
                lines.append(source[first + size : first + block, :].astype(F32))
            for i in range(4):
                wide[i : i + 1, :] = jnp.concatenate([l[i : i + 1, :size] for l in lines], axis=1)
            for i in range(2):
                narrow[i : i + 1, :] = jnp.concatenate(
                    [l[4 + i : 5 + i, :head_part] for l in lines], axis=1
                )


def key_kernel(tokens, gain, key_gain, pair_mat, cosine, sine, first_low, key_raw, pairs):
    inputs = tokens[...].astype(F32)
    low = (inputs * root(inputs) * gain[0:1, :]).astype(BF)
    first_low[...] = low
    raw = contract(low, pair_mat[...], 1, 0)
    key = raw[:, :HD]
    key_raw[...] = key
    key = key * root(key) * key_gain[1:2, :]
    pairs[:, :HD] = rotate(key, cosine[...], sine[...]).astype(BF)
    pairs[:, HD:] = raw[:, HD:].astype(BF)


def query_kernel(first_low, query_gain, query_mat, cosine, sine, query_raw, queries):
    rows = first_low.shape[0]
    raw = contract(first_low[...], query_mat[...], 1, 0)
    query_raw[...] = raw
    for h in range(H):
        head = raw[:, h * HD : (h + 1) * HD]
        head = rotate(head * root(head) * query_gain[0:1, :], cosine[...], sine[...])
        queries[h * rows : (h + 1) * rows, :] = (head * HD ** (-0.5)).astype(BF)


def attend_kernel(blocks, q, q_place, q_start, k_near, v_near, k_far, v_far, near, far, heads, mass):
    step = pl.program_id(0)
    middle = pl.num_programs(0) // 2

    @pl.when(step == 0)
    def _():
        heads[...] = jnp.zeros_like(heads)
        mass[...] = jnp.zeros_like(mass)

    def section(k, v, probs):
        scores = contract(k[...], q[...], 1, 1)
        rows = k.shape[0]
        block = 64
        place, start = q_place[...], q_start[...]
        total = jnp.zeros_like(mass)
        for i in range(rows // block):
            first = blocks[step * (rows // block) + i] * block
            keys = first + lax.broadcasted_iota(jnp.int32, (block, scores.shape[1]), 0)
            allowed = (keys <= place) & (keys >= start)
            weights = jnp.where(allowed, jnp.exp(scores[i * block : (i + 1) * block]), 0.0)
            probs[i * block : (i + 1) * block, :] = weights.astype(BF)
            total = total + jnp.sum(weights, axis=0, keepdims=True)
        mass[...] += total
        heads[...] += contract(v[...], probs[...], 0, 0)

    @pl.when(step < middle)
    def _():
        section(k_near, v_near, near)

    @pl.when(step >= middle)
    def _():
        section(k_far, v_far, far)


def halves_of(shape, steps, column=0):
    half = steps // 2
    return [
        pl.BlockSpec(shape, lambda i, *s: (jnp.minimum(i, half - 1), column)),
        pl.BlockSpec(shape, lambda i, *s: (jnp.maximum(i - half, 0), column)),
    ]


def attend(blocks, queries, q_place, q_start, near, far):
    head_rows = queries.shape[0]
    keys = near.shape[0]
    steps = 2 * keys // KEY_BLOCK
    key_blocks, value_blocks = [halves_of((KEY_BLOCK, HD), steps, c) for c in (0, 1)]
    return pl.pallas_call(
        attend_kernel,
        grid_spec=pltpu.PrefetchScalarGridSpec(
            num_scalar_prefetch=1,
            grid=(steps,),
            in_specs=[
                pl.BlockSpec((head_rows, HD), lambda i, b: (0, 0)),
                pl.BlockSpec((1, head_rows), lambda i, b: (0, 0)),
                pl.BlockSpec((1, head_rows), lambda i, b: (0, 0)),
                key_blocks[0],
                value_blocks[0],
                key_blocks[1],
                value_blocks[1],
            ],
            out_specs=[
                *halves_of((KEY_BLOCK, head_rows), steps),
                pl.BlockSpec((HD, head_rows), lambda i, b: (0, 0)),
                pl.BlockSpec((1, head_rows), lambda i, b: (0, 0)),
            ],
        ),
        out_shape=[
            jax.ShapeDtypeStruct((keys, head_rows), BF),
            jax.ShapeDtypeStruct((keys, head_rows), BF),
            jax.ShapeDtypeStruct((HD, head_rows), F32),
            jax.ShapeDtypeStruct((1, head_rows), F32),
        ],
        compiler_params=pltpu.CompilerParams(vmem_limit_bytes=VMEM_LIMIT),
        cost_estimate=pl.CostEstimate(
            flops=8 * keys * head_rows * HD,
            bytes_accessed=2 * keys * (head_rows + 2 * HD) * 2,
            transcendentals=2 * keys * head_rows,
        ),
        name="attend",
    )(blocks, queries, q_place, q_start, near, near, far, far)


def turned_line(column):
    return jnp.broadcast_to(column, (column.shape[0], 128)).T[0:1, :]


def after_attend_kernel(weighted, mass, out_mat, tokens, gains, heads, heads_low, attn_raw, hidden, second_low):
    rows = tokens.shape[0]
    heads[...] = (weighted[...] * (1.0 / mass[...])).T
    for h in range(H):
        heads_low[:, h * HD : (h + 1) * HD] = heads[h * rows : (h + 1) * rows, :].astype(BF)
    raw = contract(heads_low[...], out_mat[...], 1, 0)
    attn_raw[...] = raw
    total = tokens[...].astype(F32) + raw * root(raw) * gains[1:2, :]
    hidden[...] = total
    second_low[...] = (total * root(total) * gains[2:3, :]).astype(BF)


def after_ffn_kernel(part, other, hidden, cotangent, gains, block_out, d_ffn_low, d_gain):
    raw = part[...] + other[...].astype(F32)
    block_out[...] = (hidden[...] + raw * root(raw) * gains[3:4, :]).astype(BF)
    d_ffn, d_gain[...] = rms_back(raw, gains[3:4, :], cotangent[...].astype(F32))
    d_ffn_low[...] = d_ffn.astype(BF)


def before_attend_back_kernel(
    part, other, hidden, cotangent, gains, attn_raw, out_mat, heads,
    d_hidden, d_attn_low, d_heads, dots, d_gain_ffn_in, d_gain_attn_out,
):
    rows = part.shape[0]
    d_second = part[...] + other[...].astype(F32)
    extra, d_gain_ffn_in[...] = rms_back(hidden[...], gains[2:3, :], d_second)
    total = cotangent[...].astype(F32) + extra
    d_hidden[...] = total
    d_attn, d_gain_attn_out[...] = rms_back(attn_raw[...], gains[1:2, :], total)
    low = d_attn.astype(BF)
    d_attn_low[...] = low
    for h in range(H):
        at = pl.ds(h * rows, rows)
        head = contract(low, out_mat[h * HD : (h + 1) * HD, :], 1, 1).astype(BF)
        d_heads[at, :] = head
        dots[:, at] = turned_line(
            jnp.sum(head.astype(F32) * heads[at, :], axis=1, keepdims=True)
        )


def attend_back_kernel(
    q, d_heads, mass, dots, near, far, k_near, v_near, k_far, v_far, d_queries, d_near, d_far
):
    step = pl.program_id(0)
    middle = pl.num_programs(0) // 2

    @pl.when(step == 0)
    def _():
        d_queries[...] = jnp.zeros_like(d_queries)

    def section(probs, k, v, out):
        d_probs = contract(v[...], d_heads[...], 1, 1)
        chance = probs[...].astype(F32) * (1.0 / mass[...])
        d_scores = (chance * (d_probs - dots[...])).astype(BF)
        out[:, :HD] = contract(d_scores, q[...], 1, 0).astype(BF)
        out[:, HD:] = contract(chance.astype(BF), d_heads[...], 1, 0).astype(BF)
        d_queries[...] += contract(k[...], d_scores, 0, 0)

    @pl.when(step < middle)
    def _():
        section(near, k_near, v_near, d_near)

    @pl.when(step >= middle)
    def _():
        section(far, k_far, v_far, d_far)


def attend_back(queries, d_heads, mass, dots, probs, pairs):
    head_rows = queries.shape[0]
    keys = pairs[0].shape[0]
    steps = 2 * keys // KEY_BLOCK
    whole = pl.BlockSpec((head_rows, HD), lambda i: (0, 0))
    line = pl.BlockSpec((1, head_rows), lambda i: (0, 0))
    key_blocks, value_blocks = [halves_of((KEY_BLOCK, HD), steps, c) for c in (0, 1)]
    return pl.pallas_call(
        attend_back_kernel,
        grid=(steps,),
        in_specs=[
            whole,
            whole,
            line,
            line,
            *halves_of((KEY_BLOCK, head_rows), steps),
            key_blocks[0],
            value_blocks[0],
            key_blocks[1],
            value_blocks[1],
        ],
        out_specs=[
            pl.BlockSpec((HD, head_rows), lambda i: (0, 0)),
            *halves_of((KEY_BLOCK, 2 * HD), steps),
        ],
        out_shape=[
            jax.ShapeDtypeStruct((HD, head_rows), F32),
            jax.ShapeDtypeStruct((keys, 2 * HD), BF),
            jax.ShapeDtypeStruct((keys, 2 * HD), BF),
        ],
        compiler_params=pltpu.CompilerParams(vmem_limit_bytes=VMEM_LIMIT),
        cost_estimate=pl.CostEstimate(
            flops=16 * keys * head_rows * HD,
            bytes_accessed=2 * keys * (head_rows + 4 * HD) * 2,
            transcendentals=0,
        ),
        name="attend_back",
    )(queries, d_heads, mass, dots, *probs, pairs[0], pairs[0], pairs[1], pairs[1])


def spread_rows(product, mine, size, keep, send, first):
    step = keep.shape[0] // 2
    width = product.shape[1]
    for offset in range(4):
        rows = product[pl.ds(pl.multiple_of((mine ^ offset) * size, 32), size), :]
        out = send if offset % 2 else keep
        begin = offset // 2 * step + first
        out[begin : begin + size, :width] = rows.astype(out.dtype)


def query_back_kernel(
    mine, d_queries, query_raw, gains, cosine, sine, query_mat, first_low, heads_low, d_attn_low,
    keep, send, d_first, d_gain, product, out_product, query_low,
):
    rows = first_low.shape[0]
    gain = gains[0:1, :]
    d_gain[...] = jnp.zeros_like(d_gain)
    for h in range(H):
        columns = pl.ds(h * HD, HD)
        head = d_queries[:, h * rows : (h + 1) * rows].T * HD ** (-0.5)
        head = rotate(head, cosine[...], -sine[...])
        d_raw, d_head_gain = rms_back(query_raw[:, columns], gain, head)
        d_gain[...] += d_head_gain
        query_low[:, columns] = d_raw.astype(BF)
    d_first[...] = contract(query_low[...], query_mat[...], 1, 1)
    model, inner = product.shape[0] // 4, out_product.shape[0] // 4
    keep[...] = jnp.zeros_like(keep)
    send[...] = jnp.zeros_like(send)
    product[...] = contract(first_low[...], query_low[...], 0, 0)
    spread_rows(product, mine[0], model, keep, send, 0)
    out_product[...] = contract(heads_low[...], d_attn_low[...], 0, 0)
    spread_rows(out_product, mine[0], inner, keep, send, model)


def key_back_kernel(
    mine, sums, *refs
):
    terms, refs = refs[:-19], refs[-19:]
    (
        key_raw, gains, head_gains, cosine, sine, pair_mat, first_low, d_first_query, tokens, d_hidden,
        d_gain_attn_out, d_gain_ffn_in, d_gain_ffn_out, d_gain_query,
        grad_tokens, keep, send, product, gain_lines,
    ) = refs
    total = sums[...]
    for term in terms:
        total = total + term[...].astype(F32)
    d_key = rotate(total[:, :HD], cosine[...], -sine[...])
    d_raw, d_gain_key = rms_back(key_raw[...], head_gains[1:2, :], d_key)
    low = jnp.concatenate([d_raw, total[:, HD:]], axis=1).astype(BF)
    d_first = d_first_query[...] + contract(low, pair_mat[...], 1, 1)
    extra, d_gain_attn_in = rms_back(tokens[...].astype(F32), gains[0:1, :], d_first)
    grad_tokens[...] = d_hidden[...] + extra
    product[:, : 2 * HD] = contract(first_low[...], low, 0, 0)
    gain_lines[...] = jnp.zeros_like(gain_lines)
    for i, line in enumerate(
        (d_gain_attn_in, d_gain_attn_out[...], d_gain_ffn_in[...], d_gain_ffn_out[...])
    ):
        gain_lines[i : i + 1, :] = line
    size, head_size = product.shape[0] // 4, HD // 4
    for i, line in enumerate((d_gain_query[...], d_gain_key)):
        pieces = []
        for r in range(4):
            pieces += [line[:, r * head_size : (r + 1) * head_size], jnp.zeros((1, size - head_size), F32)]
        gain_lines[4 + i : 5 + i, :] = jnp.concatenate(pieces, axis=1)
    product[:, 2 * HD :] = gain_lines[...].T
    keep[...] = jnp.zeros_like(keep)
    send[...] = jnp.zeros_like(send)
    spread_rows(product, mine[0], size, keep, send, 0)


def left_of(owner, part):
    return pl.multiple_of(owner * part - part % 128 * (owner % 2), 128)


def carve_kernel(part, mine, w, own, core):
    for offset, out in enumerate((own, core)):
        out[...] = w[:, :, pl.ds(left_of(mine[0] ^ offset, part), out.shape[2])]


def carve(w, mine, part, wide):
    rows, step = w.shape[1], 48
    return pl.pallas_call(
        functools.partial(carve_kernel, part),
        grid_spec=pltpu.PrefetchScalarGridSpec(
            num_scalar_prefetch=1,
            grid=(rows // step,),
            in_specs=[pl.BlockSpec((2, step, w.shape[2]), lambda i, p: (0, i, 0))],
            out_specs=[pl.BlockSpec((2, step, wide), lambda i, p: (0, i, 0))] * 2,
        ),
        out_shape=[jax.ShapeDtypeStruct((2, rows, wide), BF)] * 2,
        compiler_params=pltpu.CompilerParams(vmem_limit_bytes=VMEM_LIMIT),
        name="carve",
    )(mine[None], w)


def carve_quarters_kernel(part, place, w, near, corner):
    mine, side = place[0], place[2]
    for offset, out in ((2, near), (3, corner)):
        at = pl.ds(left_of(mine ^ offset, part), out.shape[2])
        for s in range(2):

            @pl.when(side == s)
            def _(s=s):
                out[0] = w[:, s, at]


def carve_quarters(w, place, part, wide):
    rows, step = w.shape[0], 48
    half = rows // 2 // step
    return pl.pallas_call(
        functools.partial(carve_quarters_kernel, part),
        grid_spec=pltpu.PrefetchScalarGridSpec(
            num_scalar_prefetch=1,
            grid=(half,),
            in_specs=[pl.BlockSpec((step, 2, w.shape[2]), lambda i, p: (i + half * p[1], 0, 0))],
            out_specs=[pl.BlockSpec((1, step, wide), lambda i, p: (0, i, 0))] * 2,
        ),
        out_shape=[jax.ShapeDtypeStruct((1, rows // 2, wide), BF)] * 2,
        compiler_params=pltpu.CompilerParams(vmem_limit_bytes=VMEM_ALL),
        name="carve_quarters",
    )(place, w)


def walk(shape, first, count, scalars, dim=0):
    def place(i, *unused):
        return tuple(jnp.clip(i - first, 0, count - 1) if d == dim else 0 for d in range(len(shape)))

    return pl.BlockSpec(shape, place)


def settle_kernel(counts, places, *refs):
    out, sources = refs[-1], refs[:-1]
    step, first = pl.program_id(0), 0
    for source, count in zip(sources, counts):

        @pl.when((step >= first) & (step < first + count))
        def _(source=source):
            out[...] = source[...]

        first += count


def settle(places, rows, *sources):
    counts = [source.shape[0] // rows for source in sources]
    width = sources[0].shape[1]
    starts = [sum(counts[:i]) for i in range(len(counts))]
    return pl.pallas_call(
        functools.partial(settle_kernel, counts),
        grid_spec=pltpu.PrefetchScalarGridSpec(
            num_scalar_prefetch=1,
            grid=(sum(counts),),
            in_specs=[walk((rows, width), f, c, 1) for f, c in zip(starts, counts)],
            out_specs=pl.BlockSpec((rows, width), lambda i, p: (p[i], 0)),
        ),
        out_shape=jax.ShapeDtypeStruct((sum(counts) * rows, width), sources[0].dtype),
        compiler_params=pltpu.CompilerParams(vmem_limit_bytes=VMEM_LIMIT),
        name="settle",
    )(places, *sources)


def lay_kernel(counts, sides, rows, *refs):
    out, sources = refs[-1], refs[: len(counts)]
    step, first = pl.program_id(0), 0
    width = out.shape[3]
    for source, count in zip(sources, counts):

        @pl.when((step >= first) & (step < first + count))
        def _(source=source):
            for block in range(out.shape[1]):
                out[0, block] = source[0, :, block * width : (block + 1) * width]

        first += count


def lay(places, sources, laid=None):
    half, wide = sources[-1].shape[1], sources[-1].shape[2]
    counts = [source.shape[0] * source.shape[1] // half for source in sources]

    def run(first, count):
        def place(i, s, r):
            j = jnp.clip(i - first, 0, count - 1)
            return (j // 2, j % 2, 0)

        return pl.BlockSpec((1, half, wide), place)

    base = [] if laid is None else [laid]
    sides, rows = [jnp.stack([jnp.asarray(p[i], jnp.int32) for p in places]) for i in (0, 1)]
    return pl.pallas_call(
        functools.partial(lay_kernel, counts),
        grid_spec=pltpu.PrefetchScalarGridSpec(
            num_scalar_prefetch=2,
            grid=(sum(counts),),
            in_specs=[run(sum(counts[:i]), count) for i, count in enumerate(counts)]
            + [pl.BlockSpec(memory_space=pl.ANY)] * len(base),
            out_specs=pl.BlockSpec(
                (1, wide // 256, half, 256), lambda i, s, r: (s[i], 0, r[i], 0)
            ),
        ),
        out_shape=jax.ShapeDtypeStruct((2, wide // 256, 8 * half, 256), BF),
        input_output_aliases={2 + len(sources): 0} if base else {},
        compiler_params=pltpu.CompilerParams(vmem_limit_bytes=VMEM_ALL),
        name="lay",
    )(sides, rows, *sources, *base)


def contract(left, right, left_dim, right_dim):
    return lax.dot_general(
        left, right, (((left_dim,), (right_dim,)), ((), ())), preferred_element_type=F32
    )


def gelu_and_slope(x):
    scale = math.sqrt(2.0 / math.pi)
    cubic = (scale * 0.044715) * (x * x * x)
    inner = scale * x + cubic
    share = 0.5 + 0.5 * jnp.tanh(inner)
    return x * share, share + share * (1.0 - share) * (2.0 * inner + 4.0 * cubic)


def ffn_gradients_kernel(part, first, blocks, mine, second, d_ffn, w_gate, w_up, w_down, *rest):
    outs, down_rows, act, d_both, both_sum, down_sum, sem = rest[-10:-6], *rest[-6:]
    step = pl.program_id(1)
    rows, slab = second.shape[0], 256
    width = act.shape[1]

    def products(r):
        at = pl.ds(r * slab, slab)
        return (
            contract(second[at, :], w_gate[0, 0], 1, 0),
            contract(second[at, :], w_up[0, 0], 1, 0),
            contract(d_ffn[at, :], w_down[...], 1, 1),
        )

    ahead = products(0)
    for r in range(rows // slab):
        at = pl.ds(r * slab, slab)
        gate, upper, d_act = ahead
        if r + 1 < rows // slab:
            ahead = products(r + 1)
        value, slope = gelu_and_slope(gate)
        act[at, :] = (value * upper).astype(BF)
        d_both[at, :width] = (d_act * upper * slope).astype(BF)
        d_both[at, width:] = (d_act * value).astype(BF)
    grad_both = contract(second[...], d_both[...], 0, 0)
    grad_down = contract(act[...], d_ffn[...], 0, 0)

    @pl.when(step == 0)
    def _():
        both_sum[...] = grad_both
        down_sum[...] = grad_down

    @pl.when(step > 0)
    def _():
        both_sum[...] += grad_both
        down_sum[...] += grad_down

    @pl.when(step == pl.num_programs(1) - 1)
    def _():
        block = first + pl.program_id(0)
        odd = mine[0] % 2
        extra = blocks * width - part
        begins = (block == 0) & (odd == 1)
        ends = (block == blocks - 1) & (odd == 0)

        def put(source, at, size):
            copy = pltpu.make_async_copy(
                down_sum.at[pl.ds(source, size), :], down_rows.at[pl.ds(at, size), :], sem
            )
            copy.start()
            copy.wait()

        @pl.when(begins)
        def _():
            put(extra, 0, width - extra)

        @pl.when(ends)
        def _():
            put(0, (blocks - 1) * width, width - extra)

        @pl.when(jnp.logical_not(begins | ends))
        def _():
            put(0, pl.multiple_of(block * width - odd * extra, 64), width)

        quarter = second.shape[1] // 4
        for offset, out in enumerate(outs):
            at = pl.ds(pl.multiple_of((mine[0] ^ offset) * quarter, 32), quarter)
            out[0] = both_sum[at, :width].astype(BF)
            out[1] = both_sum[at, width:].astype(BF)


def ffn_gradients(mine, second_all, d_ffn_all, in_mat, down_mat, part, first, last, down_rows):
    tokens, model = second_all.shape
    slab, width = min(2048, tokens), 256
    columns = (last - first) * width
    tall = pl.BlockSpec((slab, model), lambda j, t, m: (t, 0))
    anywhere = pl.BlockSpec(memory_space=pl.ANY)
    earlier = [] if down_rows is None else [down_rows]
    return pl.pallas_call(
        functools.partial(ffn_gradients_kernel, part, first, down_mat.shape[0] // width),
        grid_spec=pltpu.PrefetchScalarGridSpec(
            num_scalar_prefetch=1,
            grid=(last - first, tokens // slab),
            in_specs=[
                tall,
                tall,
                pl.BlockSpec((1, 1, model, width), lambda j, t, m: (0, j + first, 0, 0)),
                pl.BlockSpec((1, 1, model, width), lambda j, t, m: (1, j + first, 0, 0)),
                pl.BlockSpec((width, model), lambda j, t, m: (j + first, 0)),
            ]
            + [anywhere] * len(earlier),
            out_specs=[pl.BlockSpec((2, model // 4, width), lambda j, t, m: (0, 0, j))] * 4
            + [anywhere],
            scratch_shapes=[
                pltpu.VMEM((slab, width), BF),
                pltpu.VMEM((slab, 2 * width), BF),
                pltpu.VMEM((model, 2 * width), F32),
                pltpu.VMEM((width, model), F32),
                pltpu.SemaphoreType.DMA,
            ],
        ),
        out_shape=[jax.ShapeDtypeStruct((2, model // 4, columns), BF)] * 4
        + [jax.ShapeDtypeStruct((part, model), F32)],
        input_output_aliases={6: 4} if earlier else {},
        compiler_params=pltpu.CompilerParams(vmem_limit_bytes=VMEM_ALL),
        cost_estimate=pl.CostEstimate(
            flops=12 * tokens * model * columns,
            bytes_accessed=4 * tokens * model * (last - first),
            transcendentals=tokens * columns,
        ),
        name="ffn_gradients",
    )(mine[None], second_all, d_ffn_all, in_mat, in_mat, down_mat, *earlier)


def ffn_forward_kernel(near, far, w_gate, w_up, w_down, gate, up, keep, send, act, total):
    step, half = pl.program_id(0), near.shape[0]

    @pl.when(step == 0)
    def _():
        total[...] = jnp.zeros_like(total)

    def products(rows):
        return contract(rows[...], w_gate[0, 0], 1, 0), contract(rows[...], w_up[0, 0], 1, 0)

    ahead = products(near)
    for i in range(2):
        at = pl.ds(i * half, half)
        left, right = ahead
        if i == 0:
            ahead = products(far)
        gate[at, :], up[at, :] = left, right
        act[at, :] = (gelu_and_slope(left)[0] * right).astype(BF)
    total[...] += contract(act[...], w_down[...], 1, 0)

    @pl.when(step == pl.num_programs(0) - 1)
    def _():
        keep[...], send[...] = total[:half, :], total[half:, :].astype(BF)


def ffn_backward_kernel(near, far, gate, up, w_gate, w_up, w_down, keep, send, d_gate, d_up, total):
    step, half = pl.program_id(0), near.shape[0]

    @pl.when(step == 0)
    def _():
        total[...] = jnp.zeros_like(total)

    ahead = contract(near[...], w_down[...], 1, 1)
    for i in range(2):
        at = pl.ds(i * half, half)
        d_act = ahead
        if i == 0:
            ahead = contract(far[...], w_down[...], 1, 1)
        value, slope = gelu_and_slope(gate[at, :])
        d_gate[at, :] = (d_act * up[at, :] * slope).astype(BF)
        d_up[at, :] = (d_act * value).astype(BF)
    total[...] += contract(d_gate[...], w_gate[0, 0], 1, 1) + contract(d_up[...], w_up[0, 0], 1, 1)

    @pl.when(step == pl.num_programs(0) - 1)
    def _():
        keep[...], send[...] = total[:half, :], total[half:, :].astype(BF)


def ffn_group(kernel, near, far, in_mat, down_mat, *kept):
    half, model = near.shape
    wide, width = down_mat.shape[0], 256
    rows = pl.BlockSpec((half, model), lambda j: (0, 0))
    column = pl.BlockSpec((2 * half, width), lambda j: (0, j))
    forward = not kept
    shape = jax.ShapeDtypeStruct((2 * half, wide), F32)
    return pl.pallas_call(
        kernel,
        grid=(wide // width,),
        in_specs=[rows, rows]
        + [column] * len(kept)
        + [
            pl.BlockSpec((1, 1, model, width), lambda j: (0, j, 0, 0)),
            pl.BlockSpec((1, 1, model, width), lambda j: (1, j, 0, 0)),
            pl.BlockSpec((width, model), lambda j: (j, 0)),
        ],
        out_specs=[column] * (2 * forward) + [rows, rows],
        out_shape=[shape] * (2 * forward)
        + [jax.ShapeDtypeStruct((half, model), F32), jax.ShapeDtypeStruct((half, model), BF)],
        scratch_shapes=[pltpu.VMEM((2 * half, width), BF)] * (1 if forward else 2)
        + [pltpu.VMEM((2 * half, model), F32)],
        compiler_params=pltpu.CompilerParams(vmem_limit_bytes=VMEM_ALL),
        cost_estimate=pl.CostEstimate(
            flops=12 * half * model * wide,
            bytes_accessed=6 * model * wide + 16 * half * wide,
            transcendentals=2 * half * wide,
        ),
        name="ffn_forward" if forward else "ffn_backward",
    )(near, far, *kept, in_mat, in_mat, down_mat)


def unfold_kernel(part, mine, *refs):
    out, sources = refs[-1], refs[:-1]
    ranges = len(sources) // 4
    extra = part % 128
    for m in range(4):

        @pl.when(mine[0] == m)
        def _(m=m):
            for side in range(2):
                rows = [
                    jnp.concatenate(
                        [sources[r * 4 + (m ^ owner)][side] for r in range(ranges)], axis=1
                    ).astype(F32)
                    for owner in range(4)
                ]
                wide = rows[0].shape[1]
                cut = wide - 128
                left = lax.broadcasted_iota(jnp.int32, (rows[0].shape[0], 128), 1) < extra
                pieces = []
                for even, odd in (rows[:2], rows[2:]):
                    shared = jnp.where(left, even[:, cut:], odd[:, :128])
                    pieces += [even[:, :cut], shared, odd[:, 128:]]
                out[:, side, :] = jnp.concatenate(pieces, axis=1)


def unfold(mine, part, ranges):
    sources = [piece for pieces in ranges for piece in pieces]
    rows, step = sources[0].shape[1], 16
    return pl.pallas_call(
        functools.partial(unfold_kernel, part),
        grid_spec=pltpu.PrefetchScalarGridSpec(
            num_scalar_prefetch=1,
            grid=(rows // step,),
            in_specs=[
                pl.BlockSpec((2, step, s.shape[2]), lambda i, m: (0, i, 0)) for s in sources
            ],
            out_specs=pl.BlockSpec((step, 2, 4 * part), lambda i, m: (i, 0, 0)),
        ),
        out_shape=jax.ShapeDtypeStruct((rows, 2, 4 * part), F32),
        compiler_params=pltpu.CompilerParams(vmem_limit_bytes=VMEM_LIMIT),
        name="unfold",
    )(mine[None], *sources)


def pick(table, index):
    hit = index[:, None] == jnp.arange(table.shape[0], dtype=jnp.int32)[None, :]
    return jnp.sum(jnp.where(hit, table[None, :], 0), axis=1)


def body(
    tokens,
    cotangent,
    block_table,
    sequence_ids,
    w_query,
    w_key,
    w_value,
    w_out,
    w_in,
    w_down,
    gain_attn_in,
    gain_attn_out,
    gain_ffn_in,
    gain_ffn_out,
    gain_query,
    gain_key,
):
    rows = tokens.shape[0]
    block = rows // 2
    model, part = w_in.shape[0] * 4, w_down.shape[0]
    mine = lax.axis_index("fsdp")
    me = lax.axis_index("ctx") * 4 + mine

    gains = (gain_attn_in, gain_attn_out, gain_ffn_in, gain_ffn_out, gain_query, gain_key)
    sizes = [g.shape[0] for g in gains]
    (packed,) = kernel_call(
        pack_kernel,
        [((w_key.shape[0] + 16, 2 * HD), BF)],
        w_key,
        w_value,
        *[g[None] for g in gains],
        name="pack",
    )
    packed_flow = Flow(gather_group(packed))

    wide = -(-part // 256) * 256
    quarter = model // 4
    boundary = jnp.sum((sequence_ids == 0).astype(jnp.int32))
    everyone = me ^ jnp.array(wide_offsets(), jnp.int32)
    blocks = pick(block_table, jnp.stack([2 * everyone, 2 * everyone + 1], axis=1).reshape(-1))
    place = (blocks[:2, None] * block + jnp.arange(block, dtype=jnp.int32)[None, :]).reshape(-1)
    start = jnp.where(place >= boundary, boundary, 0)
    position = place - start
    inverse_angle = 1000000.0 ** (-jnp.arange(HD // 2, dtype=F32) / (HD // 2))
    angles = position.astype(F32)[:, None] * inverse_angle[None, :]
    cosine, sine = jnp.cos(angles), jnp.sin(angles)
    q_place, q_start = jnp.tile(place, H)[None], jnp.tile(start, H)[None]

    low_bit, high_bit = lax.axis_index("ctx") % 2, lax.axis_index("ctx") // 2 % 2
    quarters = carve_quarters(w_in, jnp.stack([mine, low_bit, high_bit]), part, wide)
    quarters = pace(quarters, packed_flow)
    arrived = []
    columns_flow = Flow(exchange_columns(quarters, arrived))
    cosine, sine, q_place, q_start = pace((cosine, sine, q_place, q_start), packed_flow)
    pair_mat, model_gains, head_gains = kernel_call(
        unpack_kernel,
        [((model, 2 * HD), BF), ((8, model), F32), ((8, HD), F32)],
        *packed_flow.result,
        scalars=(mine[None],),
        name="unpack",
    )
    first_low, key_raw, pair_rows = kernel_call(
        key_kernel,
        [((rows, model), BF), ((rows, HD), F32), ((rows, 2 * HD), BF)],
        tokens,
        model_gains,
        head_gains,
        pair_mat,
        cosine,
        sine,
        name="keys",
    )
    pairs_flow = Flow(gather_wide(pair_rows))
    own, to_core = carve(jnp.swapaxes(w_in, 0, 1), mine, part, wide)
    own, to_core, w_query = pace((own, to_core, w_query), pairs_flow, columns_flow)
    core_flow = Flow(iter_once([swap(to_core, 1)]))
    query_flow = Flow(gather_rows(w_query, mine))
    w_out, w_down = pace((w_out, w_down), pairs_flow, columns_flow, core_flow)
    w_out, w_down = pace((w_out, w_down), pairs_flow, columns_flow, query_flow)
    out_flow = Flow(gather_rows(w_out, mine))
    pairs = finish(pairs_flow)
    query_mat = finish(query_flow)
    query_raw, queries = kernel_call(
        query_kernel,
        [((rows, H * HD), F32), ((H * rows, HD), BF)],
        first_low,
        head_gains,
        query_mat,
        cosine,
        sine,
        name="queries",
    )
    down_mat = lax.dynamic_update_slice_in_dim(
        jnp.zeros((wide, model), BF), w_down, part % 128 * (mine % 2), 0
    )
    *probs, weighted, mass = attend(blocks, queries, q_place, q_start, *pairs)
    weighted, mass = pace((weighted, mass), out_flow, columns_flow)
    out_mat = finish(out_flow)
    heads, heads_low, attn_raw, hidden, second_low = kernel_call(
        after_attend_kernel,
        [
            ((H * rows, HD), F32),
            ((rows, H * HD), BF),
            ((rows, model), F32),
            ((rows, model), F32),
            ((rows, model), BF),
        ],
        weighted,
        mass,
        out_mat,
        tokens,
        model_gains,
        name="after_attend",
    )

    group_flow = Flow(gather_group(second_low))
    second_all = lax.all_gather(second_low, AXES, axis=0, tiled=True)
    places = [
        (side, (mine ^ offset) * 2 + bit) for offset in (0, 1) for side in (0, 1) for bit in (0, 1)
    ]
    for offset in (2, 3):
        places += [
            (side, (mine ^ offset) * 2 + bit)
            for side in (high_bit, 1 - high_bit)
            for bit in (low_bit, 1 - low_bit)
        ]
    laid = lay(places[:9] + places[10:], (own, *core_flow.result, *arrived))
    (laid,) = pace((laid,), group_flow, columns_flow)
    in_mat = lay(places[9:10], columns_flow.result, laid)
    gate, upper, keep, send = ffn_group(ffn_forward_kernel, *finish(group_flow), in_mat, down_mat)
    block_out, d_ffn_low, d_gain_ffn_out = kernel_call(
        after_ffn_kernel,
        [((rows, model), BF), ((rows, model), BF), ((1, model), F32)],
        *finish(Flow(scatter_group(keep, send))),
        hidden,
        cotangent,
        model_gains,
        name="after_ffn",
    )
    group_flow = Flow(gather_group(d_ffn_low))
    d_ffn_all = lax.all_gather(d_ffn_low, AXES, axis=0, tiled=True)
    keep, send = ffn_group(
        ffn_backward_kernel, *finish(group_flow), in_mat, down_mat, gate, upper
    )
    d_hidden, d_attn_low, d_heads, dots, d_gain_ffn_in, d_gain_attn_out = kernel_call(
        before_attend_back_kernel,
        [
            ((rows, model), F32),
            ((rows, model), BF),
            ((H * rows, HD), BF),
            ((1, H * rows), F32),
            ((1, model), F32),
            ((1, model), F32),
        ],
        *finish(Flow(scatter_group(keep, send))),
        hidden,
        cotangent,
        model_gains,
        attn_raw,
        out_mat,
        heads,
        name="before_attend_back",
    )

    d_queries, *d_pairs = attend_back(queries, d_heads, mass, dots, probs, pairs)
    sums_flow = Flow(scatter_wide(*d_pairs))
    early_rows = quarter + H * HD // 4
    keep, send, d_first_query, d_gain_query = kernel_call(
        query_back_kernel,
        [
            ((2 * early_rows, model), F32),
            ((2 * early_rows, model), BF),
            ((rows, model), F32),
            ((1, HD), F32),
        ],
        d_queries,
        query_raw,
        head_gains,
        cosine,
        sine,
        query_mat,
        first_low,
        heads_low,
        d_attn_low,
        scalars=(mine[None],),
        scratch=[((model, H * HD), F32), ((H * HD, model), F32), ((rows, H * HD), BF)],
        name="query_back",
    )
    keep, send, d_first_query = pace((keep, send, d_first_query), sums_flow)
    pace((), sums_flow)
    pace((), sums_flow)
    early_flow = Flow(scatter_group(keep, send))
    pace((), sums_flow, early_flow)
    grad_tokens, keep, send = kernel_call(
        key_back_kernel,
        [
            ((rows, model), F32),
            ((2 * quarter, 2 * HD + 128), F32),
            ((2 * quarter, 2 * HD + 128), BF),
        ],
        *sums_flow.result,
        key_raw,
        model_gains,
        head_gains,
        cosine,
        sine,
        pair_mat,
        first_low,
        d_first_query,
        tokens,
        d_hidden,
        d_gain_attn_out,
        d_gain_ffn_in,
        d_gain_ffn_out,
        d_gain_query,
        scalars=(mine[None],),
        scratch=[((model, 2 * HD + 128), F32), ((128, model), F32)],
        name="key_back",
    )
    tail_flow = Flow(scatter_group(keep, send))

    count = wide // 256
    unit = count // 7
    cuts = [0, 2 * unit, 4 * unit, 5 * unit, 6 * unit, count]
    ranges, grad_down = [], None
    both = (second_all, d_ffn_all)

    def columns_step(*flows):
        nonlocal both, grad_down
        i = len(ranges)
        *pieces, grad_down = ffn_gradients(
            mine, *both, in_mat, down_mat, part, cuts[i], cuts[i + 1], grad_down
        )
        over_x = [sent[2:] for sent in ranges]
        both, grad_down, over_x = pace((both, grad_down, over_x), *flows)
        for sent, arrays in zip(ranges, over_x):
            sent[2:] = arrays
        ranges.append([pieces[0]] + [swap(pieces[o], o) for o in (1, 2, 3)])

    def total(flow):
        near, far = flow.result
        return near + far.astype(F32)

    pace((), tail_flow)
    columns_step(tail_flow, early_flow)
    early, tail = total(early_flow), total(tail_flow)
    tail = jnp.pad(tail, ((0, 0), (0, model - tail.shape[1])))
    spare = -(early.shape[0] + tail.shape[0]) % 128
    rest_flow = Flow(sum_over_ctx(join(early, tail, jnp.zeros((spare, model), F32))))
    for _ in range(4):
        columns_step(rest_flow)
    early, tail = rest_flow.result[:early_rows], rest_flow.result[early_rows:]
    grad_query = early[:quarter, : H * HD]
    grad_out = early[quarter:]
    grad_key, grad_value = tail[:quarter, :HD], tail[:quarter, HD : 2 * HD]
    gain_grads = [tail[:size, 2 * HD + i] for i, size in enumerate(sizes)]
    grad_in = unfold(mine, part, ranges)

    return (
        block_out,
        grad_tokens,
        grad_query,
        grad_key,
        grad_value,
        grad_out,
        grad_in,
        grad_down,
        *gain_grads,
    )


def solution(mesh):
    in_specs = (
        P(AXES, None),
        P(AXES, None),
        P(),
        P(),
        P("fsdp", None),
        P("fsdp", None),
        P("fsdp", None),
        P("fsdp", None),
        P("fsdp", None, None),
        P("fsdp", None),
        P("fsdp"),
        P("fsdp"),
        P("fsdp"),
        P("fsdp"),
        P("fsdp"),
        P("fsdp"),
    )
    out_specs = (
        P(AXES, None),
        P(AXES, None),
        P("fsdp", None),
        P("fsdp", None),
        P("fsdp", None),
        P("fsdp", None),
        P("fsdp", None, None),
        P("fsdp", None),
        P("fsdp"),
        P("fsdp"),
        P("fsdp"),
        P("fsdp"),
        P("fsdp"),
        P("fsdp"),
    )
    return jax.shard_map(body, mesh=mesh, in_specs=in_specs, out_specs=out_specs, check_vma=False)
```

```python
import functools
import math

import jax
import jax.numpy as jnp
from jax import lax
from jax.experimental import pallas as pl
from jax.experimental.pallas import tpu as pltpu
from jax.sharding import PartitionSpec as P

H = 4
HD = 256
EPS = 1e-06
AXES = ("ctx", "fsdp")
BF = jnp.bfloat16
F32 = jnp.float32
KEY_BLOCK = 512
VMEM_LIMIT = 32 * 2**20
VMEM_ALL = 60 * 2**20


def root(values):
    return lax.rsqrt(jnp.mean(values * values, axis=-1, keepdims=True) + EPS)


def rms_back(values, gain, grad):
    scale = root(values)
    scaled = gain * grad
    mean = jnp.mean(values * scaled, axis=-1, keepdims=True)
    return (
        scale * scaled - values * (scale * scale * scale * mean),
        jnp.sum(grad * values * scale, axis=0, keepdims=True),
    )


def rotate(values, cosine, sine):
    half = values.shape[-1] // 2
    first, second = values[:, :half], values[:, half:]
    return jnp.concatenate(
        [first * cosine - second * sine, second * cosine + first * sine], axis=1
    )


class Flow:
    def __init__(self, steps):
        self.steps = steps
        self.result = None
        self.flying = next(steps)

    def land(self, arrays):
        try:
            self.flying = self.steps.send(arrays)
        except StopIteration as stop:
            self.flying, self.result = None, stop.value


def pace(values, *flows):
    flying = [flow.flying for flow in flows]
    values, flying = lax.optimization_barrier((values, flying))
    for flow, arrays in zip(flows, flying):
        flow.land(arrays)
    return values


def finish(flow):
    while flow.flying is not None:
        flow.land(flow.flying)
    return flow.result


def swap(value, offset):
    count = lax.axis_size("ctx") * lax.axis_size("fsdp")
    return lax.ppermute(value, AXES, [(i, i ^ offset) for i in range(count)])


def join(*parts):
    return jnp.concatenate(parts, axis=0)


def iter_once(arrays):
    return (yield arrays)


def gather_group(value):
    (other,) = yield [swap(value, 2)]
    pair = join(value, other)
    (other,) = yield [swap(pair, 1)]
    return pair, other


def scatter_group(keep, send):
    (other,) = yield [swap(send, 1)]
    half = keep.shape[0] // 2
    (far,) = yield [swap((keep[half:] + other[half:].astype(F32)).astype(BF), 2)]
    return keep[:half] + other[:half].astype(F32), far


def wide_offsets():
    highs = [8 * s for s in range(lax.axis_size("ctx") // 2)]
    chip = [low + high for low in (0, 4, 2, 6) for high in highs]
    return chip + [1 + o for o in chip]


def gather_wide(value):
    highs = lax.axis_size("ctx") // 2
    line = join(value, *(yield [swap(value, 8 * s) for s in range(1, highs)]))
    half = line.shape[0] // 2
    along_y, along_x = yield [swap(line, o) for o in (4, 2)]
    corner = yield [swap(along_y[:half], 2), swap(along_x[half:], 4)]
    chip = join(line, along_y, along_x, *corner)
    (other,) = yield [swap(chip, 1)]
    return chip, other


def scatter_wide(near, far):
    highs = lax.axis_size("ctx") // 2
    (other,) = yield [swap(far, 1)]
    chip = near.astype(F32) + other.astype(F32)
    line, along_y, along_x, corner = jnp.split(chip, 4, axis=0)
    mid = line.shape[0] // 2
    corner = corner.astype(BF)
    from_x, from_y = yield [swap(corner[:mid], 2), swap(corner[mid:], 4)]
    along_y = join(along_y[:mid] + from_x.astype(F32), along_y[mid:])
    along_x = join(along_x[:mid], along_x[mid:] + from_y.astype(F32))
    from_y, from_x = yield [swap(along_y.astype(BF), 4), swap(along_x.astype(BF), 2)]
    line = line + from_y.astype(F32) + from_x.astype(F32)
    rows = line.shape[0] // highs
    terms = yield [
        swap(line[s * rows : (s + 1) * rows].astype(BF), 8 * s) for s in range(1, highs)
    ]
    return [line[:rows], *terms]


def gather_rows(value, me):
    pair, other = yield from gather_group(value)
    return settle(me ^ jnp.array([0, 2, 1, 3], jnp.int32), value.shape[0], pair, other)


def exchange_columns(quarters, arrived):
    first, second = yield [swap(quarters[0], 2), swap(quarters[1], 3)]
    (first_z,) = yield [swap(first, 8)]
    second_z, second_y = yield [swap(second, 8), swap(second, 4)]
    first_far, second_far = yield [swap(first_z, 4), swap(second_y, 8)]
    arrived += [first, first_z, first_far, second, second_y, second_z, second_far]
    return (yield [swap(first, 4)])


def exchange_results(pieces, down):
    others = yield [swap(pieces[o], o) for o in (1, 2, 3)]
    mixed = join(*[piece.reshape(-1, piece.shape[2]) for piece in (pieces[0], *others)])
    width = mixed.shape[1] // 2
    first, second = [
        jnp.concatenate([mixed[:, at], down[:, at].reshape(-1, down.shape[2])], axis=1)
        for at in (slice(0, width), slice(width, 2 * width))
    ]
    first_y, second_z = yield [swap(first, 4), swap(second, 8)]
    return [first, first_y, second, second_z]


def kernel_call(kernel, out_shape, *operands, scalars=(), scratch=(), name):
    whole = pl.BlockSpec(memory_space=pltpu.VMEM)
    return pl.pallas_call(
        kernel,
        out_shape=[jax.ShapeDtypeStruct(shape, dtype) for shape, dtype in out_shape],
        in_specs=[pl.BlockSpec(memory_space=pltpu.SMEM)] * len(scalars) + [whole] * len(operands),
        out_specs=[whole] * len(out_shape),
        scratch_shapes=[pltpu.VMEM(shape, dtype) for shape, dtype in scratch],
        compiler_params=pltpu.CompilerParams(vmem_limit_bytes=VMEM_LIMIT),
        name=name,
    )(*scalars, *operands)


def pack_kernel(w_key, w_value, *refs):
    gains, out = refs[:-1], refs[-1]
    rows, width = w_key.shape[0], out.shape[1]
    out[:rows, : w_key.shape[1]] = w_key[...]
    out[:rows, w_key.shape[1] :] = w_value[...]
    lines = [
        jnp.concatenate([g[...].astype(F32), jnp.zeros((1, width - g.shape[1]), F32)], axis=1)
        for g in gains
    ]
    lines.append(jnp.zeros((out.shape[0] - rows - len(lines), width), F32))
    out[rows:, :] = jnp.concatenate(lines, axis=0).astype(BF)


def unpack_kernel(mine, pair, other, pair_mat, wide, narrow):
    size, head_part = wide.shape[1] // 4, narrow.shape[1] // 4
    block = pair.shape[0] // 2
    for m in range(4):

        @pl.when(mine[0] == m)
        def _(m=m):
            lines = []
            for r in range(4):
                source, first = (pair, other)[(m ^ r) % 2], (m ^ r) // 2 * block
                pair_mat[r * size : (r + 1) * size, :] = source[first : first + size, :]
                lines.append(source[first + size : first + block, :].astype(F32))
            for i in range(4):
                wide[i : i + 1, :] = jnp.concatenate([l[i : i + 1, :size] for l in lines], axis=1)
            for i in range(2):
                narrow[i : i + 1, :] = jnp.concatenate(
                    [l[4 + i : 5 + i, :head_part] for l in lines], axis=1
                )


def key_kernel(tokens, gain, key_gain, pair_mat, cosine, sine, first_low, key_raw, pairs):
    inputs = tokens[...].astype(F32)
    low = (inputs * root(inputs) * gain[0:1, :]).astype(BF)
    first_low[...] = low
    raw = contract(low, pair_mat[...], 1, 0)
    key = raw[:, :HD]
    key_raw[...] = key
    key = key * root(key) * key_gain[1:2, :]
    pairs[:, :HD] = rotate(key, cosine[...], sine[...]).astype(BF)
    pairs[:, HD:] = raw[:, HD:].astype(BF)


def query_kernel(first_low, query_gain, query_mat, cosine, sine, query_raw, queries):
    rows = first_low.shape[0]
    raw = contract(first_low[...], query_mat[...], 1, 0)
    query_raw[...] = raw
    for h in range(H):
        head = raw[:, h * HD : (h + 1) * HD]
        head = rotate(head * root(head) * query_gain[0:1, :], cosine[...], sine[...])
        queries[h * rows : (h + 1) * rows, :] = (head * HD ** (-0.5)).astype(BF)


def attend_kernel(blocks, q, q_place, q_start, k_near, v_near, k_far, v_far, near, far, heads, mass):
    step = pl.program_id(0)
    middle = pl.num_programs(0) // 2

    @pl.when(step == 0)
    def _():
        heads[...] = jnp.zeros_like(heads)
        mass[...] = jnp.zeros_like(mass)

    def section(k, v, probs):
        scores = contract(k[...], q[...], 1, 1)
        rows = k.shape[0]
        block = 64
        place, start = q_place[...], q_start[...]
        total = jnp.zeros_like(mass)
        for i in range(rows // block):
            first = blocks[step * (rows // block) + i] * block
            keys = first + lax.broadcasted_iota(jnp.int32, (block, scores.shape[1]), 0)
            allowed = (keys <= place) & (keys >= start)
            weights = jnp.where(allowed, jnp.exp(scores[i * block : (i + 1) * block]), 0.0)
            probs[i * block : (i + 1) * block, :] = weights.astype(BF)
            total = total + jnp.sum(weights, axis=0, keepdims=True)
        mass[...] += total
        heads[...] += contract(v[...], probs[...], 0, 0)

    @pl.when(step < middle)
    def _():
        section(k_near, v_near, near)

    @pl.when(step >= middle)
    def _():
        section(k_far, v_far, far)


def halves_of(shape, steps, column=0):
    half = steps // 2
    return [
        pl.BlockSpec(shape, lambda i, *s: (jnp.minimum(i, half - 1), column)),
        pl.BlockSpec(shape, lambda i, *s: (jnp.maximum(i - half, 0), column)),
    ]


def attend(blocks, queries, q_place, q_start, near, far):
    head_rows = queries.shape[0]
    keys = near.shape[0]
    steps = 2 * keys // KEY_BLOCK
    key_blocks, value_blocks = [halves_of((KEY_BLOCK, HD), steps, c) for c in (0, 1)]
    return pl.pallas_call(
        attend_kernel,
        grid_spec=pltpu.PrefetchScalarGridSpec(
            num_scalar_prefetch=1,
            grid=(steps,),
            in_specs=[
                pl.BlockSpec((head_rows, HD), lambda i, b: (0, 0)),
                pl.BlockSpec((1, head_rows), lambda i, b: (0, 0)),
                pl.BlockSpec((1, head_rows), lambda i, b: (0, 0)),
                key_blocks[0],
                value_blocks[0],
                key_blocks[1],
                value_blocks[1],
            ],
            out_specs=[
                *halves_of((KEY_BLOCK, head_rows), steps),
                pl.BlockSpec((HD, head_rows), lambda i, b: (0, 0)),
                pl.BlockSpec((1, head_rows), lambda i, b: (0, 0)),
            ],
        ),
        out_shape=[
            jax.ShapeDtypeStruct((keys, head_rows), BF),
            jax.ShapeDtypeStruct((keys, head_rows), BF),
            jax.ShapeDtypeStruct((HD, head_rows), F32),
            jax.ShapeDtypeStruct((1, head_rows), F32),
        ],
        compiler_params=pltpu.CompilerParams(vmem_limit_bytes=VMEM_LIMIT),
        cost_estimate=pl.CostEstimate(
            flops=8 * keys * head_rows * HD,
            bytes_accessed=2 * keys * (head_rows + 2 * HD) * 2,
            transcendentals=2 * keys * head_rows,
        ),
        name="attend",
    )(blocks, queries, q_place, q_start, near, near, far, far)


def turned_line(column):
    return jnp.broadcast_to(column, (column.shape[0], 128)).T[0:1, :]


def after_attend_kernel(weighted, mass, out_mat, tokens, gains, heads, heads_low, attn_raw, hidden, second_low):
    rows = tokens.shape[0]
    heads[...] = (weighted[...] * (1.0 / mass[...])).T
    for h in range(H):
        heads_low[:, h * HD : (h + 1) * HD] = heads[h * rows : (h + 1) * rows, :].astype(BF)
    raw = contract(heads_low[...], out_mat[...], 1, 0)
    attn_raw[...] = raw
    total = tokens[...].astype(F32) + raw * root(raw) * gains[1:2, :]
    hidden[...] = total
    second_low[...] = (total * root(total) * gains[2:3, :]).astype(BF)


def after_ffn_kernel(part, other, hidden, cotangent, gains, block_out, d_ffn_low, d_gain):
    raw = part[...] + other[...].astype(F32)
    block_out[...] = (hidden[...] + raw * root(raw) * gains[3:4, :]).astype(BF)
    d_ffn, d_gain[...] = rms_back(raw, gains[3:4, :], cotangent[...].astype(F32))
    d_ffn_low[...] = d_ffn.astype(BF)


def before_attend_back_kernel(
    part, other, hidden, cotangent, gains, attn_raw, out_mat, heads,
    d_hidden, d_attn_low, d_heads, dots, d_gain_ffn_in, d_gain_attn_out,
):
    rows = part.shape[0]
    d_second = part[...] + other[...].astype(F32)
    extra, d_gain_ffn_in[...] = rms_back(hidden[...], gains[2:3, :], d_second)
    total = cotangent[...].astype(F32) + extra
    d_hidden[...] = total
    d_attn, d_gain_attn_out[...] = rms_back(attn_raw[...], gains[1:2, :], total)
    low = d_attn.astype(BF)
    d_attn_low[...] = low
    for h in range(H):
        at = pl.ds(h * rows, rows)
        head = contract(low, out_mat[h * HD : (h + 1) * HD, :], 1, 1).astype(BF)
        d_heads[at, :] = head
        dots[:, at] = turned_line(
            jnp.sum(head.astype(F32) * heads[at, :], axis=1, keepdims=True)
        )


def attend_back_kernel(
    q, d_heads, mass, dots, near, far, k_near, v_near, k_far, v_far, d_queries, d_near, d_far
):
    step = pl.program_id(0)
    middle = pl.num_programs(0) // 2

    @pl.when(step == 0)
    def _():
        d_queries[...] = jnp.zeros_like(d_queries)

    def section(probs, k, v, out):
        d_probs = contract(v[...], d_heads[...], 1, 1)
        chance = probs[...].astype(F32) * (1.0 / mass[...])
        d_scores = (chance * (d_probs - dots[...])).astype(BF)
        out[:, :HD] = contract(d_scores, q[...], 1, 0).astype(BF)
        out[:, HD:] = contract(chance.astype(BF), d_heads[...], 1, 0).astype(BF)
        d_queries[...] += contract(k[...], d_scores, 0, 0)

    @pl.when(step < middle)
    def _():
        section(near, k_near, v_near, d_near)

    @pl.when(step >= middle)
    def _():
        section(far, k_far, v_far, d_far)


def attend_back(queries, d_heads, mass, dots, probs, pairs):
    head_rows = queries.shape[0]
    keys = pairs[0].shape[0]
    steps = 2 * keys // KEY_BLOCK
    whole = pl.BlockSpec((head_rows, HD), lambda i: (0, 0))
    line = pl.BlockSpec((1, head_rows), lambda i: (0, 0))
    key_blocks, value_blocks = [halves_of((KEY_BLOCK, HD), steps, c) for c in (0, 1)]
    return pl.pallas_call(
        attend_back_kernel,
        grid=(steps,),
        in_specs=[
            whole,
            whole,
            line,
            line,
            *halves_of((KEY_BLOCK, head_rows), steps),
            key_blocks[0],
            value_blocks[0],
            key_blocks[1],
            value_blocks[1],
        ],
        out_specs=[
            pl.BlockSpec((HD, head_rows), lambda i: (0, 0)),
            *halves_of((KEY_BLOCK, 2 * HD), steps),
        ],
        out_shape=[
            jax.ShapeDtypeStruct((HD, head_rows), F32),
            jax.ShapeDtypeStruct((keys, 2 * HD), BF),
            jax.ShapeDtypeStruct((keys, 2 * HD), BF),
        ],
        compiler_params=pltpu.CompilerParams(vmem_limit_bytes=VMEM_LIMIT),
        cost_estimate=pl.CostEstimate(
            flops=16 * keys * head_rows * HD,
            bytes_accessed=2 * keys * (head_rows + 4 * HD) * 2,
            transcendentals=0,
        ),
        name="attend_back",
    )(queries, d_heads, mass, dots, *probs, pairs[0], pairs[0], pairs[1], pairs[1])


def spread_rows(product, mine, size, keep, send, first):
    step = keep.shape[0] // 2
    width = product.shape[1]
    for offset in range(4):
        rows = product[pl.ds(pl.multiple_of((mine ^ offset) * size, 32), size), :]
        out = send if offset % 2 else keep
        begin = offset // 2 * step + first
        out[begin : begin + size, :width] = rows.astype(out.dtype)


def query_back_kernel(
    mine, d_queries, query_raw, gains, cosine, sine, query_mat, first_low, heads_low, d_attn_low,
    keep, send, d_first, d_gain, product, out_product, query_low,
):
    rows = first_low.shape[0]
    gain = gains[0:1, :]
    d_gain[...] = jnp.zeros_like(d_gain)
    for h in range(H):
        columns = pl.ds(h * HD, HD)
        head = d_queries[:, h * rows : (h + 1) * rows].T * HD ** (-0.5)
        head = rotate(head, cosine[...], -sine[...])
        d_raw, d_head_gain = rms_back(query_raw[:, columns], gain, head)
        d_gain[...] += d_head_gain
        query_low[:, columns] = d_raw.astype(BF)
    d_first[...] = contract(query_low[...], query_mat[...], 1, 1)
    model, inner = product.shape[0] // 4, out_product.shape[0] // 4
    keep[...] = jnp.zeros_like(keep)
    send[...] = jnp.zeros_like(send)
    product[...] = contract(first_low[...], query_low[...], 0, 0)
    spread_rows(product, mine[0], model, keep, send, 0)
    out_product[...] = contract(heads_low[...], d_attn_low[...], 0, 0)
    spread_rows(out_product, mine[0], inner, keep, send, model)


def key_back_kernel(
    mine, sums, *refs
):
    terms, refs = refs[:-19], refs[-19:]
    (
        key_raw, gains, head_gains, cosine, sine, pair_mat, first_low, d_first_query, tokens, d_hidden,
        d_gain_attn_out, d_gain_ffn_in, d_gain_ffn_out, d_gain_query,
        grad_tokens, keep, send, product, gain_lines,
    ) = refs
    total = sums[...]
    for term in terms:
        total = total + term[...].astype(F32)
    d_key = rotate(total[:, :HD], cosine[...], -sine[...])
    d_raw, d_gain_key = rms_back(key_raw[...], head_gains[1:2, :], d_key)
    low = jnp.concatenate([d_raw, total[:, HD:]], axis=1).astype(BF)
    d_first = d_first_query[...] + contract(low, pair_mat[...], 1, 1)
    extra, d_gain_attn_in = rms_back(tokens[...].astype(F32), gains[0:1, :], d_first)
    grad_tokens[...] = d_hidden[...] + extra
    product[:, : 2 * HD] = contract(first_low[...], low, 0, 0)
    gain_lines[...] = jnp.zeros_like(gain_lines)
    for i, line in enumerate(
        (d_gain_attn_in, d_gain_attn_out[...], d_gain_ffn_in[...], d_gain_ffn_out[...])
    ):
        gain_lines[i : i + 1, :] = line
    size, head_size = product.shape[0] // 4, HD // 4
    for i, line in enumerate((d_gain_query[...], d_gain_key)):
        pieces = []
        for r in range(4):
            pieces += [line[:, r * head_size : (r + 1) * head_size], jnp.zeros((1, size - head_size), F32)]
        gain_lines[4 + i : 5 + i, :] = jnp.concatenate(pieces, axis=1)
    product[:, 2 * HD :] = gain_lines[...].T
    keep[...] = jnp.zeros_like(keep)
    send[...] = jnp.zeros_like(send)
    spread_rows(product, mine[0], size, keep, send, 0)


def left_of(owner, part):
    return pl.multiple_of(owner * part - part % 128 * (owner % 2), 128)


def carve_kernel(part, mine, w, own, core):
    for offset, out in enumerate((own, core)):
        out[...] = w[:, :, pl.ds(left_of(mine[0] ^ offset, part), out.shape[2])]


def carve(w, mine, part, wide):
    rows, step = w.shape[1], 48
    return pl.pallas_call(
        functools.partial(carve_kernel, part),
        grid_spec=pltpu.PrefetchScalarGridSpec(
            num_scalar_prefetch=1,
            grid=(rows // step,),
            in_specs=[pl.BlockSpec((2, step, w.shape[2]), lambda i, p: (0, i, 0))],
            out_specs=[pl.BlockSpec((2, step, wide), lambda i, p: (0, i, 0))] * 2,
        ),
        out_shape=[jax.ShapeDtypeStruct((2, rows, wide), BF)] * 2,
        compiler_params=pltpu.CompilerParams(vmem_limit_bytes=VMEM_LIMIT),
        name="carve",
    )(mine[None], w)


def carve_quarters_kernel(part, place, w, near, corner):
    mine, side = place[0], place[2]
    for offset, out in ((2, near), (3, corner)):
        at = pl.ds(left_of(mine ^ offset, part), out.shape[2])
        for s in range(2):

            @pl.when(side == s)
            def _(s=s):
                out[0] = w[:, s, at]


def carve_quarters(w, place, part, wide):
    rows, step = w.shape[0], 48
    half = rows // 2 // step
    return pl.pallas_call(
        functools.partial(carve_quarters_kernel, part),
        grid_spec=pltpu.PrefetchScalarGridSpec(
            num_scalar_prefetch=1,
            grid=(half,),
            in_specs=[pl.BlockSpec((step, 2, w.shape[2]), lambda i, p: (i + half * p[1], 0, 0))],
            out_specs=[pl.BlockSpec((1, step, wide), lambda i, p: (0, i, 0))] * 2,
        ),
        out_shape=[jax.ShapeDtypeStruct((1, rows // 2, wide), BF)] * 2,
        compiler_params=pltpu.CompilerParams(vmem_limit_bytes=VMEM_ALL),
        name="carve_quarters",
    )(place, w)


def walk(shape, first, count, scalars, dim=0):
    def place(i, *unused):
        return tuple(jnp.clip(i - first, 0, count - 1) if d == dim else 0 for d in range(len(shape)))

    return pl.BlockSpec(shape, place)


def settle_kernel(counts, places, *refs):
    out, sources = refs[-1], refs[:-1]
    step, first = pl.program_id(0), 0
    for source, count in zip(sources, counts):

        @pl.when((step >= first) & (step < first + count))
        def _(source=source):
            out[...] = source[...]

        first += count


def settle(places, rows, *sources):
    counts = [source.shape[0] // rows for source in sources]
    width = sources[0].shape[1]
    starts = [sum(counts[:i]) for i in range(len(counts))]
    return pl.pallas_call(
        functools.partial(settle_kernel, counts),
        grid_spec=pltpu.PrefetchScalarGridSpec(
            num_scalar_prefetch=1,
            grid=(sum(counts),),
            in_specs=[walk((rows, width), f, c, 1) for f, c in zip(starts, counts)],
            out_specs=pl.BlockSpec((rows, width), lambda i, p: (p[i], 0)),
        ),
        out_shape=jax.ShapeDtypeStruct((sum(counts) * rows, width), sources[0].dtype),
        compiler_params=pltpu.CompilerParams(vmem_limit_bytes=VMEM_LIMIT),
        name="settle",
    )(places, *sources)


def lay_kernel(counts, sides, rows, *refs):
    out, sources = refs[-1], refs[: len(counts)]
    step, first = pl.program_id(0), 0
    width = out.shape[3]
    for source, count in zip(sources, counts):

        @pl.when((step >= first) & (step < first + count))
        def _(source=source):
            for block in range(out.shape[1]):
                out[0, block] = source[0, :, block * width : (block + 1) * width]

        first += count


def lay(places, sources, laid=None):
    half, wide = sources[-1].shape[1], sources[-1].shape[2]
    counts = [source.shape[0] * source.shape[1] // half for source in sources]

    def run(first, count):
        def place(i, s, r):
            j = jnp.clip(i - first, 0, count - 1)
            return (j // 2, j % 2, 0)

        return pl.BlockSpec((1, half, wide), place)

    base = [] if laid is None else [laid]
    sides, rows = [jnp.stack([jnp.asarray(p[i], jnp.int32) for p in places]) for i in (0, 1)]
    return pl.pallas_call(
        functools.partial(lay_kernel, counts),
        grid_spec=pltpu.PrefetchScalarGridSpec(
            num_scalar_prefetch=2,
            grid=(sum(counts),),
            in_specs=[run(sum(counts[:i]), count) for i, count in enumerate(counts)]
            + [pl.BlockSpec(memory_space=pl.ANY)] * len(base),
            out_specs=pl.BlockSpec(
                (1, wide // 256, half, 256), lambda i, s, r: (s[i], 0, r[i], 0)
            ),
        ),
        out_shape=jax.ShapeDtypeStruct((2, wide // 256, 8 * half, 256), BF),
        input_output_aliases={2 + len(sources): 0} if base else {},
        compiler_params=pltpu.CompilerParams(vmem_limit_bytes=VMEM_ALL),
        name="lay",
    )(sides, rows, *sources, *base)


def contract(left, right, left_dim, right_dim):
    return lax.dot_general(
        left, right, (((left_dim,), (right_dim,)), ((), ())), preferred_element_type=F32
    )


def gelu_and_slope(x):
    scale = math.sqrt(2.0 / math.pi)
    cubic = (scale * 0.044715) * (x * x * x)
    inner = scale * x + cubic
    share = 0.5 + 0.5 * jnp.tanh(inner)
    return x * share, share + share * (1.0 - share) * (2.0 * inner + 4.0 * cubic)


def place_rows(part, blocks, mine, block, source, rows, sem):
    width = source.shape[0]
    odd = mine % 2
    extra = blocks * width - part
    begins = (block == 0) & (odd == 1)
    ends = (block == blocks - 1) & (odd == 0)

    def put(first, at, size):
        copy = pltpu.make_async_copy(
            source.at[pl.ds(first, size), :], rows.at[pl.ds(at, size), :], sem
        )
        copy.start()
        copy.wait()

    @pl.when(begins)
    def _():
        put(extra, 0, width - extra)

    @pl.when(ends)
    def _():
        put(0, (blocks - 1) * width, width - extra)

    @pl.when(jnp.logical_not(begins | ends))
    def _():
        put(0, pl.multiple_of(block * width - odd * extra, 64), width)


def fill_rows_kernel(part, blocks, info, *refs):
    sources, (rows, block, sem) = refs[:-4], refs[-3:]
    for partner, source in enumerate(sources):
        width = block.shape[0]
        for tile in range(block.shape[1] // 128):
            block[:, tile * 128 : (tile + 1) * 128] = source[
                tile * width : (tile + 1) * width, width : width + 128
            ].astype(F32)
        place_rows(part, blocks, info[0], info[1 + partner], block, rows, sem)


def fill_rows(info, part, blocks, sources, rows):
    whole = pl.BlockSpec(memory_space=pltpu.VMEM)
    anywhere = pl.BlockSpec(memory_space=pl.ANY)
    return pl.pallas_call(
        functools.partial(fill_rows_kernel, part, blocks),
        in_specs=[pl.BlockSpec(memory_space=pltpu.SMEM)] + [whole] * len(sources) + [anywhere],
        out_specs=anywhere,
        out_shape=jax.ShapeDtypeStruct(rows.shape, rows.dtype),
        scratch_shapes=[pltpu.VMEM((256, rows.shape[1]), F32), pltpu.SemaphoreType.DMA],
        input_output_aliases={1 + len(sources): 0},
        compiler_params=pltpu.CompilerParams(vmem_limit_bytes=VMEM_LIMIT),
        name="fill_rows",
    )(info, *sources, rows)


def ffn_gradients_kernel(part, apart, blocks, info, second, d_ffn, w_gate, w_up, w_down, *rest):
    outs, down_out, act, d_both, both_sum, down_sum, sem = rest[-10:-6], *rest[-6:]
    step = pl.program_id(1)
    rows, slab = second.shape[0], 256
    width = act.shape[1]

    def products(r):
        at = pl.ds(r * slab, slab)
        return (
            contract(second[at, :], w_gate[0, 0], 1, 0),
            contract(second[at, :], w_up[0, 0], 1, 0),
            contract(d_ffn[at, :], w_down[...], 1, 1),
        )

    ahead = products(0)
    for r in range(rows // slab):
        at = pl.ds(r * slab, slab)
        gate, upper, d_act = ahead
        if r + 1 < rows // slab:
            ahead = products(r + 1)
        value, slope = gelu_and_slope(gate)
        act[at, :] = (value * upper).astype(BF)
        d_both[at, :width] = (d_act * upper * slope).astype(BF)
        d_both[at, width:] = (d_act * value).astype(BF)
    grad_both = contract(second[...], d_both[...], 0, 0)
    grad_down = contract(act[...], d_ffn[...], 0, 0)

    @pl.when(step == 0)
    def _():
        both_sum[...] = grad_both
        down_sum[...] = grad_down

    @pl.when(step > 0)
    def _():
        both_sum[...] += grad_both
        down_sum[...] += grad_down

    @pl.when(step == pl.num_programs(1) - 1)
    def _():
        if apart:
            for tile in range(down_out.shape[0]):
                down_out[tile] = down_sum[:, tile * 128 : (tile + 1) * 128].astype(BF)
        else:
            place_rows(part, blocks, info[0], info[1 + pl.program_id(0)], down_sum, down_out, sem)

        quarter = second.shape[1] // 4
        for offset, out in enumerate(outs):
            at = pl.ds(pl.multiple_of((info[0] ^ offset) * quarter, 32), quarter)
            out[0] = both_sum[at, :width].astype(BF)
            out[1] = both_sum[at, width:].astype(BF)


def ffn_gradients(info, second_all, d_ffn_all, in_mat, down_mat, part, count, down_rows, apart):
    tokens, model = second_all.shape
    slab, width = min(2048, tokens), 256
    columns = count * width
    tall = pl.BlockSpec((slab, model), lambda j, t, m: (t, 0))
    anywhere = pl.BlockSpec(memory_space=pl.ANY)
    earlier = [] if down_rows is None else [down_rows]
    return pl.pallas_call(
        functools.partial(ffn_gradients_kernel, part, apart, down_mat.shape[0] // width),
        grid_spec=pltpu.PrefetchScalarGridSpec(
            num_scalar_prefetch=1,
            grid=(count, tokens // slab),
            in_specs=[
                tall,
                tall,
                pl.BlockSpec((1, 1, model, width), lambda j, t, m: (0, m[1 + j], 0, 0)),
                pl.BlockSpec((1, 1, model, width), lambda j, t, m: (1, m[1 + j], 0, 0)),
                pl.BlockSpec((width, model), lambda j, t, m: (m[1 + j], 0)),
            ]
            + [anywhere] * len(earlier),
            out_specs=[pl.BlockSpec((2, model // 4, width), lambda j, t, m: (0, 0, j))] * 4
            + [
                pl.BlockSpec((model // 128, width, 128), lambda j, t, m: (0, j, 0))
                if apart
                else anywhere
            ],
            scratch_shapes=[
                pltpu.VMEM((slab, width), BF),
                pltpu.VMEM((slab, 2 * width), BF),
                pltpu.VMEM((model, 2 * width), F32),
                pltpu.VMEM((width, model), F32),
                pltpu.SemaphoreType.DMA,
            ],
        ),
        out_shape=[jax.ShapeDtypeStruct((2, model // 4, columns), BF)] * 4
        + [
            jax.ShapeDtypeStruct((model // 128, columns, 128), BF)
            if apart
            else jax.ShapeDtypeStruct((part, model), F32)
        ],
        input_output_aliases={6: 4} if earlier else {},
        compiler_params=pltpu.CompilerParams(vmem_limit_bytes=VMEM_ALL),
        cost_estimate=pl.CostEstimate(
            flops=12 * tokens * model * columns,
            bytes_accessed=4 * tokens * model * count,
            transcendentals=tokens * columns,
        ),
        name="ffn_gradients",
    )(info, second_all, d_ffn_all, in_mat, in_mat, down_mat, *earlier)


def ffn_forward_kernel(near, far, w_gate, w_up, w_down, value, factor, keep, send, act, total):
    step, half = pl.program_id(0), near.shape[0]

    @pl.when(step == 0)
    def _():
        total[...] = jnp.zeros_like(total)

    def products(rows):
        return contract(rows[...], w_gate[0, 0], 1, 0), contract(rows[...], w_up[0, 0], 1, 0)

    ahead = products(near)
    for i in range(2):
        at = pl.ds(i * half, half)
        gate, upper = ahead
        if i == 0:
            ahead = products(far)
        gelu, slope = gelu_and_slope(gate)
        act[at, :] = (gelu * upper).astype(BF)
        value[at, :] = gelu.astype(BF)
        factor[at, :] = (upper * slope).astype(BF)
    total[...] += contract(act[...], w_down[...], 1, 0)

    @pl.when(step == pl.num_programs(0) - 1)
    def _():
        keep[...], send[...] = total[:half, :], total[half:, :].astype(BF)


def ffn_backward_kernel(
    near, far, value, factor, w_gate, w_up, w_down, keep, send, d_gate, d_up, total
):
    step, half = pl.program_id(0), near.shape[0]

    @pl.when(step == 0)
    def _():
        total[...] = jnp.zeros_like(total)

    for rows, at in ((near, pl.ds(0, half)), (far, pl.ds(half, half))):
        d_act = contract(rows[...], w_down[...], 1, 1)
        d_gate[at, :] = (d_act * factor[at, :].astype(F32)).astype(BF)
        d_up[at, :] = (d_act * value[at, :].astype(F32)).astype(BF)
    total[...] += contract(d_gate[...], w_gate[0, 0], 1, 1) + contract(d_up[...], w_up[0, 0], 1, 1)

    @pl.when(step == pl.num_programs(0) - 1)
    def _():
        keep[...], send[...] = total[:half, :], total[half:, :].astype(BF)


def ffn_group(kernel, near, far, in_mat, down_mat, *kept):
    half, model = near.shape
    wide, width = down_mat.shape[0], 256
    rows = pl.BlockSpec((half, model), lambda j: (0, 0))
    column = pl.BlockSpec((2 * half, width), lambda j: (0, j))
    forward = not kept
    shape = jax.ShapeDtypeStruct((2 * half, wide), BF)
    return pl.pallas_call(
        kernel,
        grid=(wide // width,),
        in_specs=[rows, rows]
        + [column] * len(kept)
        + [
            pl.BlockSpec((1, 1, model, width), lambda j: (0, j, 0, 0)),
            pl.BlockSpec((1, 1, model, width), lambda j: (1, j, 0, 0)),
            pl.BlockSpec((width, model), lambda j: (j, 0)),
        ],
        out_specs=[column] * (2 * forward) + [rows, rows],
        out_shape=[shape] * (2 * forward)
        + [jax.ShapeDtypeStruct((half, model), F32), jax.ShapeDtypeStruct((half, model), BF)],
        scratch_shapes=[pltpu.VMEM((2 * half, width), BF)] * (1 if forward else 2)
        + [pltpu.VMEM((2 * half, model), F32)],
        compiler_params=pltpu.CompilerParams(vmem_limit_bytes=VMEM_ALL),
        cost_estimate=pl.CostEstimate(
            flops=12 * half * model * wide,
            bytes_accessed=6 * model * wide + 16 * half * wide,
            transcendentals=2 * half * wide,
        ),
        name="ffn_forward" if forward else "ffn_backward",
    )(near, far, *kept, in_mat, in_mat, down_mat)


def unfold_kernel(part, info, *refs):
    shared, sources, (out, wide) = refs[:4], refs[4:-2], refs[-2:]
    mine, width = info[0], 256
    for partner, source in enumerate(shared):
        at = pl.ds(pl.multiple_of(info[1 + partner] * width, 128), width)
        for offset in range(4):
            wide[mine ^ offset, :, :, at] = source[offset, :, :, :width]
    first = 4 * width
    for r in range(0, len(sources), 4):
        last = first + sources[r].shape[2]
        for offset in range(4):
            wide[mine ^ offset, :, :, first:last] = sources[r + offset][...]
        first = last
    cut = wide.shape[3] - 128
    left = lax.broadcasted_iota(jnp.int32, (wide.shape[2], 128), 1) < part % 128
    for side in range(2):
        rows = [wide[owner, side].astype(F32) for owner in range(4)]
        pieces = []
        for even, odd in (rows[:2], rows[2:]):
            shared_tile = jnp.where(left, even[:, cut:], odd[:, :128])
            pieces += [even[:, :cut], shared_tile, odd[:, 128:]]
        out[:, side, :] = jnp.concatenate(pieces, axis=1)


def unfold(info, part, shared, ranges):
    sources = [piece for pieces in ranges for piece in pieces]
    rows, step = sources[0].shape[1], 32
    shared = [s.reshape(4, 2, rows, s.shape[1]) for s in shared]
    columns = sum(pieces[0].shape[2] for pieces in ranges) + 4 * 256
    return pl.pallas_call(
        functools.partial(unfold_kernel, part),
        grid_spec=pltpu.PrefetchScalarGridSpec(
            num_scalar_prefetch=1,
            grid=(rows // step,),
            in_specs=[
                pl.BlockSpec((4, 2, step, s.shape[3]), lambda i, m: (0, 0, i, 0)) for s in shared
            ]
            + [pl.BlockSpec((2, step, s.shape[2]), lambda i, m: (0, i, 0)) for s in sources],
            out_specs=pl.BlockSpec((step, 2, 4 * part), lambda i, m: (i, 0, 0)),
            scratch_shapes=[pltpu.VMEM((4, 2, step, columns), BF)],
        ),
        out_shape=jax.ShapeDtypeStruct((rows, 2, 4 * part), F32),
        compiler_params=pltpu.CompilerParams(vmem_limit_bytes=VMEM_LIMIT),
        name="unfold",
    )(info, *shared, *sources)


def pick(table, index):
    hit = index[:, None] == jnp.arange(table.shape[0], dtype=jnp.int32)[None, :]
    return jnp.sum(jnp.where(hit, table[None, :], 0), axis=1)


def body(
    tokens,
    cotangent,
    block_table,
    sequence_ids,
    w_query,
    w_key,
    w_value,
    w_out,
    w_in,
    w_down,
    gain_attn_in,
    gain_attn_out,
    gain_ffn_in,
    gain_ffn_out,
    gain_query,
    gain_key,
):
    rows = tokens.shape[0]
    block = rows // 2
    model, part = w_in.shape[0] * 4, w_down.shape[0]
    mine = lax.axis_index("fsdp")
    me = lax.axis_index("ctx") * 4 + mine

    gains = (gain_attn_in, gain_attn_out, gain_ffn_in, gain_ffn_out, gain_query, gain_key)
    sizes = [g.shape[0] for g in gains]
    (packed,) = kernel_call(
        pack_kernel,
        [((w_key.shape[0] + 16, 2 * HD), BF)],
        w_key,
        w_value,
        *[g[None] for g in gains],
        name="pack",
    )
    packed_flow = Flow(gather_group(packed))

    wide = -(-part // 256) * 256
    quarter = model // 4
    boundary = jnp.sum((sequence_ids == 0).astype(jnp.int32))
    everyone = me ^ jnp.array(wide_offsets(), jnp.int32)
    blocks = pick(block_table, jnp.stack([2 * everyone, 2 * everyone + 1], axis=1).reshape(-1))
    place = (blocks[:2, None] * block + jnp.arange(block, dtype=jnp.int32)[None, :]).reshape(-1)
    start = jnp.where(place >= boundary, boundary, 0)
    position = place - start
    inverse_angle = 1000000.0 ** (-jnp.arange(HD // 2, dtype=F32) / (HD // 2))
    angles = position.astype(F32)[:, None] * inverse_angle[None, :]
    cosine, sine = jnp.cos(angles), jnp.sin(angles)
    q_place, q_start = jnp.tile(place, H)[None], jnp.tile(start, H)[None]

    low_bit, high_bit = lax.axis_index("ctx") % 2, lax.axis_index("ctx") // 2 % 2
    quarters = carve_quarters(w_in, jnp.stack([mine, low_bit, high_bit]), part, wide)
    quarters = pace(quarters, packed_flow)
    arrived = []
    columns_flow = Flow(exchange_columns(quarters, arrived))
    cosine, sine, q_place, q_start = pace((cosine, sine, q_place, q_start), packed_flow)
    pair_mat, model_gains, head_gains = kernel_call(
        unpack_kernel,
        [((model, 2 * HD), BF), ((8, model), F32), ((8, HD), F32)],
        *packed_flow.result,
        scalars=(mine[None],),
        name="unpack",
    )
    first_low, key_raw, pair_rows = kernel_call(
        key_kernel,
        [((rows, model), BF), ((rows, HD), F32), ((rows, 2 * HD), BF)],
        tokens,
        model_gains,
        head_gains,
        pair_mat,
        cosine,
        sine,
        name="keys",
    )
    pairs_flow = Flow(gather_wide(pair_rows))
    own, to_core = carve(jnp.swapaxes(w_in, 0, 1), mine, part, wide)
    down_mat = lax.dynamic_update_slice_in_dim(
        jnp.zeros((wide, model), BF), w_down, part % 128 * (mine % 2), 0
    )
    own, to_core, w_query, down_mat = pace(
        (own, to_core, w_query, down_mat), pairs_flow, columns_flow
    )
    core_flow = Flow(iter_once([swap(to_core, 1)]))
    query_flow = Flow(gather_rows(w_query, mine))
    pace((), pairs_flow, columns_flow, core_flow)
    (w_out,) = pace((w_out,), pairs_flow, columns_flow, query_flow)
    out_flow = Flow(gather_rows(w_out, mine))
    pairs = finish(pairs_flow)
    query_mat = finish(query_flow)
    query_raw, queries = kernel_call(
        query_kernel,
        [((rows, H * HD), F32), ((H * rows, HD), BF)],
        first_low,
        head_gains,
        query_mat,
        cosine,
        sine,
        name="queries",
    )
    *probs, weighted, mass = attend(blocks, queries, q_place, q_start, *pairs)
    weighted, mass = pace((weighted, mass), out_flow, columns_flow)
    out_mat = finish(out_flow)
    heads, heads_low, attn_raw, hidden, second_low = kernel_call(
        after_attend_kernel,
        [
            ((H * rows, HD), F32),
            ((rows, H * HD), BF),
            ((rows, model), F32),
            ((rows, model), F32),
            ((rows, model), BF),
        ],
        weighted,
        mass,
        out_mat,
        tokens,
        model_gains,
        name="after_attend",
    )

    group_flow = Flow(gather_group(second_low))
    second_all = lax.all_gather(second_low, AXES, axis=0, tiled=True)
    places = [
        (side, (mine ^ offset) * 2 + bit) for offset in (0, 1) for side in (0, 1) for bit in (0, 1)
    ]
    for offset in (2, 3):
        places += [
            (side, (mine ^ offset) * 2 + bit)
            for side in (high_bit, 1 - high_bit)
            for bit in (low_bit, 1 - low_bit)
        ]
    laid = lay(places[:9] + places[10:], (own, *core_flow.result, *arrived))
    (laid,) = pace((laid,), group_flow, columns_flow)
    in_mat = lay(places[9:10], columns_flow.result, laid)
    value, factor, keep, send = ffn_group(ffn_forward_kernel, *finish(group_flow), in_mat, down_mat)
    block_out, d_ffn_low, d_gain_ffn_out = kernel_call(
        after_ffn_kernel,
        [((rows, model), BF), ((rows, model), BF), ((1, model), F32)],
        *finish(Flow(scatter_group(keep, send))),
        hidden,
        cotangent,
        model_gains,
        name="after_ffn",
    )
    group_flow = Flow(gather_group(d_ffn_low))
    d_ffn_all = lax.all_gather(d_ffn_low, AXES, axis=0, tiled=True)
    keep, send = ffn_group(
        ffn_backward_kernel, *finish(group_flow), in_mat, down_mat, value, factor
    )
    d_hidden, d_attn_low, d_heads, dots, d_gain_ffn_in, d_gain_attn_out = kernel_call(
        before_attend_back_kernel,
        [
            ((rows, model), F32),
            ((rows, model), BF),
            ((H * rows, HD), BF),
            ((1, H * rows), F32),
            ((1, model), F32),
            ((1, model), F32),
        ],
        *finish(Flow(scatter_group(keep, send))),
        hidden,
        cotangent,
        model_gains,
        attn_raw,
        out_mat,
        heads,
        name="before_attend_back",
    )

    d_queries, *d_pairs = attend_back(queries, d_heads, mass, dots, probs, pairs)
    sums_flow = Flow(scatter_wide(*d_pairs))
    early_rows = quarter + H * HD // 4
    keep, send, d_first_query, d_gain_query = kernel_call(
        query_back_kernel,
        [
            ((2 * early_rows, model), F32),
            ((2 * early_rows, model), BF),
            ((rows, model), F32),
            ((1, HD), F32),
        ],
        d_queries,
        query_raw,
        head_gains,
        cosine,
        sine,
        query_mat,
        first_low,
        heads_low,
        d_attn_low,
        scalars=(mine[None],),
        scratch=[((model, H * HD), F32), ((H * HD, model), F32), ((rows, H * HD), BF)],
        name="query_back",
    )
    keep, send, d_first_query = pace((keep, send, d_first_query), sums_flow)
    pace((), sums_flow)
    early_flow = Flow(scatter_group(keep, send))
    pace((), sums_flow, early_flow)
    pace((), sums_flow)
    grad_tokens, keep, send = kernel_call(
        key_back_kernel,
        [
            ((rows, model), F32),
            ((2 * quarter, 2 * HD + 128), F32),
            ((2 * quarter, 2 * HD + 128), BF),
        ],
        *sums_flow.result,
        key_raw,
        model_gains,
        head_gains,
        cosine,
        sine,
        pair_mat,
        first_low,
        d_first_query,
        tokens,
        d_hidden,
        d_gain_attn_out,
        d_gain_ffn_in,
        d_gain_ffn_out,
        d_gain_query,
        scalars=(mine[None],),
        scratch=[((model, 2 * HD + 128), F32), ((128, model), F32)],
        name="key_back",
    )
    tail_flow = Flow(scatter_group(keep, send))

    count = wide // 256
    block_info = jnp.stack([mine, low_bit, 1 - low_bit, 2 + high_bit, 3 - high_bit])

    def total(flow):
        near, far = flow.result
        return near + far.astype(F32)

    pace((), tail_flow)
    both = (second_all, d_ffn_all)
    *pieces, down = ffn_gradients(
        block_info[jnp.array([0, 1, 3])], *both, in_mat, down_mat, part, 2, None, True
    )
    both, pieces, down = pace((both, pieces, down), tail_flow, early_flow)
    early, tail = total(early_flow), total(tail_flow)
    tail = jnp.pad(tail, ((0, 0), (0, model - tail.shape[1])))
    rest = lax.psum(join(early, tail).astype(BF), "ctx")
    shared_flow = Flow(exchange_results(pieces, down))
    ranges, grad_down = [], None
    for first, last in ((4, 5), (5, count)):
        *pieces, grad_down = ffn_gradients(
            jnp.stack([mine, *[jnp.int32(i) for i in range(first, last)]]),
            *both,
            in_mat,
            down_mat,
            part,
            last - first,
            grad_down,
            False,
        )
        over_x = [sent[2:] for sent in ranges]
        both, grad_down, over_x = pace((both, grad_down, over_x), shared_flow)
        for sent, arrays in zip(ranges, over_x):
            sent[2:] = arrays
        ranges.append([pieces[0]] + [swap(pieces[o], o) for o in (1, 2, 3)])
    shared = shared_flow.result
    grad_down = fill_rows(block_info, part, count, shared, grad_down)
    rest, grad_down = pace((rest, grad_down))
    early, tail = rest[:early_rows], rest[early_rows:]
    grad_in = unfold(block_info, part, shared, ranges)
    early, tail = early.astype(F32), tail.astype(F32)
    grad_query = early[:quarter, : H * HD]
    grad_out = early[quarter:]
    grad_key, grad_value = tail[:quarter, :HD], tail[:quarter, HD : 2 * HD]
    gain_grads = [tail[:size, 2 * HD + i] for i, size in enumerate(sizes)]

    return (
        block_out,
        grad_tokens,
        grad_query,
        grad_key,
        grad_value,
        grad_out,
        grad_in,
        grad_down,
        *gain_grads,
    )


def solution(mesh):
    in_specs = (
        P(AXES, None),
        P(AXES, None),
        P(),
        P(),
        P("fsdp", None),
        P("fsdp", None),
        P("fsdp", None),
        P("fsdp", None),
        P("fsdp", None, None),
        P("fsdp", None),
        P("fsdp"),
        P("fsdp"),
        P("fsdp"),
        P("fsdp"),
        P("fsdp"),
        P("fsdp"),
    )
    out_specs = (
        P(AXES, None),
        P(AXES, None),
        P("fsdp", None),
        P("fsdp", None),
        P("fsdp", None),
        P("fsdp", None),
        P("fsdp", None, None),
        P("fsdp", None),
        P("fsdp"),
        P("fsdp"),
        P("fsdp"),
        P("fsdp"),
        P("fsdp"),
        P("fsdp"),
    )
    return jax.shard_map(body, mesh=mesh, in_specs=in_specs, out_specs=out_specs, check_vma=False)
```

```python
import functools
import math

import jax
import jax.numpy as jnp
from jax import lax
from jax.experimental import pallas as pl
from jax.experimental.pallas import tpu as pltpu
from jax.sharding import PartitionSpec as P

H = 4
HD = 256
EPS = 1e-06
AXES = ("ctx", "fsdp")
BF = jnp.bfloat16
F32 = jnp.float32
KEY_BLOCK = 512
VMEM_LIMIT = 32 * 2**20
VMEM_ALL = 60 * 2**20


def root(values):
    return lax.rsqrt(jnp.mean(values * values, axis=-1, keepdims=True) + EPS)


def rms_back(values, gain, grad):
    scale = root(values)
    scaled = gain * grad
    mean = jnp.mean(values * scaled, axis=-1, keepdims=True)
    return (
        scale * scaled - values * (scale * scale * scale * mean),
        jnp.sum(grad * values * scale, axis=0, keepdims=True),
    )


def rotate(values, cosine, sine):
    half = values.shape[-1] // 2
    first, second = values[:, :half], values[:, half:]
    return jnp.concatenate(
        [first * cosine - second * sine, second * cosine + first * sine], axis=1
    )


class Flow:
    def __init__(self, steps):
        self.steps = steps
        self.result = None
        self.flying = next(steps)

    def land(self, arrays):
        try:
            self.flying = self.steps.send(arrays)
        except StopIteration as stop:
            self.flying, self.result = None, stop.value


def pace(values, *flows):
    flying = [flow.flying for flow in flows]
    values, flying = lax.optimization_barrier((values, flying))
    for flow, arrays in zip(flows, flying):
        flow.land(arrays)
    return values


def finish(flow):
    while flow.flying is not None:
        flow.land(flow.flying)
    return flow.result


def swap(value, offset):
    count = lax.axis_size("ctx") * lax.axis_size("fsdp")
    return lax.ppermute(value, AXES, [(i, i ^ offset) for i in range(count)])


def join(*parts):
    return jnp.concatenate(parts, axis=0)


def iter_once(arrays):
    return (yield arrays)


def gather_group(value):
    (other,) = yield [swap(value, 2)]
    pair = join(value, other)
    (other,) = yield [swap(pair, 1)]
    return pair, other


def scatter_group(keep, send):
    (other,) = yield [swap(send, 1)]
    half = keep.shape[0] // 2
    (far,) = yield [swap((keep[half:] + other[half:].astype(F32)).astype(BF), 2)]
    return keep[:half] + other[:half].astype(F32), far


def wide_offsets():
    highs = [8 * s for s in range(lax.axis_size("ctx") // 2)]
    chip = [low + high for low in (0, 4, 2, 6) for high in highs]
    return chip + [1 + o for o in chip]


def gather_wide(value):
    highs = lax.axis_size("ctx") // 2
    line = join(value, *(yield [swap(value, 8 * s) for s in range(1, highs)]))
    half = line.shape[0] // 2
    along_y, along_x = yield [swap(line, o) for o in (4, 2)]
    corner = yield [swap(along_y[:half], 2), swap(along_x[half:], 4)]
    chip = join(line, along_y, along_x, *corner)
    (other,) = yield [swap(chip, 1)]
    return chip, other


def scatter_wide(near, far):
    highs = lax.axis_size("ctx") // 2
    (other,) = yield [swap(far, 1)]
    chip = near.astype(F32) + other.astype(F32)
    line, along_y, along_x, corner = jnp.split(chip, 4, axis=0)
    mid = line.shape[0] // 2
    corner = corner.astype(BF)
    from_x, from_y = yield [swap(corner[:mid], 2), swap(corner[mid:], 4)]
    along_y = join(along_y[:mid] + from_x.astype(F32), along_y[mid:])
    along_x = join(along_x[:mid], along_x[mid:] + from_y.astype(F32))
    from_y, from_x = yield [swap(along_y.astype(BF), 4), swap(along_x.astype(BF), 2)]
    line = line + from_y.astype(F32) + from_x.astype(F32)
    rows = line.shape[0] // highs
    terms = yield [
        swap(line[s * rows : (s + 1) * rows].astype(BF), 8 * s) for s in range(1, highs)
    ]
    return [line[:rows], *terms]


def gather_rows(value, me):
    pair, other = yield from gather_group(value)
    return settle(me ^ jnp.array([0, 2, 1, 3], jnp.int32), value.shape[0], pair, other)


def exchange_columns(quarters, arrived):
    first, second = yield [swap(quarters[0], 2), swap(quarters[1], 3)]
    (first_z,) = yield [swap(first, 8)]
    second_z, second_y = yield [swap(second, 8), swap(second, 4)]
    first_far, second_far = yield [swap(first_z, 4), swap(second_y, 8)]
    arrived += [first, first_z, first_far, second, second_y, second_z, second_far]
    return (yield [swap(first, 4)])


def exchange_results(pieces, down):
    others = yield [swap(pieces[o], o) for o in (1, 2, 3)]
    mixed = join(*[piece.reshape(-1, piece.shape[2]) for piece in (pieces[0], *others)])
    width = mixed.shape[1] // 2
    first, second = [
        jnp.concatenate([mixed[:, at], down[:, at].reshape(-1, down.shape[2])], axis=1)
        for at in (slice(0, width), slice(width, 2 * width))
    ]
    first_y, second_z = yield [swap(first, 4), swap(second, 8)]
    return [first, first_y, second, second_z]


def kernel_call(kernel, out_shape, *operands, scalars=(), scratch=(), name):
    whole = pl.BlockSpec(memory_space=pltpu.VMEM)
    return pl.pallas_call(
        kernel,
        out_shape=[jax.ShapeDtypeStruct(shape, dtype) for shape, dtype in out_shape],
        in_specs=[pl.BlockSpec(memory_space=pltpu.SMEM)] * len(scalars) + [whole] * len(operands),
        out_specs=[whole] * len(out_shape),
        scratch_shapes=[pltpu.VMEM(shape, dtype) for shape, dtype in scratch],
        compiler_params=pltpu.CompilerParams(vmem_limit_bytes=VMEM_LIMIT),
        name=name,
    )(*scalars, *operands)


def pack_kernel(w_key, w_value, *refs):
    gains, out = refs[:-1], refs[-1]
    rows, width = w_key.shape[0], out.shape[1]
    out[:rows, : w_key.shape[1]] = w_key[...]
    out[:rows, w_key.shape[1] :] = w_value[...]
    lines = [
        jnp.concatenate([g[...].astype(F32), jnp.zeros((1, width - g.shape[1]), F32)], axis=1)
        for g in gains
    ]
    lines.append(jnp.zeros((out.shape[0] - rows - len(lines), width), F32))
    out[rows:, :] = jnp.concatenate(lines, axis=0).astype(BF)


def unpack_kernel(mine, pair, other, pair_mat, wide, narrow):
    size, head_part = wide.shape[1] // 4, narrow.shape[1] // 4
    block = pair.shape[0] // 2
    for m in range(4):

        @pl.when(mine[0] == m)
        def _(m=m):
            lines = []
            for r in range(4):
                source, first = (pair, other)[(m ^ r) % 2], (m ^ r) // 2 * block
                pair_mat[r * size : (r + 1) * size, :] = source[first : first + size, :]
                lines.append(source[first + size : first + block, :].astype(F32))
            for i in range(4):
                wide[i : i + 1, :] = jnp.concatenate([l[i : i + 1, :size] for l in lines], axis=1)
            for i in range(2):
                narrow[i : i + 1, :] = jnp.concatenate(
                    [l[4 + i : 5 + i, :head_part] for l in lines], axis=1
                )


def key_kernel(tokens, gain, key_gain, pair_mat, cosine, sine, first_low, key_raw, pairs):
    inputs = tokens[...].astype(F32)
    low = (inputs * root(inputs) * gain[0:1, :]).astype(BF)
    first_low[...] = low
    raw = contract(low, pair_mat[...], 1, 0)
    key = raw[:, :HD]
    key_raw[...] = key
    key = key * root(key) * key_gain[1:2, :]
    pairs[:, :HD] = rotate(key, cosine[...], sine[...]).astype(BF)
    pairs[:, HD:] = raw[:, HD:].astype(BF)


def query_kernel(first_low, query_gain, query_mat, cosine, sine, query_raw, queries):
    rows = first_low.shape[0]
    raw = contract(first_low[...], query_mat[...], 1, 0)
    query_raw[...] = raw
    for h in range(H):
        head = raw[:, h * HD : (h + 1) * HD]
        head = rotate(head * root(head) * query_gain[0:1, :], cosine[...], sine[...])
        queries[h * rows : (h + 1) * rows, :] = (head * HD ** (-0.5)).astype(BF)


def attend_kernel(blocks, q, q_place, q_start, k_near, v_near, k_far, v_far, near, far, heads, mass):
    step = pl.program_id(0)
    middle = pl.num_programs(0) // 2

    @pl.when(step == 0)
    def _():
        heads[...] = jnp.zeros_like(heads)
        mass[...] = jnp.zeros_like(mass)

    def section(k, v, probs):
        scores = contract(k[...], q[...], 1, 1)
        rows = k.shape[0]
        block = 64
        place, start = q_place[...], q_start[...]
        total = jnp.zeros_like(mass)
        for i in range(rows // block):
            first = blocks[step * (rows // block) + i] * block
            keys = first + lax.broadcasted_iota(jnp.int32, (block, scores.shape[1]), 0)
            allowed = (keys <= place) & (keys >= start)
            weights = jnp.where(allowed, jnp.exp(scores[i * block : (i + 1) * block]), 0.0)
            probs[i * block : (i + 1) * block, :] = weights.astype(BF)
            total = total + jnp.sum(weights, axis=0, keepdims=True)
        mass[...] += total
        heads[...] += contract(v[...], probs[...], 0, 0)

    @pl.when(step < middle)
    def _():
        section(k_near, v_near, near)

    @pl.when(step >= middle)
    def _():
        section(k_far, v_far, far)


def halves_of(shape, steps, column=0):
    half = steps // 2
    return [
        pl.BlockSpec(shape, lambda i, *s: (jnp.minimum(i, half - 1), column)),
        pl.BlockSpec(shape, lambda i, *s: (jnp.maximum(i - half, 0), column)),
    ]


def attend(blocks, queries, q_place, q_start, near, far):
    head_rows = queries.shape[0]
    keys = near.shape[0]
    steps = 2 * keys // KEY_BLOCK
    key_blocks, value_blocks = [halves_of((KEY_BLOCK, HD), steps, c) for c in (0, 1)]
    return pl.pallas_call(
        attend_kernel,
        grid_spec=pltpu.PrefetchScalarGridSpec(
            num_scalar_prefetch=1,
            grid=(steps,),
            in_specs=[
                pl.BlockSpec((head_rows, HD), lambda i, b: (0, 0)),
                pl.BlockSpec((1, head_rows), lambda i, b: (0, 0)),
                pl.BlockSpec((1, head_rows), lambda i, b: (0, 0)),
                key_blocks[0],
                value_blocks[0],
                key_blocks[1],
                value_blocks[1],
            ],
            out_specs=[
                *halves_of((KEY_BLOCK, head_rows), steps),
                pl.BlockSpec((HD, head_rows), lambda i, b: (0, 0)),
                pl.BlockSpec((1, head_rows), lambda i, b: (0, 0)),
            ],
        ),
        out_shape=[
            jax.ShapeDtypeStruct((keys, head_rows), BF),
            jax.ShapeDtypeStruct((keys, head_rows), BF),
            jax.ShapeDtypeStruct((HD, head_rows), F32),
            jax.ShapeDtypeStruct((1, head_rows), F32),
        ],
        compiler_params=pltpu.CompilerParams(vmem_limit_bytes=VMEM_LIMIT),
        cost_estimate=pl.CostEstimate(
            flops=8 * keys * head_rows * HD,
            bytes_accessed=2 * keys * (head_rows + 2 * HD) * 2,
            transcendentals=2 * keys * head_rows,
        ),
        name="attend",
    )(blocks, queries, q_place, q_start, near, near, far, far)


def turned_line(column):
    return jnp.broadcast_to(column, (column.shape[0], 128)).T[0:1, :]


def after_attend_kernel(weighted, mass, out_mat, tokens, gains, heads, heads_low, attn_raw, hidden, second_low):
    rows = tokens.shape[0]
    heads[...] = (weighted[...] * (1.0 / mass[...])).T
    for h in range(H):
        heads_low[:, h * HD : (h + 1) * HD] = heads[h * rows : (h + 1) * rows, :].astype(BF)
    raw = contract(heads_low[...], out_mat[...], 1, 0)
    attn_raw[...] = raw
    total = tokens[...].astype(F32) + raw * root(raw) * gains[1:2, :]
    hidden[...] = total
    second_low[...] = (total * root(total) * gains[2:3, :]).astype(BF)


def after_ffn_kernel(part, other, hidden, cotangent, gains, block_out, d_ffn_low, d_gain):
    raw = part[...] + other[...].astype(F32)
    block_out[...] = (hidden[...] + raw * root(raw) * gains[3:4, :]).astype(BF)
    d_ffn, d_gain[...] = rms_back(raw, gains[3:4, :], cotangent[...].astype(F32))
    d_ffn_low[...] = d_ffn.astype(BF)


def before_attend_back_kernel(
    part, other, hidden, cotangent, gains, attn_raw, out_mat, heads,
    d_hidden, d_attn_low, d_heads, dots, d_gain_ffn_in, d_gain_attn_out,
):
    rows = part.shape[0]
    d_second = part[...] + other[...].astype(F32)
    extra, d_gain_ffn_in[...] = rms_back(hidden[...], gains[2:3, :], d_second)
    total = cotangent[...].astype(F32) + extra
    d_hidden[...] = total
    d_attn, d_gain_attn_out[...] = rms_back(attn_raw[...], gains[1:2, :], total)
    low = d_attn.astype(BF)
    d_attn_low[...] = low
    for h in range(H):
        at = pl.ds(h * rows, rows)
        head = contract(low, out_mat[h * HD : (h + 1) * HD, :], 1, 1).astype(BF)
        d_heads[at, :] = head
        dots[:, at] = turned_line(
            jnp.sum(head.astype(F32) * heads[at, :], axis=1, keepdims=True)
        )


def attend_back_kernel(
    q, d_heads, mass, dots, near, far, k_near, v_near, k_far, v_far, d_queries, d_near, d_far
):
    step = pl.program_id(0)
    middle = pl.num_programs(0) // 2

    @pl.when(step == 0)
    def _():
        d_queries[...] = jnp.zeros_like(d_queries)

    def section(probs, k, v, out):
        d_probs = contract(v[...], d_heads[...], 1, 1)
        chance = probs[...].astype(F32) * (1.0 / mass[...])
        d_scores = (chance * (d_probs - dots[...])).astype(BF)
        out[:, :HD] = contract(d_scores, q[...], 1, 0).astype(BF)
        out[:, HD:] = contract(chance.astype(BF), d_heads[...], 1, 0).astype(BF)
        d_queries[...] += contract(k[...], d_scores, 0, 0)

    @pl.when(step < middle)
    def _():
        section(near, k_near, v_near, d_near)

    @pl.when(step >= middle)
    def _():
        section(far, k_far, v_far, d_far)


def attend_back(queries, d_heads, mass, dots, probs, pairs):
    head_rows = queries.shape[0]
    keys = pairs[0].shape[0]
    steps = 2 * keys // KEY_BLOCK
    whole = pl.BlockSpec((head_rows, HD), lambda i: (0, 0))
    line = pl.BlockSpec((1, head_rows), lambda i: (0, 0))
    key_blocks, value_blocks = [halves_of((KEY_BLOCK, HD), steps, c) for c in (0, 1)]
    return pl.pallas_call(
        attend_back_kernel,
        grid=(steps,),
        in_specs=[
            whole,
            whole,
            line,
            line,
            *halves_of((KEY_BLOCK, head_rows), steps),
            key_blocks[0],
            value_blocks[0],
            key_blocks[1],
            value_blocks[1],
        ],
        out_specs=[
            pl.BlockSpec((HD, head_rows), lambda i: (0, 0)),
            *halves_of((KEY_BLOCK, 2 * HD), steps),
        ],
        out_shape=[
            jax.ShapeDtypeStruct((HD, head_rows), F32),
            jax.ShapeDtypeStruct((keys, 2 * HD), BF),
            jax.ShapeDtypeStruct((keys, 2 * HD), BF),
        ],
        compiler_params=pltpu.CompilerParams(vmem_limit_bytes=VMEM_LIMIT),
        cost_estimate=pl.CostEstimate(
            flops=16 * keys * head_rows * HD,
            bytes_accessed=2 * keys * (head_rows + 4 * HD) * 2,
            transcendentals=0,
        ),
        name="attend_back",
    )(queries, d_heads, mass, dots, *probs, pairs[0], pairs[0], pairs[1], pairs[1])


def spread_rows(product, mine, size, keep, send, first):
    step = keep.shape[0] // 2
    width = product.shape[1]
    for offset in range(4):
        rows = product[pl.ds(pl.multiple_of((mine ^ offset) * size, 32), size), :]
        out = send if offset % 2 else keep
        begin = offset // 2 * step + first
        out[begin : begin + size, :width] = rows.astype(out.dtype)


def query_back_kernel(
    mine, d_queries, query_raw, gains, cosine, sine, query_mat, first_low, heads_low, d_attn_low,
    keep, send, d_first, d_gain, product, out_product, query_low,
):
    rows = first_low.shape[0]
    gain = gains[0:1, :]
    d_gain[...] = jnp.zeros_like(d_gain)
    for h in range(H):
        columns = pl.ds(h * HD, HD)
        head = d_queries[:, h * rows : (h + 1) * rows].T * HD ** (-0.5)
        head = rotate(head, cosine[...], -sine[...])
        d_raw, d_head_gain = rms_back(query_raw[:, columns], gain, head)
        d_gain[...] += d_head_gain
        query_low[:, columns] = d_raw.astype(BF)
    d_first[...] = contract(query_low[...], query_mat[...], 1, 1)
    model, inner = product.shape[0] // 4, out_product.shape[0] // 4
    keep[...] = jnp.zeros_like(keep)
    send[...] = jnp.zeros_like(send)
    product[...] = contract(first_low[...], query_low[...], 0, 0)
    spread_rows(product, mine[0], model, keep, send, 0)
    out_product[...] = contract(heads_low[...], d_attn_low[...], 0, 0)
    spread_rows(out_product, mine[0], inner, keep, send, model)


def key_back_kernel(
    mine, sums, *refs
):
    terms, refs = refs[:-19], refs[-19:]
    (
        key_raw, gains, head_gains, cosine, sine, pair_mat, first_low, d_first_query, tokens, d_hidden,
        d_gain_attn_out, d_gain_ffn_in, d_gain_ffn_out, d_gain_query,
        grad_tokens, keep, send, product, gain_lines,
    ) = refs
    total = sums[...]
    for term in terms:
        total = total + term[...].astype(F32)
    d_key = rotate(total[:, :HD], cosine[...], -sine[...])
    d_raw, d_gain_key = rms_back(key_raw[...], head_gains[1:2, :], d_key)
    low = jnp.concatenate([d_raw, total[:, HD:]], axis=1).astype(BF)
    d_first = d_first_query[...] + contract(low, pair_mat[...], 1, 1)
    extra, d_gain_attn_in = rms_back(tokens[...].astype(F32), gains[0:1, :], d_first)
    grad_tokens[...] = d_hidden[...] + extra
    product[:, : 2 * HD] = contract(first_low[...], low, 0, 0)
    gain_lines[...] = jnp.zeros_like(gain_lines)
    for i, line in enumerate(
        (d_gain_attn_in, d_gain_attn_out[...], d_gain_ffn_in[...], d_gain_ffn_out[...])
    ):
        gain_lines[i : i + 1, :] = line
    size, head_size = product.shape[0] // 4, HD // 4
    for i, line in enumerate((d_gain_query[...], d_gain_key)):
        pieces = []
        for r in range(4):
            pieces += [line[:, r * head_size : (r + 1) * head_size], jnp.zeros((1, size - head_size), F32)]
        gain_lines[4 + i : 5 + i, :] = jnp.concatenate(pieces, axis=1)
    product[:, 2 * HD :] = gain_lines[...].T
    keep[...] = jnp.zeros_like(keep)
    send[...] = jnp.zeros_like(send)
    spread_rows(product, mine[0], size, keep, send, 0)


def left_of(owner, part):
    return pl.multiple_of(owner * part - part % 128 * (owner % 2), 128)


def carve_kernel(part, mine, w, own, core):
    for offset, out in enumerate((own, core)):
        out[...] = w[:, :, pl.ds(left_of(mine[0] ^ offset, part), out.shape[2])]


def carve(w, mine, part, wide):
    rows, step = w.shape[1], 48
    return pl.pallas_call(
        functools.partial(carve_kernel, part),
        grid_spec=pltpu.PrefetchScalarGridSpec(
            num_scalar_prefetch=1,
            grid=(rows // step,),
            in_specs=[pl.BlockSpec((2, step, w.shape[2]), lambda i, p: (0, i, 0))],
            out_specs=[pl.BlockSpec((2, step, wide), lambda i, p: (0, i, 0))] * 2,
        ),
        out_shape=[jax.ShapeDtypeStruct((2, rows, wide), BF)] * 2,
        compiler_params=pltpu.CompilerParams(vmem_limit_bytes=VMEM_LIMIT),
        name="carve",
    )(mine[None], w)


def carve_quarters_kernel(part, place, w, near, corner):
    mine, side = place[0], place[2]
    for offset, out in ((2, near), (3, corner)):
        at = pl.ds(left_of(mine ^ offset, part), out.shape[2])
        for s in range(2):

            @pl.when(side == s)
            def _(s=s):
                out[0] = w[:, s, at]


def carve_quarters(w, place, part, wide):
    rows, step = w.shape[0], 48
    half = rows // 2 // step
    return pl.pallas_call(
        functools.partial(carve_quarters_kernel, part),
        grid_spec=pltpu.PrefetchScalarGridSpec(
            num_scalar_prefetch=1,
            grid=(half,),
            in_specs=[pl.BlockSpec((step, 2, w.shape[2]), lambda i, p: (i + half * p[1], 0, 0))],
            out_specs=[pl.BlockSpec((1, step, wide), lambda i, p: (0, i, 0))] * 2,
        ),
        out_shape=[jax.ShapeDtypeStruct((1, rows // 2, wide), BF)] * 2,
        compiler_params=pltpu.CompilerParams(vmem_limit_bytes=VMEM_ALL),
        name="carve_quarters",
    )(place, w)


def walk(shape, first, count, scalars, dim=0):
    def place(i, *unused):
        return tuple(jnp.clip(i - first, 0, count - 1) if d == dim else 0 for d in range(len(shape)))

    return pl.BlockSpec(shape, place)


def settle_kernel(counts, places, *refs):
    out, sources = refs[-1], refs[:-1]
    step, first = pl.program_id(0), 0
    for source, count in zip(sources, counts):

        @pl.when((step >= first) & (step < first + count))
        def _(source=source):
            out[...] = source[...]

        first += count


def settle(places, rows, *sources):
    counts = [source.shape[0] // rows for source in sources]
    width = sources[0].shape[1]
    starts = [sum(counts[:i]) for i in range(len(counts))]
    return pl.pallas_call(
        functools.partial(settle_kernel, counts),
        grid_spec=pltpu.PrefetchScalarGridSpec(
            num_scalar_prefetch=1,
            grid=(sum(counts),),
            in_specs=[walk((rows, width), f, c, 1) for f, c in zip(starts, counts)],
            out_specs=pl.BlockSpec((rows, width), lambda i, p: (p[i], 0)),
        ),
        out_shape=jax.ShapeDtypeStruct((sum(counts) * rows, width), sources[0].dtype),
        compiler_params=pltpu.CompilerParams(vmem_limit_bytes=VMEM_LIMIT),
        name="settle",
    )(places, *sources)


def lay_kernel(counts, sides, rows, *refs):
    out, sources = refs[-1], refs[: len(counts)]
    step, first = pl.program_id(0), 0
    width = out.shape[3]
    for source, count in zip(sources, counts):

        @pl.when((step >= first) & (step < first + count))
        def _(source=source):
            for block in range(out.shape[1]):
                out[0, block] = source[0, :, block * width : (block + 1) * width]

        first += count


def lay(places, sources, laid=None):
    half, wide = sources[-1].shape[1], sources[-1].shape[2]
    counts = [source.shape[0] * source.shape[1] // half for source in sources]

    def run(first, count):
        def place(i, s, r):
            j = jnp.clip(i - first, 0, count - 1)
            return (j // 2, j % 2, 0)

        return pl.BlockSpec((1, half, wide), place)

    base = [] if laid is None else [laid]
    sides, rows = [jnp.stack([jnp.asarray(p[i], jnp.int32) for p in places]) for i in (0, 1)]
    return pl.pallas_call(
        functools.partial(lay_kernel, counts),
        grid_spec=pltpu.PrefetchScalarGridSpec(
            num_scalar_prefetch=2,
            grid=(sum(counts),),
            in_specs=[run(sum(counts[:i]), count) for i, count in enumerate(counts)]
            + [pl.BlockSpec(memory_space=pl.ANY)] * len(base),
            out_specs=pl.BlockSpec(
                (1, wide // 256, half, 256), lambda i, s, r: (s[i], 0, r[i], 0)
            ),
        ),
        out_shape=jax.ShapeDtypeStruct((2, wide // 256, 8 * half, 256), BF),
        input_output_aliases={2 + len(sources): 0} if base else {},
        compiler_params=pltpu.CompilerParams(vmem_limit_bytes=VMEM_LIMIT),
        name="lay",
    )(sides, rows, *sources, *base)


def contract(left, right, left_dim, right_dim):
    return lax.dot_general(
        left, right, (((left_dim,), (right_dim,)), ((), ())), preferred_element_type=F32
    )


def gelu_and_slope(x):
    scale = math.sqrt(2.0 / math.pi)
    cubic = (scale * 0.044715) * (x * x * x)
    inner = scale * x + cubic
    share = 0.5 + 0.5 * jnp.tanh(inner)
    return x * share, share + share * (1.0 - share) * (2.0 * inner + 4.0 * cubic)


def place_rows(part, blocks, mine, block, source, rows, sem):
    width = source.shape[0]
    odd = mine % 2
    extra = blocks * width - part
    begins = (block == 0) & (odd == 1)
    ends = (block == blocks - 1) & (odd == 0)

    def put(first, at, size):
        copy = pltpu.make_async_copy(
            source.at[pl.ds(first, size), :], rows.at[pl.ds(at, size), :], sem
        )
        copy.start()
        copy.wait()

    @pl.when(begins)
    def _():
        put(extra, 0, width - extra)

    @pl.when(ends)
    def _():
        put(0, (blocks - 1) * width, width - extra)

    @pl.when(jnp.logical_not(begins | ends))
    def _():
        put(0, pl.multiple_of(block * width - odd * extra, 64), width)


def fill_rows_kernel(part, blocks, info, *refs):
    sources, (rows, block, sem) = refs[:-4], refs[-3:]
    for partner, source in enumerate(sources):
        width = block.shape[0]
        for tile in range(block.shape[1] // 128):
            block[:, tile * 128 : (tile + 1) * 128] = source[
                tile * width : (tile + 1) * width, width : width + 128
            ].astype(F32)
        place_rows(part, blocks, info[0], info[1 + partner], block, rows, sem)


def fill_rows(info, part, blocks, sources, rows):
    whole = pl.BlockSpec(memory_space=pltpu.VMEM)
    anywhere = pl.BlockSpec(memory_space=pl.ANY)
    return pl.pallas_call(
        functools.partial(fill_rows_kernel, part, blocks),
        in_specs=[pl.BlockSpec(memory_space=pltpu.SMEM)] + [whole] * len(sources) + [anywhere],
        out_specs=anywhere,
        out_shape=jax.ShapeDtypeStruct(rows.shape, rows.dtype),
        scratch_shapes=[pltpu.VMEM((256, rows.shape[1]), F32), pltpu.SemaphoreType.DMA],
        input_output_aliases={1 + len(sources): 0},
        compiler_params=pltpu.CompilerParams(vmem_limit_bytes=VMEM_LIMIT),
        name="fill_rows",
    )(info, *sources, rows)


def ffn_gradients_kernel(part, apart, blocks, info, second, d_ffn, w_gate, w_up, w_down, *rest):
    outs, down_out, act, d_both, both_sum, down_sum, sem = rest[-10:-6], *rest[-6:]
    step = pl.program_id(1)
    rows, slab = second.shape[0], 256
    width = act.shape[1]

    def products(r):
        at = pl.ds(r * slab, slab)
        return (
            contract(second[at, :], w_gate[0, 0], 1, 0),
            contract(second[at, :], w_up[0, 0], 1, 0),
            contract(d_ffn[at, :], w_down[...], 1, 1),
        )

    ahead = products(0)
    for r in range(rows // slab):
        at = pl.ds(r * slab, slab)
        gate, upper, d_act = ahead
        if r + 1 < rows // slab:
            ahead = products(r + 1)
        value, slope = gelu_and_slope(gate)
        act[at, :] = (value * upper).astype(BF)
        d_both[at, :width] = (d_act * upper * slope).astype(BF)
        d_both[at, width:] = (d_act * value).astype(BF)
    grad_both = contract(second[...], d_both[...], 0, 0)
    grad_down = contract(act[...], d_ffn[...], 0, 0)

    @pl.when(step == 0)
    def _():
        both_sum[...] = grad_both
        down_sum[...] = grad_down

    @pl.when(step > 0)
    def _():
        both_sum[...] += grad_both
        down_sum[...] += grad_down

    @pl.when(step == pl.num_programs(1) - 1)
    def _():
        if apart:
            for tile in range(down_out.shape[0]):
                down_out[tile] = down_sum[:, tile * 128 : (tile + 1) * 128].astype(BF)
        else:
            place_rows(part, blocks, info[0], info[1 + pl.program_id(0)], down_sum, down_out, sem)

        quarter = second.shape[1] // 4
        for offset, out in enumerate(outs):
            at = pl.ds(pl.multiple_of((info[0] ^ offset) * quarter, 32), quarter)
            out[0] = both_sum[at, :width].astype(BF)
            out[1] = both_sum[at, width:].astype(BF)


def ffn_gradients(info, second_all, d_ffn_all, in_mat, down_mat, part, count, down_rows, apart):
    tokens, model = second_all.shape
    slab, width = min(2048, tokens), 256
    columns = count * width
    tall = pl.BlockSpec((slab, model), lambda j, t, m: (t, 0))
    anywhere = pl.BlockSpec(memory_space=pl.ANY)
    earlier = [] if down_rows is None else [down_rows]
    return pl.pallas_call(
        functools.partial(ffn_gradients_kernel, part, apart, down_mat.shape[0] // width),
        grid_spec=pltpu.PrefetchScalarGridSpec(
            num_scalar_prefetch=1,
            grid=(count, tokens // slab),
            in_specs=[
                tall,
                tall,
                pl.BlockSpec((1, 1, model, width), lambda j, t, m: (0, m[1 + j], 0, 0)),
                pl.BlockSpec((1, 1, model, width), lambda j, t, m: (1, m[1 + j], 0, 0)),
                pl.BlockSpec((width, model), lambda j, t, m: (m[1 + j], 0)),
            ]
            + [anywhere] * len(earlier),
            out_specs=[pl.BlockSpec((2, model // 4, width), lambda j, t, m: (0, 0, j))] * 4
            + [
                pl.BlockSpec((model // 128, width, 128), lambda j, t, m: (0, j, 0))
                if apart
                else anywhere
            ],
            scratch_shapes=[
                pltpu.VMEM((slab, width), BF),
                pltpu.VMEM((slab, 2 * width), BF),
                pltpu.VMEM((model, 2 * width), F32),
                pltpu.VMEM((width, model), F32),
                pltpu.SemaphoreType.DMA,
            ],
        ),
        out_shape=[jax.ShapeDtypeStruct((2, model // 4, columns), BF)] * 4
        + [
            jax.ShapeDtypeStruct((model // 128, columns, 128), BF)
            if apart
            else jax.ShapeDtypeStruct((part, model), F32)
        ],
        input_output_aliases={6: 4} if earlier else {},
        compiler_params=pltpu.CompilerParams(vmem_limit_bytes=VMEM_ALL),
        cost_estimate=pl.CostEstimate(
            flops=12 * tokens * model * columns,
            bytes_accessed=4 * tokens * model * count,
            transcendentals=tokens * columns,
        ),
        name="ffn_gradients",
    )(info, second_all, d_ffn_all, in_mat, in_mat, down_mat, *earlier)


def ffn_forward_kernel(near, far, w_gate, w_up, w_down, value, factor, keep, send, act, total):
    step, half = pl.program_id(0), near.shape[0]

    @pl.when(step == 0)
    def _():
        total[...] = jnp.zeros_like(total)

    def products(rows):
        return contract(rows[...], w_gate[0, 0], 1, 0), contract(rows[...], w_up[0, 0], 1, 0)

    ahead = products(near)
    for i in range(2):
        at = pl.ds(i * half, half)
        gate, upper = ahead
        if i == 0:
            ahead = products(far)
        gelu, slope = gelu_and_slope(gate)
        act[at, :] = (gelu * upper).astype(BF)
        value[at, :] = gelu.astype(BF)
        factor[at, :] = (upper * slope).astype(BF)
    total[...] += contract(act[...], w_down[...], 1, 0)

    @pl.when(step == pl.num_programs(0) - 1)
    def _():
        keep[...], send[...] = total[:half, :], total[half:, :].astype(BF)


def ffn_backward_kernel(
    near, far, value, factor, w_gate, w_up, w_down, keep, send, d_gate, d_up, total
):
    step, half = pl.program_id(0), near.shape[0]

    @pl.when(step == 0)
    def _():
        total[...] = jnp.zeros_like(total)

    for rows, at in ((near, pl.ds(0, half)), (far, pl.ds(half, half))):
        d_act = contract(rows[...], w_down[...], 1, 1)
        d_gate[at, :] = (d_act * factor[at, :].astype(F32)).astype(BF)
        d_up[at, :] = (d_act * value[at, :].astype(F32)).astype(BF)
    total[...] += contract(d_gate[...], w_gate[0, 0], 1, 1) + contract(d_up[...], w_up[0, 0], 1, 1)

    @pl.when(step == pl.num_programs(0) - 1)
    def _():
        keep[...], send[...] = total[:half, :], total[half:, :].astype(BF)


def ffn_group(kernel, near, far, in_mat, down_mat, *kept):
    half, model = near.shape
    wide, width = down_mat.shape[0], 256
    rows = pl.BlockSpec((half, model), lambda j: (0, 0))
    column = pl.BlockSpec((2 * half, width), lambda j: (0, j))
    forward = not kept
    shape = jax.ShapeDtypeStruct((2 * half, wide), BF)
    return pl.pallas_call(
        kernel,
        grid=(wide // width,),
        in_specs=[rows, rows]
        + [column] * len(kept)
        + [
            pl.BlockSpec((1, 1, model, width), lambda j: (0, j, 0, 0)),
            pl.BlockSpec((1, 1, model, width), lambda j: (1, j, 0, 0)),
            pl.BlockSpec((width, model), lambda j: (j, 0)),
        ],
        out_specs=[column] * (2 * forward) + [rows, rows],
        out_shape=[shape] * (2 * forward)
        + [jax.ShapeDtypeStruct((half, model), F32), jax.ShapeDtypeStruct((half, model), BF)],
        scratch_shapes=[pltpu.VMEM((2 * half, width), BF)] * (1 if forward else 2)
        + [pltpu.VMEM((2 * half, model), F32)],
        compiler_params=pltpu.CompilerParams(vmem_limit_bytes=24 * 2**20),
        cost_estimate=pl.CostEstimate(
            flops=12 * half * model * wide,
            bytes_accessed=6 * model * wide + 16 * half * wide,
            transcendentals=2 * half * wide,
        ),
        name="ffn_forward" if forward else "ffn_backward",
    )(near, far, *kept, in_mat, in_mat, down_mat)


def unfold_kernel(part, info, *refs):
    shared, sources, (out, wide) = refs[:4], refs[4:-2], refs[-2:]
    mine, width = info[0], 256
    for partner, source in enumerate(shared):
        at = pl.ds(pl.multiple_of(info[1 + partner] * width, 128), width)
        for offset in range(4):
            wide[mine ^ offset, :, :, at] = source[offset, :, :, :width]
    first = 4 * width
    for r in range(0, len(sources), 4):
        last = first + sources[r].shape[2]
        for offset in range(4):
            wide[mine ^ offset, :, :, first:last] = sources[r + offset][...]
        first = last
    cut = wide.shape[3] - 128
    left = lax.broadcasted_iota(jnp.int32, (wide.shape[2], 128), 1) < part % 128
    for side in range(2):
        rows = [wide[owner, side].astype(F32) for owner in range(4)]
        pieces = []
        for even, odd in (rows[:2], rows[2:]):
            shared_tile = jnp.where(left, even[:, cut:], odd[:, :128])
            pieces += [even[:, :cut], shared_tile, odd[:, 128:]]
        out[:, side, :] = jnp.concatenate(pieces, axis=1)


def unfold(info, part, shared, ranges):
    sources = [piece for pieces in ranges for piece in pieces]
    rows, step = sources[0].shape[1], 32
    shared = [s.reshape(4, 2, rows, s.shape[1]) for s in shared]
    columns = sum(pieces[0].shape[2] for pieces in ranges) + 4 * 256
    return pl.pallas_call(
        functools.partial(unfold_kernel, part),
        grid_spec=pltpu.PrefetchScalarGridSpec(
            num_scalar_prefetch=1,
            grid=(rows // step,),
            in_specs=[
                pl.BlockSpec((4, 2, step, s.shape[3]), lambda i, m: (0, 0, i, 0)) for s in shared
            ]
            + [pl.BlockSpec((2, step, s.shape[2]), lambda i, m: (0, i, 0)) for s in sources],
            out_specs=pl.BlockSpec((step, 2, 4 * part), lambda i, m: (i, 0, 0)),
            scratch_shapes=[pltpu.VMEM((4, 2, step, columns), BF)],
        ),
        out_shape=jax.ShapeDtypeStruct((rows, 2, 4 * part), F32),
        compiler_params=pltpu.CompilerParams(vmem_limit_bytes=VMEM_LIMIT),
        name="unfold",
    )(info, *shared, *sources)


def pick(table, index):
    hit = index[:, None] == jnp.arange(table.shape[0], dtype=jnp.int32)[None, :]
    return jnp.sum(jnp.where(hit, table[None, :], 0), axis=1)


def body(
    tokens,
    cotangent,
    block_table,
    sequence_ids,
    w_query,
    w_key,
    w_value,
    w_out,
    w_in,
    w_down,
    gain_attn_in,
    gain_attn_out,
    gain_ffn_in,
    gain_ffn_out,
    gain_query,
    gain_key,
):
    rows = tokens.shape[0]
    block = rows // 2
    model, part = w_in.shape[0] * 4, w_down.shape[0]
    mine = lax.axis_index("fsdp")
    me = lax.axis_index("ctx") * 4 + mine

    gains = (gain_attn_in, gain_attn_out, gain_ffn_in, gain_ffn_out, gain_query, gain_key)
    sizes = [g.shape[0] for g in gains]
    (packed,) = kernel_call(
        pack_kernel,
        [((w_key.shape[0] + 16, 2 * HD), BF)],
        w_key,
        w_value,
        *[g[None] for g in gains],
        name="pack",
    )
    packed_flow = Flow(gather_group(packed))

    wide = -(-part // 256) * 256
    quarter = model // 4
    boundary = jnp.sum((sequence_ids == 0).astype(jnp.int32))
    everyone = me ^ jnp.array(wide_offsets(), jnp.int32)
    blocks = pick(block_table, jnp.stack([2 * everyone, 2 * everyone + 1], axis=1).reshape(-1))
    place = (blocks[:2, None] * block + jnp.arange(block, dtype=jnp.int32)[None, :]).reshape(-1)
    start = jnp.where(place >= boundary, boundary, 0)
    position = place - start
    inverse_angle = 1000000.0 ** (-jnp.arange(HD // 2, dtype=F32) / (HD // 2))
    angles = position.astype(F32)[:, None] * inverse_angle[None, :]
    cosine, sine = jnp.cos(angles), jnp.sin(angles)
    q_place, q_start = jnp.tile(place, H)[None], jnp.tile(start, H)[None]

    low_bit, high_bit = lax.axis_index("ctx") % 2, lax.axis_index("ctx") // 2 % 2
    quarters = carve_quarters(w_in, jnp.stack([mine, low_bit, high_bit]), part, wide)
    quarters = pace(quarters, packed_flow)
    arrived = []
    columns_flow = Flow(exchange_columns(quarters, arrived))
    cosine, sine, q_place, q_start = pace((cosine, sine, q_place, q_start), packed_flow)
    pair_mat, model_gains, head_gains = kernel_call(
        unpack_kernel,
        [((model, 2 * HD), BF), ((8, model), F32), ((8, HD), F32)],
        *packed_flow.result,
        scalars=(mine[None],),
        name="unpack",
    )
    first_low, key_raw, pair_rows = kernel_call(
        key_kernel,
        [((rows, model), BF), ((rows, HD), F32), ((rows, 2 * HD), BF)],
        tokens,
        model_gains,
        head_gains,
        pair_mat,
        cosine,
        sine,
        name="keys",
    )
    pairs_flow = Flow(gather_wide(pair_rows))
    own, to_core = carve(jnp.swapaxes(w_in, 0, 1), mine, part, wide)
    down_mat = lax.dynamic_update_slice_in_dim(
        jnp.zeros((wide, model), BF), w_down, part % 128 * (mine % 2), 0
    )
    own, to_core, w_query, down_mat = pace(
        (own, to_core, w_query, down_mat), pairs_flow, columns_flow
    )
    core_flow = Flow(iter_once([swap(to_core, 1)]))
    query_flow = Flow(gather_rows(w_query, mine))
    pace((), pairs_flow, columns_flow, core_flow)
    (w_out,) = pace((w_out,), pairs_flow, columns_flow, query_flow)
    out_flow = Flow(gather_rows(w_out, mine))
    pairs = finish(pairs_flow)
    query_mat = finish(query_flow)
    query_raw, queries = kernel_call(
        query_kernel,
        [((rows, H * HD), F32), ((H * rows, HD), BF)],
        first_low,
        head_gains,
        query_mat,
        cosine,
        sine,
        name="queries",
    )
    *probs, weighted, mass = attend(blocks, queries, q_place, q_start, *pairs)
    weighted, mass = pace((weighted, mass), out_flow, columns_flow)
    out_mat = finish(out_flow)
    heads, heads_low, attn_raw, hidden, second_low = kernel_call(
        after_attend_kernel,
        [
            ((H * rows, HD), F32),
            ((rows, H * HD), BF),
            ((rows, model), F32),
            ((rows, model), F32),
            ((rows, model), BF),
        ],
        weighted,
        mass,
        out_mat,
        tokens,
        model_gains,
        name="after_attend",
    )

    group_flow = Flow(gather_group(second_low))
    second_all = lax.all_gather(second_low, AXES, axis=0, tiled=True)
    places = [
        (side, (mine ^ offset) * 2 + bit) for offset in (0, 1) for side in (0, 1) for bit in (0, 1)
    ]
    for offset in (2, 3):
        places += [
            (side, (mine ^ offset) * 2 + bit)
            for side in (high_bit, 1 - high_bit)
            for bit in (low_bit, 1 - low_bit)
        ]
    laid = lay(places[:9] + places[10:], (own, *core_flow.result, *arrived))
    (laid,) = pace((laid,), group_flow, columns_flow)
    in_mat = lay(places[9:10], columns_flow.result, laid)
    value, factor, keep, send = ffn_group(ffn_forward_kernel, *finish(group_flow), in_mat, down_mat)
    block_out, d_ffn_low, d_gain_ffn_out = kernel_call(
        after_ffn_kernel,
        [((rows, model), BF), ((rows, model), BF), ((1, model), F32)],
        *finish(Flow(scatter_group(keep, send))),
        hidden,
        cotangent,
        model_gains,
        name="after_ffn",
    )
    group_flow = Flow(gather_group(d_ffn_low))
    d_ffn_all = lax.all_gather(d_ffn_low, AXES, axis=0, tiled=True)
    keep, send = ffn_group(
        ffn_backward_kernel, *finish(group_flow), in_mat, down_mat, value, factor
    )
    d_hidden, d_attn_low, d_heads, dots, d_gain_ffn_in, d_gain_attn_out = kernel_call(
        before_attend_back_kernel,
        [
            ((rows, model), F32),
            ((rows, model), BF),
            ((H * rows, HD), BF),
            ((1, H * rows), F32),
            ((1, model), F32),
            ((1, model), F32),
        ],
        *finish(Flow(scatter_group(keep, send))),
        hidden,
        cotangent,
        model_gains,
        attn_raw,
        out_mat,
        heads,
        name="before_attend_back",
    )

    d_queries, *d_pairs = attend_back(queries, d_heads, mass, dots, probs, pairs)
    sums_flow = Flow(scatter_wide(*d_pairs))
    early_rows = quarter + H * HD // 4
    keep, send, d_first_query, d_gain_query = kernel_call(
        query_back_kernel,
        [
            ((2 * early_rows, model), F32),
            ((2 * early_rows, model), BF),
            ((rows, model), F32),
            ((1, HD), F32),
        ],
        d_queries,
        query_raw,
        head_gains,
        cosine,
        sine,
        query_mat,
        first_low,
        heads_low,
        d_attn_low,
        scalars=(mine[None],),
        scratch=[((model, H * HD), F32), ((H * HD, model), F32), ((rows, H * HD), BF)],
        name="query_back",
    )
    keep, send, d_first_query = pace((keep, send, d_first_query), sums_flow)
    pace((), sums_flow)
    early_flow = Flow(scatter_group(keep, send))
    pace((), sums_flow, early_flow)
    pace((), sums_flow)
    grad_tokens, keep, send = kernel_call(
        key_back_kernel,
        [
            ((rows, model), F32),
            ((2 * quarter, 2 * HD + 128), F32),
            ((2 * quarter, 2 * HD + 128), BF),
        ],
        *sums_flow.result,
        key_raw,
        model_gains,
        head_gains,
        cosine,
        sine,
        pair_mat,
        first_low,
        d_first_query,
        tokens,
        d_hidden,
        d_gain_attn_out,
        d_gain_ffn_in,
        d_gain_ffn_out,
        d_gain_query,
        scalars=(mine[None],),
        scratch=[((model, 2 * HD + 128), F32), ((128, model), F32)],
        name="key_back",
    )
    tail_flow = Flow(scatter_group(keep, send))

    count = wide // 256
    block_info = jnp.stack([mine, low_bit, 1 - low_bit, 2 + high_bit, 3 - high_bit])

    def total(flow):
        near, far = flow.result
        return near + far.astype(F32)

    pace((), tail_flow)
    both = (second_all, d_ffn_all)
    *pieces, down = ffn_gradients(
        block_info[jnp.array([0, 1, 3])], *both, in_mat, down_mat, part, 2, None, True
    )
    both, pieces, down = pace((both, pieces, down), tail_flow, early_flow)
    early, tail = total(early_flow), total(tail_flow)
    tail = jnp.pad(tail, ((0, 0), (0, model - tail.shape[1])))
    rest = lax.psum(join(early, tail).astype(BF), "ctx")
    shared_flow = Flow(exchange_results(pieces, down))
    ranges, grad_down = [], None
    for first, last in ((4, 5), (5, 6), (6, count)):
        *pieces, grad_down = ffn_gradients(
            jnp.stack([mine, *[jnp.int32(i) for i in range(first, last)]]),
            *both,
            in_mat,
            down_mat,
            part,
            last - first,
            grad_down,
            False,
        )
        flying = [sent[1:] for sent in ranges]
        flows = () if first == 5 else (shared_flow,)
        both, grad_down, flying = pace((both, grad_down, flying), *flows)
        for sent, arrays in zip(ranges, flying):
            sent[1:] = arrays
        ranges.append([pieces[0]] + [swap(pieces[o], o) for o in (1, 2, 3)])
    shared = shared_flow.result
    grad_down = fill_rows(block_info, part, count, shared, grad_down)
    grad_in = unfold(block_info, part, shared, ranges)
    rest, grad_down, grad_in = pace((rest, grad_down, grad_in))
    early, tail = rest[:early_rows], rest[early_rows:]
    early, tail = early.astype(F32), tail.astype(F32)
    grad_query = early[:quarter, : H * HD]
    grad_out = early[quarter:]
    grad_key, grad_value = tail[:quarter, :HD], tail[:quarter, HD : 2 * HD]
    gain_grads = [tail[:size, 2 * HD + i] for i, size in enumerate(sizes)]

    return (
        block_out,
        grad_tokens,
        grad_query,
        grad_key,
        grad_value,
        grad_out,
        grad_in,
        grad_down,
        *gain_grads,
    )


def solution(mesh):
    in_specs = (
        P(AXES, None),
        P(AXES, None),
        P(),
        P(),
        P("fsdp", None),
        P("fsdp", None),
        P("fsdp", None),
        P("fsdp", None),
        P("fsdp", None, None),
        P("fsdp", None),
        P("fsdp"),
        P("fsdp"),
        P("fsdp"),
        P("fsdp"),
        P("fsdp"),
        P("fsdp"),
    )
    out_specs = (
        P(AXES, None),
        P(AXES, None),
        P("fsdp", None),
        P("fsdp", None),
        P("fsdp", None),
        P("fsdp", None),
        P("fsdp", None, None),
        P("fsdp", None),
        P("fsdp"),
        P("fsdp"),
        P("fsdp"),
        P("fsdp"),
        P("fsdp"),
        P("fsdp"),
    )
    return jax.shard_map(body, mesh=mesh, in_specs=in_specs, out_specs=out_specs, check_vma=False)
```
